32 devices in a mesh: dp: 4 (over y, x), fsdp: 8 (over z, core).
Axes of the slice: x: 2, y: 2, z: 4, core: 2. Of those that a mesh axis runs over, the one named last changes fastest.
Arguments:
- latents: float32 [32, 256, 1024], P(('dp', 'fsdp'))
- pixels: bfloat16 [32, 512, 1024], P(('dp', 'fsdp')), may hold values from -6 to 6
- slot_index: int32 [32], P(('dp', 'fsdp')), may hold values from 0 to 31, as said below
- counts: int32 [32], P(('dp', 'fsdp')), may hold values from 128 to 512, as said below
- cotangent: float32 [32, 256, 1024], P(('dp', 'fsdp')), may hold values from -6 to 6
- gain_q: bfloat16 [1024], P(('dp', 'fsdp')), may hold values from 0.5 to 1.5
- gain_kv: bfloat16 [1024], P(('dp', 'fsdp')), may hold values from 0.5 to 1.5
- w_query: bfloat16 [1024, 1024], P(('dp', 'fsdp')), may hold values from -0.1875 to 0.1875
- w_key: bfloat16 [1024, 1024], P(('dp', 'fsdp')), may hold values from -0.1875 to 0.1875
- w_value: bfloat16 [1024, 1024], P(('dp', 'fsdp')), may hold values from -0.1875 to 0.1875
- w_out: bfloat16 [1024, 1024], P(('dp', 'fsdp')), may hold values from -3.5 to 3.5
- gain_self: bfloat16 [1024], P(('dp', 'fsdp')), may hold values from 0.5 to 1.5
- w_qkv: bfloat16 [1024, 3072], P(('dp', 'fsdp')), may hold values from -0.1875 to 0.1875
- w_self_out: bfloat16 [1024, 1024], P(('dp', 'fsdp')), may hold values from -3 to 3
- gain_mlp: bfloat16 [1024], P(('dp', 'fsdp')), may hold values from 0.5 to 1.5
- w_up: bfloat16 [1024, 4096], P(('dp', 'fsdp')), may hold values from -0.1875 to 0.1875
- w_down: bfloat16 [4096, 1024], P(('dp', 'fsdp')), may hold values from -0.09375 to 0.09375
Outputs:
- latents_out: float32 [32, 256, 1024], P(('dp', 'fsdp'))
- latents_grad: float32 [32, 256, 1024], P(('dp', 'fsdp'))
- pixels_grad: float32 [32, 512, 1024], P(('dp', 'fsdp'))
- gain_q_grad: float32 [1024], P(('dp', 'fsdp'))
- gain_kv_grad: float32 [1024], P(('dp', 'fsdp'))
- w_query_grad: float32 [1024, 1024], P(('dp', 'fsdp'))
- w_key_grad: float32 [1024, 1024], P(('dp', 'fsdp'))
- w_value_grad: float32 [1024, 1024], P(('dp', 'fsdp'))
- w_out_grad: float32 [1024, 1024], P(('dp', 'fsdp'))
- gain_self_grad: float32 [1024], P(('dp', 'fsdp'))
- w_qkv_grad: float32 [1024, 3072], P(('dp', 'fsdp'))
- w_self_out_grad: float32 [1024, 1024], P(('dp', 'fsdp'))
- gain_mlp_grad: float32 [1024], P(('dp', 'fsdp'))
- w_up_grad: float32 [1024, 4096], P(('dp', 'fsdp'))
- w_down_grad: float32 [4096, 1024], P(('dp', 'fsdp'))
- norms: float32 [32], P(('dp', 'fsdp'))
The draws below stay inside these ranges and needn't reach their ends.
Inputs may be any that keep to these rules, and one draw needn't show every extreme that they name: Group i reads pixel block i (slot_index[i] = i), which lies on the same device. The first counts[b] slots of pixel block b are visible, the rest are padding; some block has all 512 slots visible.
All inputs are finite; a program needn't handle non-finite values.
Results may differ from the reference program's by a relative error of at most 0.018.
Values may be sent and summed in bfloat16 or wider, within the bound.
A program may use at most 256 MiB of HBM per device.

```python
import jax
import jax.numpy as jnp
from jax import lax

D = 1024
HEADS = 8
HEAD_DIM = 128
FF = 4096
LAT = 256
SLOTS = 512
G_DEV = 1
GROUPS = 32


def draw_latents(key, part):
    key = jax.random.fold_in(key, 1)
    position = jnp.arange(GROUPS, dtype=jnp.float32) / max(GROUPS - 1, 1)
    base = jax.random.normal(key, (GROUPS, LAT, D), jnp.float32)
    scale = 1.0 + 5.0 * position
    return base * scale[:, None, None]


def draw_slot_index(key, part):
    key = jax.random.fold_in(key, 2)
    blocks = GROUPS // G_DEV
    order = jnp.tile(jnp.arange(G_DEV, dtype=jnp.int32)[None, :], (blocks, 1))
    mixed = jax.random.permutation(key, order, axis=1, independent=True)
    return (mixed + jnp.arange(blocks, dtype=jnp.int32)[:, None] * G_DEV).reshape(GROUPS).astype(jnp.int32)


def draw_counts(key, part):
    key = jax.random.fold_in(key, 3)
    drawn = jax.random.randint(key, (GROUPS,), SLOTS // 4, SLOTS + 1, dtype=jnp.int32)
    filled = jnp.arange(GROUPS, dtype=jnp.int32) % (5 * G_DEV) == 0
    return jnp.where(filled, SLOTS, drawn).astype(jnp.int32)


def shard_levels(own_key, extent, cuts, smallest, high):
    def one(dim, blocks):
        heights = jax.random.uniform(jax.random.fold_in(jax.random.fold_in(own_key, 6), dim), (blocks,), jnp.float32, smallest / len(cuts), high / len(cuts))
        return jnp.repeat(jnp.exp(heights), extent[dim] // blocks).reshape((-1,) + (1,) * (len(extent) - dim - 1))

    level = one(*cuts[0])
    for cut in cuts[1:]:
        level = level * one(*cut)
    return level


def scatter_about(key, dims, scale, reach, cuts=(), kind=jnp.bfloat16):
    level = shard_levels(key, dims, cuts, -0.22, 0.18) if cuts else 1.0
    values = jax.random.normal(key, dims, jnp.float32) * scale * level
    return jnp.minimum(jnp.maximum(values, -reach), reach).astype(kind)


def setup_inputs(seed: int = 0) -> dict:
    streams_of = jax.random.split(jax.random.key(seed), 18)
    return {
        "latents": draw_latents(jax.random.fold_in(streams_of[17], 71), 0),
        "pixels": scatter_about(streams_of[1], (GROUPS, SLOTS, D), 1.0, 6.0, ((0, 32),)),
        "slot_index": draw_slot_index(jax.random.fold_in(streams_of[17], 71), 0),
        "counts": draw_counts(jax.random.fold_in(streams_of[17], 71), 0),
        "cotangent": scatter_about(streams_of[4], (GROUPS, LAT, D), 1.0, 6.0, ((0, 32),), jnp.float32),
        "gain_q": jnp.clip(1.0 + 0.1 * jax.random.normal(streams_of[5], (D,), jnp.float32), 0.5, 1.5).astype(jnp.bfloat16),
        "gain_kv": jnp.clip(1.0 + 0.1 * jax.random.normal(streams_of[6], (D,), jnp.float32), 0.5, 1.5).astype(jnp.bfloat16),
        "w_query": scatter_about(streams_of[7], (D, D), D ** -0.5, 0.1875, ((0, 32),)),
        "w_key": scatter_about(streams_of[8], (D, D), D ** -0.5, 0.1875, ((0, 32),)),
        "w_value": scatter_about(streams_of[9], (D, D), D ** -0.5, 0.1875, ((0, 32),)),
        "w_out": scatter_about(streams_of[10], (D, D), (max(1, 8 * D // (5 * SLOTS))) ** -0.5, 3.5, ((0, 32),)),
        "gain_self": jnp.clip(1.0 + 0.1 * jax.random.normal(streams_of[11], (D,), jnp.float32), 0.5, 1.5).astype(jnp.bfloat16),
        "w_qkv": scatter_about(streams_of[12], (D, 3 * D), D ** -0.5, 0.1875, ((0, 32),)),
        "w_self_out": scatter_about(streams_of[13], (D, D), (max(1, D // LAT)) ** -0.5, 3.0, ((0, 32),)),
        "gain_mlp": jnp.clip(1.0 + 0.1 * jax.random.normal(streams_of[14], (D,), jnp.float32), 0.5, 1.5).astype(jnp.bfloat16),
        "w_up": scatter_about(streams_of[15], (D, FF), D ** -0.5, 0.1875, ((0, 32),)),
        "w_down": scatter_about(streams_of[16], (FF, D), FF ** -0.5, 0.09375, ((0, 32),)),
    }


EPS = 1e-05
HIGH = lax.Precision.HIGHEST

@jax.custom_vjp
def low(v):
    return lax.optimization_barrier(v.astype(jnp.bfloat16)).astype(jnp.float32)

@jax.custom_vjp
def low_back(v):
    return v

def low_keep(v):
    return (low(v), None)

def low_pass(kept, grad):
    return (grad,)

def back_keep(v):
    return (v, None)

def back_low(kept, grad):
    return (low(grad),)
low.defvjp(low_keep, low_pass)
low_back.defvjp(back_keep, back_low)

def layer_norm(inputs, gain):
    center = inputs - lax.optimization_barrier(jnp.mean(inputs, axis=-1, keepdims=True))
    spread = lax.optimization_barrier(jnp.mean(center * center, axis=-1, keepdims=True))
    return center * lax.rsqrt(spread + EPS) * gain

def project(inputs, matrix):
    return jnp.einsum('gld,de->gle', inputs, matrix, precision=HIGH)

def split_heads(tensor):
    return tensor.reshape(tensor.shape[0], tensor.shape[1], HEADS, HEAD_DIM)

def attend(queries, key_rows, value_rows, visible):
    scores = jnp.einsum('glhd,gshd->ghls', queries, key_rows, precision=HIGH) * HEAD_DIM ** (-0.5)
    scores = low_back(scores)
    if visible is not None:
        scores = jnp.where(visible[:, None, None, :], scores, -1e+30)
    attn_probs = low(jax.nn.softmax(scores, axis=-1))
    mixed = jnp.einsum('ghls,gshd->glhd', attn_probs, value_rows, precision=HIGH)
    mixed = low(low_back(mixed))
    return mixed.reshape(mixed.shape[0], mixed.shape[1], HEADS * HEAD_DIM)

def block_forward(params, latent_rows, pixel_rows, visible_count):
    gain_q, gain_kv, w_query, w_key, w_value, w_out, gain_self, w_qkv, w_self_out, gain_mlp, w_up, w_down = params
    normed = low(layer_norm(latent_rows, gain_q))
    pix_normed = low(layer_norm(pixel_rows, gain_kv))
    queries = split_heads(low(low_back(project(normed, w_query))))
    key_rows = split_heads(low(low_back(project(pix_normed, w_key))))
    value_rows = split_heads(low(low_back(project(pix_normed, w_value))))
    visible = jnp.arange(SLOTS, dtype=jnp.int32)[None, :] < visible_count[:, None]
    cross_mixed = attend(queries, key_rows, value_rows, visible)
    after_cross = latent_rows + low_back(project(cross_mixed, w_out))
    normed_self = low(layer_norm(after_cross, gain_self))
    packed = low(low_back(project(normed_self, w_qkv)))
    width = HEADS * HEAD_DIM
    self_mixed = attend(split_heads(packed[..., :width]), split_heads(packed[..., width:2 * width]), split_heads(packed[..., 2 * width:]), None)
    after_self = after_cross + low_back(project(self_mixed, w_self_out))
    normed_mlp = low(layer_norm(after_self, gain_mlp))
    hidden = low_back(project(normed_mlp, w_up))
    activated = low(jax.nn.gelu(hidden))
    return after_self + low_back(project(activated, w_down))

def reference(latents, pixels, slot_index, counts, cotangent, gain_q, gain_kv, w_query, w_key, w_value, w_out, gain_self, w_qkv, w_self_out, gain_mlp, w_up, w_down):
    weights = tuple((element.astype(jnp.float32) for element in (gain_q, gain_kv, w_query, w_key, w_value, w_out, gain_self, w_qkv, w_self_out, gain_mlp, w_up, w_down)))

    def forward(latent_all, pixel_all, *params):
        chosen = jnp.take(pixel_all, slot_index, axis=0)
        visible_count = jnp.take(counts, slot_index, axis=0)
        blocks = GROUPS // G_DEV
        stacked = (latent_all.reshape(blocks, G_DEV, LAT, HEADS * HEAD_DIM), chosen.reshape(blocks, G_DEV, SLOTS, HEADS * HEAD_DIM), visible_count.reshape(blocks, G_DEV))

        def one_block(element):
            return block_forward(params, element[0], element[1], element[2])
        result = lax.map(jax.checkpoint(one_block), stacked)
        return result.reshape(latent_all.shape)
    latents_out, pull_back = jax.vjp(forward, latents.astype(jnp.float32), pixels.astype(jnp.float32), *weights)
    gradients = pull_back(cotangent.astype(jnp.float32))
    root_mean = jnp.sqrt(lax.optimization_barrier(jnp.mean(latents_out * latents_out, axis=(1, 2))))
    norms = root_mean / jnp.mean(root_mean)
    return (latents_out, gradients[0], gradients[1], gradients[2], gradients[3], gradients[4], gradients[5], gradients[6], gradients[7], gradients[8], gradients[9], gradients[10], gradients[11], gradients[12], gradients[13], norms)
```

```python
import functools

import jax
import jax.numpy as jnp
from jax import lax
from jax.experimental import pallas as pl
from jax.experimental.pallas import tpu as pltpu
from jax.sharding import PartitionSpec as P

MESH = pl.DeviceIdType.MESH
DMA = pltpu.SemaphoreType.DMA
UNIT_COLS = 1024
UNIT_ROWS = 32
WIDTHS = ((256, 256, 256, 256), (128, 128, 384, 384), (128, 128, 384, 384))


class Place:
    def __init__(self):
        dp, f = lax.axis_index("dp"), lax.axis_index("fsdp")
        self.y, self.x, self.z, self.c = dp // 2, dp % 2, f // 2, f % 2
        step = jnp.where(self.z < 2, 1, -1)
        self.is_end = (self.z == 0) | (self.z == 3)
        self.z1 = jnp.where(self.is_end, self.z + step, self.z - step)
        self.z2 = jnp.where(self.is_end, self.z + 2 * step, self.z + step)
        self.z3 = jnp.where(self.is_end, self.z + 3 * step, self.z + 2 * step)

    def dev(self, y=None, x=None, z=None, c=None):
        y = self.y if y is None else y
        x = self.x if x is None else x
        z = self.z if z is None else z
        c = self.c if c is None else c
        return (y * 2 + x, z * 2 + c)

    def barrier(self):
        bar = pltpu.get_barrier_semaphore()
        peers = [
            self.dev(c=1 - self.c),
            self.dev(x=1 - self.x),
            self.dev(y=1 - self.y),
            self.dev(z=self.z1),
            self.dev(z=self.z2),
            self.dev(z=self.z3),
        ]
        for peer in peers:
            pl.semaphore_signal(bar, inc=1, device_id=peer, device_id_type=MESH)
        pl.semaphore_wait(bar, len(peers))


def remote(src, dst, send_sem, recv_sem, dev):
    return pltpu.make_async_remote_copy(
        src_ref=src, dst_ref=dst, send_sem=send_sem, recv_sem=recv_sem, device_id=dev, device_id_type=MESH
    )


def part_cols(u, p, base):
    widths = WIDTHS[u % 3]
    return pl.ds(base + sum(widths[:p]), widths[p])


class Gather:
    STAGES = 7

    def __init__(self, me, units, sems):
        self.me, self.units = me, units
        self.loc, self.sib_s, self.sib_r, self.zs, self.zr, self.xs, self.xr, self.ys, self.yr = sems

    @staticmethod
    def sems(n):
        return [DMA((n,))] * 3 + [DMA((n, 4, 4))] * 2 + [DMA((n, 4))] * 4

    def at(self, u, y, x, z, c, p=None):
        _, full, row, col = self.units[u]
        cols = pl.ds(col, UNIT_COLS) if p is None else part_cols(u, p, col)
        return full.at[y, x, z, c, pl.ds(row, UNIT_ROWS), cols]

    def own(self, u):
        me, (shard, _, row, col) = self.me, self.units[u]
        src = shard.at[pl.ds(row, UNIT_ROWS), pl.ds(col, UNIT_COLS)]
        return pltpu.make_async_copy(src, self.at(u, me.y, me.x, me.z, me.c), self.loc.at[u])

    def zblk(self, u, p, z):
        me, s = self.me, slice(None)
        return self.at(u, me.y if p != 3 else s, me.x if p != 2 else s, z, me.c, p)

    def zcopy(self, u, p, z_to, z_block=None):
        me = self.me
        if z_block is None:
            b = self.zblk(u, p, me.z)
            return remote(b, b, self.zs.at[u, p, z_to], self.zr.at[u, p, me.z], me.dev(z=z_to))
        b = self.zblk(u, p, z_block)
        return remote(b, b, self.zs.at[u, p, me.z], self.zr.at[u, p, z_block], me.dev(z=z_to))

    def zin(self, u, p, z_block):
        b = self.zblk(u, p, z_block)
        return remote(b, b, self.zs.at[u, p, z_block], self.zr.at[u, p, z_block], self.me.dev(z=z_block))

    def z_a(self, u, p):
        me = self.me
        self.zcopy(u, p, me.z1).start()
        self.zcopy(u, p, me.z2).start()

        @pl.when(~me.is_end)
        def _():
            self.zcopy(u, p, me.z3).start()

    def z_b(self, u, p):
        me = self.me

        @pl.when(~me.is_end)
        def _():
            self.zin(u, p, me.z3).wait_recv()
            self.zcopy(u, p, me.z1, me.z3).start()

    def z_wait(self, u, p):
        me = self.me
        self.zin(u, p, me.z1).wait_recv()
        self.zin(u, p, me.z2).wait_recv()

        @pl.when(me.is_end)
        def _():
            self.zin(u, p, me.z3).wait_recv()

    def z_sent(self, u, p):
        me = self.me
        self.zcopy(u, p, me.z1).wait_send()
        self.zcopy(u, p, me.z2).wait_send()

        @pl.when(~me.is_end)
        def _():
            self.zcopy(u, p, me.z3).wait_send()
            self.zcopy(u, p, me.z1, me.z3).wait_send()

    def xcopy(self, u, p, out=True):
        me, s = self.me, slice(None)
        b = self.at(u, me.y if p != 3 and p != 1 else s, me.x if out else 1 - me.x, me.z if p == 2 else s, me.c, p)
        return remote(b, b, self.xs.at[u, p], self.xr.at[u, p], me.dev(x=1 - me.x))

    def ycopy(self, u, p, out=True):
        me, s = self.me, slice(None)
        b = self.at(u, me.y if out else 1 - me.y, me.x if p != 2 and p != 0 else s, me.z if p == 3 else s, me.c, p)
        return remote(b, b, self.ys.at[u, p], self.yr.at[u, p], me.dev(y=1 - me.y))

    def final(self, u, out=True):
        me, s = self.me, slice(None)
        b = self.at(u, s, s, s, me.c if out else 1 - me.c)
        return remote(b, b, self.sib_s.at[u], self.sib_r.at[u], me.dev(c=1 - me.c))

    def stage(self, s, u):
        if s == 0:
            self.own(u).start()
        elif s == 1:
            self.own(u).wait()
            self.xcopy(u, 2).start()
            self.ycopy(u, 3).start()
            self.z_a(u, 0)
            self.z_a(u, 1)
        elif s == 2:
            self.z_b(u, 0)
            self.z_b(u, 1)
            self.xcopy(u, 2, False).wait_recv()
            self.z_a(u, 2)
            self.ycopy(u, 3, False).wait_recv()
            self.z_a(u, 3)
        elif s == 3:
            self.z_wait(u, 0)
            self.xcopy(u, 0).start()
            self.z_wait(u, 1)
            self.ycopy(u, 1).start()
            self.z_b(u, 2)
            self.z_b(u, 3)
        elif s == 4:
            self.z_wait(u, 2)
            self.ycopy(u, 2).start()
            self.z_wait(u, 3)
            self.xcopy(u, 3).start()
            self.xcopy(u, 0, False).wait_recv()
            self.ycopy(u, 0).start()
            self.ycopy(u, 1, False).wait_recv()
            self.xcopy(u, 1).start()
        elif s == 5:
            self.ycopy(u, 2, False).wait_recv()
            self.xcopy(u, 3, False).wait_recv()
            self.ycopy(u, 0, False).wait_recv()
            self.xcopy(u, 1, False).wait_recv()
            self.final(u).start()
        elif s == 6:
            self.final(u, False).wait_recv()

    def sent(self, u):
        for p in range(4):
            self.z_sent(u, p)
            self.xcopy(u, p).wait_send()
            self.ycopy(u, p).wait_send()
        self.final(u).wait_send()

    def tick(self, t, wide):
        for u in range(len(self.units)):
            s = t - max(0, u - wide + 1)
            if 0 <= s < self.STAGES:
                self.stage(s, u)

    def ticks(self, wide):
        return self.STAGES + max(0, len(self.units) - wide)


class Scatter:
    STAGES = 5

    def __init__(self, me, units, refs, sems):
        self.me, self.units = me, units
        self.part, self.r1, self.r2, self.rz = refs
        self.s1, self.q1, self.s2, self.q2, self.zs, self.zr = sems

    @staticmethod
    def scratch(n):
        return [
            pltpu.VMEM((n, 2, 2, 4, UNIT_ROWS, UNIT_COLS), jnp.bfloat16),
            pltpu.VMEM((n, 2, 4, UNIT_ROWS, UNIT_COLS), jnp.bfloat16),
            pltpu.VMEM((n, 4, UNIT_ROWS, UNIT_COLS), jnp.bfloat16),
            pltpu.VMEM((n, 4, 2, UNIT_ROWS, UNIT_COLS), jnp.bfloat16),
        ]

    @staticmethod
    def sems(n):
        return [DMA((n, 4))] * 4 + [DMA((n, 4, 4))] * 2

    def pt(self, u, p, y, x, z):
        return self.part.at[u, y, x, z, :, part_cols(u, p, 0)]

    def first(self, u, p):
        me, s = self.me, slice(None)
        dst = self.r1.at[u, :, :, :, part_cols(u, p, 0)]
        if p in (0, 2):
            return remote(self.pt(u, p, 1 - me.y, s, s), dst, self.s1.at[u, p], self.q1.at[u, p], me.dev(y=1 - me.y))
        return remote(self.pt(u, p, s, 1 - me.x, s), dst, self.s1.at[u, p], self.q1.at[u, p], me.dev(x=1 - me.x))

    def add(self, count, dst, srcs):
        def body(i, carry):
            total = dst(i)[...].astype(jnp.float32)
            for src in srcs:
                total = total + src(i)[...].astype(jnp.float32)
            dst(i)[...] = total.astype(jnp.bfloat16)
            return carry

        if count == 1:
            body(0, 0)
        else:
            lax.fori_loop(0, count, body, 0)

    def first_in(self, u, p):
        me = self.me
        self.first(u, p).wait_recv()
        if p in (0, 2):
            dst = lambda i: self.pt(u, p, me.y, i // 4, i % 4)
        else:
            dst = lambda i: self.pt(u, p, i // 4, me.x, i % 4)
        self.add(8, dst, [lambda i: self.r1.at[u, i // 4, i % 4, :, part_cols(u, p, 0)]])

    def second(self, u, p):
        me, s = self.me, slice(None)
        cols = part_cols(u, p, 0)
        z = s if p < 2 else me.z
        dst = self.r2.at[u, :, :, cols] if p < 2 else self.r2.at[u, 0, :, cols]
        if p in (0, 2):
            return remote(self.pt(u, p, me.y, 1 - me.x, z), dst, self.s2.at[u, p], self.q2.at[u, p], me.dev(x=1 - me.x))
        return remote(self.pt(u, p, 1 - me.y, me.x, z), dst, self.s2.at[u, p], self.q2.at[u, p], me.dev(y=1 - me.y))

    def second_in(self, u, p):
        me = self.me
        self.second(u, p).wait_recv()
        self.add(
            4,
            lambda i: self.pt(u, p, me.y, me.x, i),
            [lambda i: self.r2.at[u, i, :, part_cols(u, p, 0)]],
        )

    def zblk(self, u, p, z):
        me, s = self.me, slice(None)
        return self.pt(u, p, me.y if p != 3 else s, me.x if p != 2 else s, z)

    def zslot(self, u, p, slot):
        cols = part_cols(u, p, 0)
        return self.rz.at[u, slot, 0, :, cols] if p < 2 else self.rz.at[u, slot, :, :, cols]

    def zcopy(self, u, p, which, block, slot, z_to):
        return remote(
            self.zblk(u, p, block), self.zslot(u, p, slot), self.zs.at[u, p, which], self.zr.at[u, p, slot], self.me.dev(z=z_to)
        )

    def z_ends(self, u, p):
        me = self.me
        return [
            self.zcopy(u, p, 2, me.z3, 3, me.z1),
            self.zcopy(u, p, 1, me.z2, 2, me.z2),
            self.zcopy(u, p, 0, me.z1, 0, me.z1),
        ]

    def z_mids(self, u, p):
        me = self.me
        return [self.zcopy(u, p, 0, me.z1, 0, me.z1), self.zcopy(u, p, 1, me.z2, 1, me.z2)]

    def z_gone(self, u, p):
        return self.zcopy(u, p, 2, self.me.z3, 1, self.me.z3)

    def z_a(self, u, p):
        me = self.me

        @pl.when(me.is_end)
        def _():
            for c in self.z_ends(u, p):
                c.start()

        @pl.when(~me.is_end)
        def _():
            for c in self.z_mids(u, p):
                c.start()

    def zget(self, u, p, slot):
        return self.zcopy(u, p, 0, self.me.z, slot, self.me.z1)

    def z_b(self, u, p):
        me = self.me

        @pl.when(~me.is_end)
        def _():
            self.zget(u, p, 3).wait_recv()
            self.z_add(u, p, me.z3, (3,))
            self.z_gone(u, p).start()

    def z_add(self, u, p, block, slots):
        cols = part_cols(u, p, 0)
        me = self.me
        if p < 2:
            dst, count = (lambda i: self.pt(u, p, me.y, me.x, block)), 1
        elif p == 2:
            dst, count = (lambda i: self.pt(u, p, me.y, i, block)), 2
        else:
            dst, count = (lambda i: self.pt(u, p, i, me.x, block)), 2
        self.add(count, dst, [functools.partial(lambda slot, i: self.rz.at[u, slot, i, :, cols], k) for k in slots])

    def z_in(self, u, p):
        me = self.me
        self.zget(u, p, 0).wait_recv()
        self.zget(u, p, 1).wait_recv()

        @pl.when(~me.is_end)
        def _():
            self.zget(u, p, 2).wait_recv()

    def out(self, u, p):
        out, row, col = self.units[u]
        return out.at[pl.ds(row, UNIT_ROWS), part_cols(u, p, col)]

    def finish_z(self, u, p):
        me, cols = self.me, part_cols(u, p, 0)
        self.z_in(u, p)
        f32 = lambda ref: ref[...].astype(jnp.float32)
        total = f32(self.pt(u, p, me.y, me.x, me.z)) + f32(self.rz.at[u, 0, 0, :, cols]) + f32(self.rz.at[u, 1, 0, :, cols])

        @pl.when(me.is_end)
        def _():
            self.out(u, p)[...] = total

        @pl.when(~me.is_end)
        def _():
            self.out(u, p)[...] = total + f32(self.rz.at[u, 2, 0, :, cols])

    def pass_z(self, u, p):
        me = self.me
        self.z_in(u, p)

        @pl.when(me.is_end)
        def _():
            self.z_add(u, p, me.z, (0, 1))

        @pl.when(~me.is_end)
        def _():
            self.z_add(u, p, me.z, (0, 1, 2))

        self.second(u, p).start()

    def finish_last(self, u, p):
        me, cols = self.me, part_cols(u, p, 0)
        self.second(u, p).wait_recv()
        total = self.pt(u, p, me.y, me.x, me.z)[...].astype(jnp.float32) + self.r2.at[u, 0, :, cols][...].astype(jnp.float32)
        self.out(u, p)[...] = total

    def stage(self, s, u):
        if s == 0:
            for p in (2, 3, 0, 1):
                self.first(u, p).start()
        elif s == 1:
            for p in (2, 3):
                self.first_in(u, p)
                self.z_a(u, p)
            for p in (0, 1):
                self.first_in(u, p)
                self.second(u, p).start()
        elif s == 2:
            for p in (2, 3):
                self.z_b(u, p)
            for p in (0, 1):
                self.second_in(u, p)
                self.z_a(u, p)
        elif s == 3:
            for p in (2, 3):
                self.pass_z(u, p)
            for p in (0, 1):
                self.z_b(u, p)
        elif s == 4:
            for p in (0, 1):
                self.finish_z(u, p)
            for p in (2, 3):
                self.finish_last(u, p)

    def sent(self, u):
        me = self.me
        for p in range(4):
            self.first(u, p).wait_send()
            self.second(u, p).wait_send()

            @pl.when(me.is_end)
            def _():
                for c in self.z_ends(u, p):
                    c.wait_send()

            @pl.when(~me.is_end)
            def _():
                for c in self.z_mids(u, p) + [self.z_gone(u, p)]:
                    c.wait_send()


def gather_units(shards, fulls):
    units = [(shards[i], fulls[i], 0, 0) for i in (1, 2, 0, 3)]
    units += [(shards[4], fulls[4], 0, k * UNIT_COLS) for k in range(3)]
    units += [(shards[5], fulls[5], 0, 0)]
    units += [(shards[6], fulls[6], 0, k * UNIT_COLS) for k in range(4)]
    units += [(shards[7], fulls[7], k * UNIT_ROWS, 0) for k in range(4)]
    return units


def gather_kernel(wide, *refs):
    shards, fulls, sems = refs[:8], refs[8:16], refs[16:]
    me = Place()
    me.barrier()
    gather = Gather(me, gather_units(shards, fulls), sems)
    for t in range(gather.ticks(wide)):
        gather.tick(t, wide)
    for u in range(len(gather.units)):
        gather.sent(u)


def gather_all(shards, wide=4):
    outs = [jax.ShapeDtypeStruct((2, 2, 4, 2) + s.shape, s.dtype) for s in shards]
    return pl.pallas_call(
        functools.partial(gather_kernel, wide),
        out_shape=outs,
        in_specs=[pl.BlockSpec(memory_space=pl.ANY)] * 8,
        out_specs=[pl.BlockSpec(memory_space=pl.ANY)] * 8,
        scratch_shapes=Gather.sems(16),
        compiler_params=pltpu.CompilerParams(collective_id=0, has_side_effects=True, vmem_limit_bytes=60 * 2**20),
    )(*shards)


def scatter_kernel(*refs):
    grads, outs = refs[:8], refs[8:16]
    part, r1, r2, rz, r0 = refs[16:21]
    sems, (la, lb, ls, lr) = refs[21:27], refs[27:]
    me = Place()
    me.barrier()
    units = [(outs[7], k * UNIT_ROWS, 0) for k in range(4)]
    units += [(outs[6], 0, k * UNIT_COLS) for k in range(4)]
    units += [(outs[4], 0, k * UNIT_COLS) for k in range(3)]
    units += [(outs[i], 0, 0) for i in (5, 3, 0, 1, 2)]
    which = [7] * 4 + [6] * 4 + [4] * 3 + [5, 3, 0, 1, 2]
    sc = Scatter(me, units, (part, r1, r2, rz), sems)
    n = len(units)

    def mine(u):
        _, row, col = units[u]
        src = grads[which[u]].at[:, :, :, me.c, pl.ds(row, UNIT_ROWS), pl.ds(col, UNIT_COLS)]
        return pltpu.make_async_copy(src, part.at[u], la.at[u])

    def give(u):
        _, row, col = units[u]
        src = grads[which[u]].at[:, :, :, 1 - me.c, pl.ds(row, UNIT_ROWS), pl.ds(col, UNIT_COLS)]
        return remote(src, r0.at[u], ls.at[u], lr.at[u], me.dev(c=1 - me.c))

    for t in range(n + 6):
        for s in (4, 3, 2, 1, 0, -1, -2):
            u = t - (s + 2)
            if not 0 <= u < n:
                continue
            if s == -2:
                mine(u).start()
                give(u).start()
            elif s == -1:
                mine(u).wait()
                give(u).wait_recv()
                idx = lambda i: (i // 8, (i // 4) % 2, i % 4)
                sc.add(16, lambda i: part.at[(u,) + idx(i)], [lambda i: r0.at[(u,) + idx(i)]])
                give(u).wait_send()
            else:
                sc.stage(s, u)
    for u in range(n):
        sc.sent(u)


def scatter_all(grads):
    outs = [jax.ShapeDtypeStruct(g.shape[4:], jnp.float32) for g in grads]
    n = 16
    return pl.pallas_call(
        scatter_kernel,
        out_shape=outs,
        in_specs=[pl.BlockSpec(memory_space=pl.ANY)] * 8,
        out_specs=[pl.BlockSpec(memory_space=pltpu.VMEM)] * 8,
        scratch_shapes=Scatter.scratch(n)
        + [pltpu.VMEM((n, 2, 2, 4, UNIT_ROWS, UNIT_COLS), jnp.bfloat16)]
        + Scatter.sems(n)
        + [DMA((n,))] * 4,
        compiler_params=pltpu.CompilerParams(collective_id=1, has_side_effects=True, vmem_limit_bytes=62 * 2**20),
    )(*grads)


HEADS = 8


EPS = 1e-05


def layer_norm(inputs, gain):
    center = inputs - jnp.mean(inputs, axis=-1, keepdims=True)
    spread = jnp.mean(center * center, axis=-1, keepdims=True)
    return center * lax.rsqrt(spread + EPS) * gain


def project(inputs, matrix):
    return jnp.einsum("gld,de->gle", inputs, matrix, preferred_element_type=jnp.float32)


def project_back(grad_rows, matrix):
    return jnp.einsum("gle,de->gld", grad_rows, matrix, preferred_element_type=jnp.float32)


def weight_grad(inputs, grad_rows):
    return jnp.einsum("gld,gle->de", inputs, grad_rows, preferred_element_type=jnp.float32)


def split_heads(tensor):
    return tensor.reshape(tensor.shape[0], tensor.shape[1], HEADS, -1)


def merge_heads(tensor):
    return tensor.reshape(tensor.shape[0], tensor.shape[1], -1)


def scores_of(queries, key_rows, visible):
    scores = jnp.einsum("glhd,gshd->ghls", queries, key_rows, preferred_element_type=jnp.float32)
    scores = scores * queries.shape[-1] ** (-0.5)
    if visible is not None:
        scores = jnp.where(visible[:, None, None, :], scores, -1e30)
    return scores


def attend_forward(queries, key_rows, value_rows, visible):
    scores = scores_of(queries, key_rows, visible)
    largest = jnp.max(scores, axis=-1, keepdims=True)
    exp_scores = jnp.exp(scores - largest)
    totals = jnp.sum(exp_scores, axis=-1, keepdims=True)
    attn_probs = exp_scores / totals
    log_total = largest + jnp.log(totals)
    mixed = jnp.einsum(
        "ghls,gshd->glhd",
        attn_probs.astype(jnp.bfloat16),
        value_rows,
        preferred_element_type=jnp.float32,
    ).astype(jnp.bfloat16)
    return (mixed, log_total)


def attend_backward(queries, key_rows, value_rows, visible, log_total, mixed_grad):
    scale = queries.shape[-1] ** (-0.5)
    attn_probs = jnp.exp(scores_of(queries, key_rows, visible) - log_total)
    probs_grad = jnp.einsum(
        "glhd,gshd->ghls", mixed_grad, value_rows, preferred_element_type=jnp.float32
    )
    value_grad = jnp.einsum(
        "ghls,glhd->gshd",
        attn_probs.astype(jnp.bfloat16),
        mixed_grad,
        preferred_element_type=jnp.float32,
    ).astype(jnp.bfloat16)
    score_grad = attn_probs * (
        probs_grad - jnp.sum(probs_grad * attn_probs, axis=-1, keepdims=True)
    )
    score_grad = score_grad.astype(jnp.bfloat16)
    query_grad = (
        jnp.einsum("ghls,gshd->glhd", score_grad, key_rows, preferred_element_type=jnp.float32)
        * scale
    ).astype(jnp.bfloat16)
    key_grad = (
        jnp.einsum("ghls,glhd->gshd", score_grad, queries, preferred_element_type=jnp.float32)
        * scale
    ).astype(jnp.bfloat16)
    return (query_grad, key_grad, value_grad)


def local_plain(
    latents,
    pixels,
    slot_index,
    counts,
    cotangent,
    gain_q,
    gain_kv,
    w_query,
    w_key,
    w_value,
    w_out,
    gain_self,
    w_qkv,
    w_self_out,
    gain_mlp,
    w_up,
    w_down,
):
    groups = latents.shape[0]
    slots = pixels.shape[1]
    width = latents.shape[2]
    local_slot = slot_index % groups
    chosen = jnp.take(pixels, local_slot, axis=0).astype(jnp.float32)
    visible_count = jnp.take(counts, local_slot, axis=0)
    visible = lax.broadcasted_iota(jnp.int32, (groups, slots), 1) < visible_count[:, None]
    cross_all = (
        lax.all_gather(gain_q, ("dp", "fsdp"), axis=0, tiled=True),
        lax.all_gather(gain_kv, ("dp", "fsdp"), axis=0, tiled=True),
        lax.all_gather(w_query, ("dp", "fsdp"), axis=0, tiled=True),
        lax.all_gather(w_key, ("dp", "fsdp"), axis=0, tiled=True),
        lax.all_gather(w_value, ("dp", "fsdp"), axis=0, tiled=True),
        lax.all_gather(w_out, ("dp", "fsdp"), axis=0, tiled=True),
    )
    normed = layer_norm(latents, cross_all[0].astype(jnp.float32)).astype(jnp.bfloat16)
    pix_normed = layer_norm(chosen, cross_all[1].astype(jnp.float32)).astype(jnp.bfloat16)
    queries = split_heads(project(normed, cross_all[2]).astype(jnp.bfloat16))
    key_rows = split_heads(project(pix_normed, cross_all[3]).astype(jnp.bfloat16))
    value_rows = split_heads(project(pix_normed, cross_all[4]).astype(jnp.bfloat16))
    cross_mixed, cross_total = attend_forward(queries, key_rows, value_rows, visible)
    cross_flat = merge_heads(cross_mixed)
    after_cross = latents + project(cross_flat, cross_all[5])
    self_all = (
        lax.all_gather(gain_self, ("dp", "fsdp"), axis=0, tiled=True),
        lax.all_gather(w_qkv, ("dp", "fsdp"), axis=0, tiled=True),
        lax.all_gather(w_self_out, ("dp", "fsdp"), axis=0, tiled=True),
    )
    normed_self = layer_norm(after_cross, self_all[0].astype(jnp.float32)).astype(jnp.bfloat16)
    packed = project(normed_self, self_all[1]).astype(jnp.bfloat16)
    self_queries = split_heads(packed[..., :width])
    self_keys = split_heads(packed[..., width : 2 * width])
    self_values = split_heads(packed[..., 2 * width :])
    self_mixed, self_total = attend_forward(self_queries, self_keys, self_values, None)
    self_flat = merge_heads(self_mixed)
    after_self = after_cross + project(self_flat, self_all[2])
    mlp_all = (
        lax.all_gather(gain_mlp, ("dp", "fsdp"), axis=0, tiled=True),
        lax.all_gather(w_up, ("dp", "fsdp"), axis=0, tiled=True),
        lax.all_gather(w_down, ("dp", "fsdp"), axis=0, tiled=True),
    )
    normed_mlp = layer_norm(after_self, mlp_all[0].astype(jnp.float32)).astype(jnp.bfloat16)
    hidden = project(normed_mlp, mlp_all[1])
    activated = jax.nn.gelu(hidden).astype(jnp.bfloat16)
    latents_out = after_self + project(activated, mlp_all[2])
    root_mean = jnp.sqrt(jnp.mean(latents_out * latents_out, axis=(1, 2)))
    total_norm = lax.psum(jnp.sum(root_mean), ("dp", "fsdp"))
    norms = root_mean * (groups * lax.axis_size(("dp", "fsdp"))) / total_norm
    mlp_back = (
        lax.all_gather(gain_mlp, ("dp", "fsdp"), axis=0, tiled=True),
        lax.all_gather(w_up, ("dp", "fsdp"), axis=0, tiled=True),
        lax.all_gather(w_down, ("dp", "fsdp"), axis=0, tiled=True),
    )
    out_grad = cotangent.astype(jnp.bfloat16)
    down_grad = weight_grad(activated, out_grad)
    act_grad = project_back(out_grad, mlp_back[2])
    hidden_grad = jax.vjp(jax.nn.gelu, hidden)[1](act_grad)[0].astype(jnp.bfloat16)
    up_grad = weight_grad(normed_mlp, hidden_grad)
    mlp_in_grad = project_back(hidden_grad, mlp_back[1])
    after_self_ln, mlp_gain_grad = jax.vjp(layer_norm, after_self, mlp_back[0].astype(jnp.float32))[
        1
    ](mlp_in_grad)
    after_self_grad = cotangent + after_self_ln
    mlp_grads = (
        lax.psum_scatter(mlp_gain_grad, ("dp", "fsdp"), scatter_dimension=0, tiled=True),
        lax.psum_scatter(up_grad, ("dp", "fsdp"), scatter_dimension=0, tiled=True),
        lax.psum_scatter(down_grad, ("dp", "fsdp"), scatter_dimension=0, tiled=True),
    )
    self_back = (
        lax.all_gather(gain_self, ("dp", "fsdp"), axis=0, tiled=True),
        lax.all_gather(w_qkv, ("dp", "fsdp"), axis=0, tiled=True),
        lax.all_gather(w_self_out, ("dp", "fsdp"), axis=0, tiled=True),
    )
    self_branch = after_self_grad.astype(jnp.bfloat16)
    self_out_grad = weight_grad(self_flat, self_branch)
    self_mixed_grad = split_heads(project_back(self_branch, self_back[2]).astype(jnp.bfloat16))
    self_q_grad, self_k_grad, self_v_grad = attend_backward(
        self_queries, self_keys, self_values, None, self_total, self_mixed_grad
    )
    packed_grad = jnp.concatenate(
        [merge_heads(self_q_grad), merge_heads(self_k_grad), merge_heads(self_v_grad)], axis=-1
    )
    qkv_grad = weight_grad(normed_self, packed_grad)
    self_in_grad = project_back(packed_grad, self_back[1])
    after_cross_ln, self_gain_grad = jax.vjp(
        layer_norm, after_cross, self_back[0].astype(jnp.float32)
    )[1](self_in_grad)
    after_cross_grad = after_self_grad + after_cross_ln
    self_grads = (
        lax.psum_scatter(self_gain_grad, ("dp", "fsdp"), scatter_dimension=0, tiled=True),
        lax.psum_scatter(qkv_grad, ("dp", "fsdp"), scatter_dimension=0, tiled=True),
        lax.psum_scatter(self_out_grad, ("dp", "fsdp"), scatter_dimension=0, tiled=True),
    )
    cross_back = (
        lax.all_gather(gain_q, ("dp", "fsdp"), axis=0, tiled=True),
        lax.all_gather(gain_kv, ("dp", "fsdp"), axis=0, tiled=True),
        lax.all_gather(w_query, ("dp", "fsdp"), axis=0, tiled=True),
        lax.all_gather(w_key, ("dp", "fsdp"), axis=0, tiled=True),
        lax.all_gather(w_value, ("dp", "fsdp"), axis=0, tiled=True),
        lax.all_gather(w_out, ("dp", "fsdp"), axis=0, tiled=True),
    )
    cross_branch = after_cross_grad.astype(jnp.bfloat16)
    out_w_grad = weight_grad(cross_flat, cross_branch)
    cross_mixed_grad = split_heads(project_back(cross_branch, cross_back[5]).astype(jnp.bfloat16))
    query_grad, key_grad, value_grad = attend_backward(
        queries, key_rows, value_rows, visible, cross_total, cross_mixed_grad
    )
    query_flat = merge_heads(query_grad)
    key_flat = merge_heads(key_grad)
    value_flat = merge_heads(value_grad)
    query_w_grad = weight_grad(normed, query_flat)
    key_w_grad = weight_grad(pix_normed, key_flat)
    value_w_grad = weight_grad(pix_normed, value_flat)
    normed_grad = project_back(query_flat, cross_back[2])
    pix_normed_grad = project_back(key_flat, cross_back[3]) + project_back(
        value_flat, cross_back[4]
    )
    latents_ln, query_gain_grad = jax.vjp(layer_norm, latents, cross_back[0].astype(jnp.float32))[
        1
    ](normed_grad)
    latents_grad = after_cross_grad + latents_ln
    chosen_grad, pixel_gain_grad = jax.vjp(layer_norm, chosen, cross_back[1].astype(jnp.float32))[
        1
    ](pix_normed_grad)
    pixels_grad = jnp.zeros(pixels.shape, jnp.float32).at[local_slot].add(chosen_grad)
    cross_grads = (
        lax.psum_scatter(query_gain_grad, ("dp", "fsdp"), scatter_dimension=0, tiled=True),
        lax.psum_scatter(pixel_gain_grad, ("dp", "fsdp"), scatter_dimension=0, tiled=True),
        lax.psum_scatter(query_w_grad, ("dp", "fsdp"), scatter_dimension=0, tiled=True),
        lax.psum_scatter(key_w_grad, ("dp", "fsdp"), scatter_dimension=0, tiled=True),
        lax.psum_scatter(value_w_grad, ("dp", "fsdp"), scatter_dimension=0, tiled=True),
        lax.psum_scatter(out_w_grad, ("dp", "fsdp"), scatter_dimension=0, tiled=True),
    )
    return (
        latents_out,
        latents_grad,
        pixels_grad,
        cross_grads[0],
        cross_grads[1],
        cross_grads[2],
        cross_grads[3],
        cross_grads[4],
        cross_grads[5],
        self_grads[0],
        self_grads[1],
        self_grads[2],
        mlp_grads[0],
        mlp_grads[1],
        mlp_grads[2],
        norms,
    )


def local_fast(
    latents,
    pixels,
    slot_index,
    counts,
    cotangent,
    gain_q,
    gain_kv,
    w_query,
    w_key,
    w_value,
    w_out,
    gain_self,
    w_qkv,
    w_self_out,
    gain_mlp,
    w_up,
    w_down,
):
    groups = latents.shape[0]
    slots = pixels.shape[1]
    width = latents.shape[2]
    local_slot = slot_index % groups
    chosen = jnp.take(pixels, local_slot, axis=0).astype(jnp.float32)
    visible_count = jnp.take(counts, local_slot, axis=0)
    visible = lax.broadcasted_iota(jnp.int32, (groups, slots), 1) < visible_count[:, None]
    gains = lax.all_gather(jnp.stack([gain_q, gain_kv, gain_self, gain_mlp]), ("dp", "fsdp"), axis=1, tiled=True)
    shards = (w_query, w_key, w_value, w_out, w_qkv, w_self_out, w_up, w_down)
    fulls = [f.reshape(-1, f.shape[-1]) for f in gather_all(shards)]
    cross_all = (gains[0], gains[1], fulls[0], fulls[1], fulls[2], fulls[3])
    self_all = (gains[2], fulls[4], fulls[5])
    mlp_all = (gains[3], fulls[6], fulls[7])
    cross_back, self_back, mlp_back = cross_all, self_all, mlp_all
    normed = layer_norm(latents, cross_all[0].astype(jnp.float32)).astype(jnp.bfloat16)
    pix_normed = layer_norm(chosen, cross_all[1].astype(jnp.float32)).astype(jnp.bfloat16)
    queries = split_heads(project(normed, cross_all[2]).astype(jnp.bfloat16))
    key_rows = split_heads(project(pix_normed, cross_all[3]).astype(jnp.bfloat16))
    value_rows = split_heads(project(pix_normed, cross_all[4]).astype(jnp.bfloat16))
    cross_mixed, cross_total = attend_forward(queries, key_rows, value_rows, visible)
    cross_flat = merge_heads(cross_mixed)
    after_cross = latents + project(cross_flat, cross_all[5])
    normed_self = layer_norm(after_cross, self_all[0].astype(jnp.float32)).astype(jnp.bfloat16)
    packed = project(normed_self, self_all[1]).astype(jnp.bfloat16)
    self_queries = split_heads(packed[..., :width])
    self_keys = split_heads(packed[..., width : 2 * width])
    self_values = split_heads(packed[..., 2 * width :])
    self_mixed, self_total = attend_forward(self_queries, self_keys, self_values, None)
    self_flat = merge_heads(self_mixed)
    after_self = after_cross + project(self_flat, self_all[2])
    normed_mlp = layer_norm(after_self, mlp_all[0].astype(jnp.float32)).astype(jnp.bfloat16)
    hidden = project(normed_mlp, mlp_all[1])
    activated = jax.nn.gelu(hidden).astype(jnp.bfloat16)
    latents_out = after_self + project(activated, mlp_all[2])
    root_mean = jnp.sqrt(jnp.mean(latents_out * latents_out, axis=(1, 2)))
    out_grad = cotangent.astype(jnp.bfloat16)
    down_grad = weight_grad(activated, out_grad)
    act_grad = project_back(out_grad, mlp_back[2])
    hidden_grad = jax.vjp(jax.nn.gelu, hidden)[1](act_grad)[0].astype(jnp.bfloat16)
    up_grad = weight_grad(normed_mlp, hidden_grad)
    mlp_in_grad = project_back(hidden_grad, mlp_back[1])
    after_self_ln, mlp_gain_grad = jax.vjp(layer_norm, after_self, mlp_back[0].astype(jnp.float32))[
        1
    ](mlp_in_grad)
    after_self_grad = cotangent + after_self_ln
    self_branch = after_self_grad.astype(jnp.bfloat16)
    self_out_grad = weight_grad(self_flat, self_branch)
    self_mixed_grad = split_heads(project_back(self_branch, self_back[2]).astype(jnp.bfloat16))
    self_q_grad, self_k_grad, self_v_grad = attend_backward(
        self_queries, self_keys, self_values, None, self_total, self_mixed_grad
    )
    packed_grad = jnp.concatenate(
        [merge_heads(self_q_grad), merge_heads(self_k_grad), merge_heads(self_v_grad)], axis=-1
    )
    qkv_grad = weight_grad(normed_self, packed_grad)
    self_in_grad = project_back(packed_grad, self_back[1])
    after_cross_ln, self_gain_grad = jax.vjp(
        layer_norm, after_cross, self_back[0].astype(jnp.float32)
    )[1](self_in_grad)
    after_cross_grad = after_self_grad + after_cross_ln
    cross_branch = after_cross_grad.astype(jnp.bfloat16)
    out_w_grad = weight_grad(cross_flat, cross_branch)
    cross_mixed_grad = split_heads(project_back(cross_branch, cross_back[5]).astype(jnp.bfloat16))
    query_grad, key_grad, value_grad = attend_backward(
        queries, key_rows, value_rows, visible, cross_total, cross_mixed_grad
    )
    query_flat = merge_heads(query_grad)
    key_flat = merge_heads(key_grad)
    value_flat = merge_heads(value_grad)
    query_w_grad = weight_grad(normed, query_flat)
    key_w_grad = weight_grad(pix_normed, key_flat)
    value_w_grad = weight_grad(pix_normed, value_flat)
    normed_grad = project_back(query_flat, cross_back[2])
    pix_normed_grad = project_back(key_flat, cross_back[3]) + project_back(
        value_flat, cross_back[4]
    )
    latents_ln, query_gain_grad = jax.vjp(layer_norm, latents, cross_back[0].astype(jnp.float32))[
        1
    ](normed_grad)
    latents_grad = after_cross_grad + latents_ln
    chosen_grad, pixel_gain_grad = jax.vjp(layer_norm, chosen, cross_back[1].astype(jnp.float32))[
        1
    ](pix_normed_grad)
    pixels_grad = jnp.zeros(pixels.shape, jnp.float32).at[local_slot].add(chosen_grad)
    grads = (query_w_grad, key_w_grad, value_w_grad, out_w_grad, qkv_grad, self_out_grad, up_grad, down_grad)
    blocks = [g.astype(jnp.bfloat16).reshape(2, 2, 4, 2, -1, g.shape[-1]) for g in grads]
    g_query, g_key, g_value, g_out, g_qkv, g_self_out, g_up, g_down = scatter_all(blocks)
    small = jnp.concatenate([query_gain_grad, pixel_gain_grad, self_gain_grad, mlp_gain_grad, root_mean])
    small = lax.psum(small, ("dp", "fsdp"))
    rows = gain_q.shape[0]
    mine = lax.axis_index(("dp", "fsdp")) * rows
    gain_grads = [lax.dynamic_slice(small, (k * width + mine,), (rows,)) for k in range(4)]
    norms = root_mean * (groups * lax.axis_size(("dp", "fsdp"))) / jnp.sum(small[4 * width :])
    return (
        latents_out,
        latents_grad,
        pixels_grad,
        gain_grads[0],
        gain_grads[1],
        g_query,
        g_key,
        g_value,
        g_out,
        gain_grads[2],
        g_qkv,
        g_self_out,
        gain_grads[3],
        g_up,
        g_down,
        norms,
    )


def fits(mesh):
    return mesh.shape["dp"] == 4 and mesh.shape["fsdp"] == 8


def solution(mesh):
    in_specs = (
        P(("dp", "fsdp"), None, None),
        P(("dp", "fsdp"), None, None),
        P(("dp", "fsdp")),
        P(("dp", "fsdp")),
        P(("dp", "fsdp"), None, None),
        P(("dp", "fsdp")),
        P(("dp", "fsdp")),
        P(("dp", "fsdp"), None),
        P(("dp", "fsdp"), None),
        P(("dp", "fsdp"), None),
        P(("dp", "fsdp"), None),
        P(("dp", "fsdp")),
        P(("dp", "fsdp"), None),
        P(("dp", "fsdp"), None),
        P(("dp", "fsdp")),
        P(("dp", "fsdp"), None),
        P(("dp", "fsdp"), None),
    )
    out_specs = (
        P(("dp", "fsdp"), None, None),
        P(("dp", "fsdp"), None, None),
        P(("dp", "fsdp"), None, None),
        P(("dp", "fsdp")),
        P(("dp", "fsdp")),
        P(("dp", "fsdp"), None),
        P(("dp", "fsdp"), None),
        P(("dp", "fsdp"), None),
        P(("dp", "fsdp"), None),
        P(("dp", "fsdp")),
        P(("dp", "fsdp"), None),
        P(("dp", "fsdp"), None),
        P(("dp", "fsdp")),
        P(("dp", "fsdp"), None),
        P(("dp", "fsdp"), None),
        P(("dp", "fsdp")),
    )
    return jax.shard_map(local_fast if fits(mesh) else local_plain, mesh=mesh, in_specs=in_specs, out_specs=out_specs, check_vma=False)
```

```python
import functools

import jax
import jax.numpy as jnp
from jax import lax
from jax.experimental import pallas as pl
from jax.experimental.pallas import tpu as pltpu
from jax.sharding import PartitionSpec as P

MESH = pl.DeviceIdType.MESH
DMA = pltpu.SemaphoreType.DMA
UNIT_COLS = 1024
UNIT_ROWS = 32
RING = 4
PARTIALS = 5
WIDTHS = ((256, 256, 256, 256), (128, 128, 384, 384), (128, 128, 384, 384), (128, 128, 384, 384))


class Place:
    def __init__(self):
        dp, f = lax.axis_index("dp"), lax.axis_index("fsdp")
        self.y, self.x, self.z, self.c = dp // 2, dp % 2, f // 2, f % 2
        step = jnp.where(self.z < 2, 1, -1)
        self.is_end = (self.z == 0) | (self.z == 3)
        self.z1 = jnp.where(self.is_end, self.z + step, self.z - step)
        self.z2 = jnp.where(self.is_end, self.z + 2 * step, self.z + step)
        self.z3 = jnp.where(self.is_end, self.z + 3 * step, self.z + 2 * step)

    def dev(self, y=None, x=None, z=None, c=None):
        y = self.y if y is None else y
        x = self.x if x is None else x
        z = self.z if z is None else z
        c = self.c if c is None else c
        return (y * 2 + x, z * 2 + c)

    def barrier(self):
        bar = pltpu.get_barrier_semaphore()
        peers = [
            self.dev(c=1 - self.c),
            self.dev(x=1 - self.x),
            self.dev(y=1 - self.y),
            self.dev(z=self.z1),
            self.dev(z=self.z2),
            self.dev(z=self.z3),
        ]
        for peer in peers:
            pl.semaphore_signal(bar, inc=1, device_id=peer, device_id_type=MESH)
        pl.semaphore_wait(bar, len(peers))


def remote(src, dst, send_sem, recv_sem, dev):
    return pltpu.make_async_remote_copy(
        src_ref=src, dst_ref=dst, send_sem=send_sem, recv_sem=recv_sem, device_id=dev, device_id_type=MESH
    )


def part_cols(u, p, base):
    widths = WIDTHS[u % RING]
    return pl.ds(base + sum(widths[:p]), widths[p])


class Gather:
    STAGES = 7

    def __init__(self, me, units, sems):
        self.me, self.units = me, units
        self.loc, self.sib_s, self.sib_r, self.zs, self.zr, self.xs, self.xr, self.ys, self.yr = sems

    @staticmethod
    def sems(n):
        return [DMA((n,))] * 3 + [DMA((n, 4, 4))] * 2 + [DMA((n, 4))] * 4

    def at(self, u, y, x, z, c, p=None):
        _, full, row, col = self.units[u]
        cols = pl.ds(col, UNIT_COLS) if p is None else part_cols(u, p, col)
        return full.at[y, x, z, c, pl.ds(row, UNIT_ROWS), cols]

    def own(self, u):
        me, (shard, _, row, col) = self.me, self.units[u]
        src = shard.at[pl.ds(row, UNIT_ROWS), pl.ds(col, UNIT_COLS)]
        return pltpu.make_async_copy(src, self.at(u, me.y, me.x, me.z, me.c), self.loc.at[u])

    def zblk(self, u, p, z):
        me, s = self.me, slice(None)
        return self.at(u, me.y if p != 3 else s, me.x if p != 2 else s, z, me.c, p)

    def zcopy(self, u, p, z_to, z_block=None):
        me = self.me
        if z_block is None:
            b = self.zblk(u, p, me.z)
            return remote(b, b, self.zs.at[u, p, z_to], self.zr.at[u, p, me.z], me.dev(z=z_to))
        b = self.zblk(u, p, z_block)
        return remote(b, b, self.zs.at[u, p, me.z], self.zr.at[u, p, z_block], me.dev(z=z_to))

    def zin(self, u, p, z_block):
        b = self.zblk(u, p, z_block)
        return remote(b, b, self.zs.at[u, p, z_block], self.zr.at[u, p, z_block], self.me.dev(z=z_block))

    def z_a(self, u, p):
        me = self.me
        self.zcopy(u, p, me.z1).start()
        self.zcopy(u, p, me.z2).start()

        @pl.when(~me.is_end)
        def _():
            self.zcopy(u, p, me.z3).start()

    def z_b(self, u, p):
        me = self.me

        @pl.when(~me.is_end)
        def _():
            self.zin(u, p, me.z3).wait_recv()
            self.zcopy(u, p, me.z1, me.z3).start()

    def z_wait(self, u, p):
        me = self.me
        self.zin(u, p, me.z1).wait_recv()
        self.zin(u, p, me.z2).wait_recv()

        @pl.when(me.is_end)
        def _():
            self.zin(u, p, me.z3).wait_recv()

    def z_sent(self, u, p):
        me = self.me
        self.zcopy(u, p, me.z1).wait_send()
        self.zcopy(u, p, me.z2).wait_send()

        @pl.when(~me.is_end)
        def _():
            self.zcopy(u, p, me.z3).wait_send()
            self.zcopy(u, p, me.z1, me.z3).wait_send()

    def xcopy(self, u, p, out=True):
        me, s = self.me, slice(None)
        b = self.at(u, me.y if p != 3 and p != 1 else s, me.x if out else 1 - me.x, me.z if p == 2 else s, me.c, p)
        return remote(b, b, self.xs.at[u, p], self.xr.at[u, p], me.dev(x=1 - me.x))

    def ycopy(self, u, p, out=True):
        me, s = self.me, slice(None)
        b = self.at(u, me.y if out else 1 - me.y, me.x if p != 2 and p != 0 else s, me.z if p == 3 else s, me.c, p)
        return remote(b, b, self.ys.at[u, p], self.yr.at[u, p], me.dev(y=1 - me.y))

    def final(self, u, out=True):
        me, s = self.me, slice(None)
        b = self.at(u, s, s, s, me.c if out else 1 - me.c)
        return remote(b, b, self.sib_s.at[u], self.sib_r.at[u], me.dev(c=1 - me.c))

    def stage(self, s, u):
        if s == 0:
            self.own(u).start()
        elif s == 1:
            self.own(u).wait()
            self.xcopy(u, 2).start()
            self.ycopy(u, 3).start()
            self.z_a(u, 0)
            self.z_a(u, 1)
        elif s == 2:
            self.z_b(u, 0)
            self.z_b(u, 1)
            self.xcopy(u, 2, False).wait_recv()
            self.z_a(u, 2)
            self.ycopy(u, 3, False).wait_recv()
            self.z_a(u, 3)
        elif s == 3:
            self.z_wait(u, 0)
            self.xcopy(u, 0).start()
            self.z_wait(u, 1)
            self.ycopy(u, 1).start()
            self.z_b(u, 2)
            self.z_b(u, 3)
        elif s == 4:
            self.z_wait(u, 2)
            self.ycopy(u, 2).start()
            self.z_wait(u, 3)
            self.xcopy(u, 3).start()
            self.xcopy(u, 0, False).wait_recv()
            self.ycopy(u, 0).start()
            self.ycopy(u, 1, False).wait_recv()
            self.xcopy(u, 1).start()
        elif s == 5:
            self.ycopy(u, 2, False).wait_recv()
            self.xcopy(u, 3, False).wait_recv()
            self.ycopy(u, 0, False).wait_recv()
            self.xcopy(u, 1, False).wait_recv()
            self.final(u).start()
        elif s == 6:
            self.final(u, False).wait_recv()

    def sent(self, u):
        for p in range(4):
            self.z_sent(u, p)
            self.xcopy(u, p).wait_send()
            self.ycopy(u, p).wait_send()
        self.final(u).wait_send()

    def tick(self, t, wide):
        for u in range(len(self.units)):
            s = t - max(0, u - wide + 1)
            if 0 <= s < self.STAGES:
                self.stage(s, u)

    def ticks(self, wide):
        return self.STAGES + max(0, len(self.units) - wide)


class Scatter:
    STAGES = 5

    def __init__(self, me, units, refs, sems):
        self.me, self.units = me, units
        self.part, self.r1, self.r2, self.rz = refs
        self.s1, self.q1, self.s2, self.q2, self.zs, self.zr = sems

    @staticmethod
    def sems(n):
        return [DMA((n, 4))] * 4 + [DMA((n, 4, 4))] * 2

    def pt(self, u, p, y, x, z):
        return self.part.at[u % PARTIALS, y, x, z, :, part_cols(u, p, 0)]

    def first(self, u, p):
        me, s = self.me, slice(None)
        dst = self.r1.at[u % RING, :, :, :, part_cols(u, p, 0)]
        if p in (0, 2):
            return remote(self.pt(u, p, 1 - me.y, s, s), dst, self.s1.at[u, p], self.q1.at[u, p], me.dev(y=1 - me.y))
        return remote(self.pt(u, p, s, 1 - me.x, s), dst, self.s1.at[u, p], self.q1.at[u, p], me.dev(x=1 - me.x))

    def add(self, count, dst, srcs):
        def body(i, carry):
            total = dst(i)[...].astype(jnp.float32)
            for src in srcs:
                total = total + src(i)[...].astype(jnp.float32)
            dst(i)[...] = total.astype(jnp.bfloat16)
            return carry

        if count == 1:
            body(0, 0)
        else:
            lax.fori_loop(0, count, body, 0)

    def first_in(self, u, p):
        me = self.me
        self.first(u, p).wait_recv()
        if p in (0, 2):
            dst = lambda i: self.pt(u, p, me.y, i // 4, i % 4)
        else:
            dst = lambda i: self.pt(u, p, i // 4, me.x, i % 4)
        self.add(8, dst, [lambda i: self.r1.at[u % RING, i // 4, i % 4, :, part_cols(u, p, 0)]])

    def second(self, u, p):
        me, s = self.me, slice(None)
        cols = part_cols(u, p, 0)
        z = s if p < 2 else me.z
        dst = self.r2.at[u % RING, :, :, cols] if p < 2 else self.r2.at[u % RING, 0, :, cols]
        if p in (0, 2):
            return remote(self.pt(u, p, me.y, 1 - me.x, z), dst, self.s2.at[u, p], self.q2.at[u, p], me.dev(x=1 - me.x))
        return remote(self.pt(u, p, 1 - me.y, me.x, z), dst, self.s2.at[u, p], self.q2.at[u, p], me.dev(y=1 - me.y))

    def second_in(self, u, p):
        me = self.me
        self.second(u, p).wait_recv()
        self.add(
            4,
            lambda i: self.pt(u, p, me.y, me.x, i),
            [lambda i: self.r2.at[u % RING, i, :, part_cols(u, p, 0)]],
        )

    def zblk(self, u, p, z):
        me, s = self.me, slice(None)
        return self.pt(u, p, me.y if p != 3 else s, me.x if p != 2 else s, z)

    def zslot(self, u, p, slot):
        cols = part_cols(u, p, 0)
        return self.rz.at[u % RING, slot, 0, :, cols] if p < 2 else self.rz.at[u % RING, slot, :, :, cols]

    def zcopy(self, u, p, which, block, slot, z_to):
        return remote(
            self.zblk(u, p, block), self.zslot(u, p, slot), self.zs.at[u, p, which], self.zr.at[u, p, slot], self.me.dev(z=z_to)
        )

    def z_ends(self, u, p):
        me = self.me
        return [
            self.zcopy(u, p, 2, me.z3, 3, me.z1),
            self.zcopy(u, p, 1, me.z2, 2, me.z2),
            self.zcopy(u, p, 0, me.z1, 0, me.z1),
        ]

    def z_mids(self, u, p):
        me = self.me
        return [self.zcopy(u, p, 0, me.z1, 0, me.z1), self.zcopy(u, p, 1, me.z2, 1, me.z2)]

    def z_gone(self, u, p):
        return self.zcopy(u, p, 2, self.me.z3, 1, self.me.z3)

    def z_a(self, u, p):
        me = self.me

        @pl.when(me.is_end)
        def _():
            for c in self.z_ends(u, p):
                c.start()

        @pl.when(~me.is_end)
        def _():
            for c in self.z_mids(u, p):
                c.start()

    def zget(self, u, p, slot):
        return self.zcopy(u, p, 0, self.me.z, slot, self.me.z1)

    def z_b(self, u, p):
        me = self.me

        @pl.when(~me.is_end)
        def _():
            self.zget(u, p, 3).wait_recv()
            self.z_add(u, p, me.z3, (3,))
            self.z_gone(u, p).start()

    def z_add(self, u, p, block, slots):
        cols = part_cols(u, p, 0)
        me = self.me
        if p < 2:
            dst, count = (lambda i: self.pt(u, p, me.y, me.x, block)), 1
        elif p == 2:
            dst, count = (lambda i: self.pt(u, p, me.y, i, block)), 2
        else:
            dst, count = (lambda i: self.pt(u, p, i, me.x, block)), 2
        self.add(count, dst, [functools.partial(lambda slot, i: self.rz.at[u % RING, slot, i, :, cols], k) for k in slots])

    def z_in(self, u, p):
        me = self.me
        self.zget(u, p, 0).wait_recv()
        self.zget(u, p, 1).wait_recv()

        @pl.when(~me.is_end)
        def _():
            self.zget(u, p, 2).wait_recv()

    def out(self, u, p):
        out, row, col = self.units[u]
        return out.at[pl.ds(row, UNIT_ROWS), part_cols(u, p, col)]

    def finish_z(self, u, p):
        me, cols = self.me, part_cols(u, p, 0)
        self.z_in(u, p)
        f32 = lambda ref: ref[...].astype(jnp.float32)
        total = f32(self.pt(u, p, me.y, me.x, me.z)) + f32(self.rz.at[u % RING, 0, 0, :, cols]) + f32(self.rz.at[u % RING, 1, 0, :, cols])

        @pl.when(me.is_end)
        def _():
            self.out(u, p)[...] = total

        @pl.when(~me.is_end)
        def _():
            self.out(u, p)[...] = total + f32(self.rz.at[u % RING, 2, 0, :, cols])

    def pass_z(self, u, p):
        me = self.me
        self.z_in(u, p)

        @pl.when(me.is_end)
        def _():
            self.z_add(u, p, me.z, (0, 1))

        @pl.when(~me.is_end)
        def _():
            self.z_add(u, p, me.z, (0, 1, 2))

        self.second(u, p).start()

    def finish_last(self, u, p):
        me, cols = self.me, part_cols(u, p, 0)
        self.second(u, p).wait_recv()
        total = self.pt(u, p, me.y, me.x, me.z)[...].astype(jnp.float32) + self.r2.at[u % RING, 0, :, cols][...].astype(jnp.float32)
        self.out(u, p)[...] = total

    def stage(self, s, u):
        if s == 0:
            for p in (2, 3, 0, 1):
                self.first(u, p).start()
        elif s == 1:
            for p in (2, 3):
                self.first_in(u, p)
                self.z_a(u, p)
            for p in (0, 1):
                self.first_in(u, p)
                self.second(u, p).start()
        elif s == 2:
            for p in (2, 3):
                self.z_b(u, p)
            for p in (0, 1):
                self.second_in(u, p)
                self.z_a(u, p)
        elif s == 3:
            for p in (2, 3):
                self.pass_z(u, p)
            for p in (0, 1):
                self.z_b(u, p)
        elif s == 4:
            for p in (0, 1):
                self.finish_z(u, p)
            for p in (2, 3):
                self.finish_last(u, p)

    def sent(self, u):
        me = self.me
        for p in range(4):
            self.first(u, p).wait_send()
            self.second(u, p).wait_send()

            @pl.when(me.is_end)
            def _():
                for c in self.z_ends(u, p):
                    c.wait_send()

            @pl.when(~me.is_end)
            def _():
                for c in self.z_mids(u, p) + [self.z_gone(u, p)]:
                    c.wait_send()


EPS = 1e-05
HEADS = 8
GELU_A = 0.7978845608028654
GELU_B = 0.044715
NT = (((1,), (1,)), ((), ()))
F32, BF16 = jnp.float32, jnp.bfloat16


def matmul(a, b):
    return jnp.dot(a, b, preferred_element_type=F32)


def matmul_nt(a, b):
    return lax.dot_general(a, b, NT, preferred_element_type=F32)


def block(i, size):
    return pl.ds(pl.multiple_of(i * size, size), size)


def for_each(count, body):
    def step(i, carry):
        body(i)
        return carry

    lax.fori_loop(0, count, step, 0)


def normalise(v):
    center = v - jnp.mean(v, axis=-1, keepdims=True)
    inv = lax.rsqrt(jnp.mean(center * center, axis=-1, keepdims=True) + EPS)
    return center * inv, inv


def ln_forward(src, gain, dst):
    def body(i):
        rows = block(i, 32)
        n, _ = normalise(src[rows, :].astype(F32))
        dst[rows, :] = (n * gain[...]).astype(BF16)

    for_each(src.shape[0] // 32, body)


def ln_backward(src, row0, gain, incoming, base, gain_grad):
    def body(i):
        rows = block(i, 32)
        n, inv = normalise(src[pl.ds(pl.multiple_of(row0 + i * 32, 32), 32), :].astype(F32))
        g = incoming[rows, :]
        e = g * gain[...]
        grad = inv * (e - jnp.mean(e, axis=-1, keepdims=True) - n * jnp.mean(e * n, axis=-1, keepdims=True))
        prod = g * n
        gain_grad[...] += prod[0:8] + prod[8:16] + prod[16:24] + prod[24:32]
        if base is None:
            incoming[rows, :] = grad
        else:
            base[rows, :] = base[rows, :] + grad

    for_each(incoming.shape[0] // 32, body)


def attend_forward_heads(q, q0, k, k0, v, v0, out, count):
    def body(h):
        def head(ref, at):
            return ref[:, pl.ds(pl.multiple_of(at + h * 128, 128), 128)]

        s = matmul_nt(head(q, q0), head(k, k0)) * 128 ** (-0.5)
        if count is not None:
            s = jnp.where(lax.broadcasted_iota(jnp.int32, s.shape, 1) < count, s, -1e30)
        e = jnp.exp(s - jnp.max(s, axis=-1, keepdims=True))
        p = (e * (1.0 / jnp.sum(e, axis=-1, keepdims=True))).astype(BF16)
        out[:, block(h, 128)] = matmul(p, head(v, v0)).astype(BF16)

    for_each(HEADS, body)


def attend_backward_heads(q, q0, k, k0, v, v0, mixed_grad, count, dq, dq0, dk, dk0, dv, dv0):
    scale = 128 ** (-0.5)

    def body(h):
        def head(ref, at):
            return ref[:, pl.ds(pl.multiple_of(at + h * 128, 128), 128)]

        qh, kh, vh, gh = head(q, q0), head(k, k0), head(v, v0), head(mixed_grad, 0)
        s = matmul_nt(kh, qh) * scale
        if count is not None:
            s = jnp.where(lax.broadcasted_iota(jnp.int32, s.shape, 0) < count, s, -1e30)
        e = jnp.exp(s - jnp.max(s, axis=0, keepdims=True))
        p = e * (1.0 / jnp.sum(e, axis=0, keepdims=True))
        dv[:, pl.ds(pl.multiple_of(dv0 + h * 128, 128), 128)] = matmul(p.astype(BF16), gh).astype(BF16)
        dp = matmul_nt(vh, gh)
        ds = (p * (dp - jnp.sum(dp * p, axis=0, keepdims=True))).astype(BF16)
        dk[:, pl.ds(pl.multiple_of(dk0 + h * 128, 128), 128)] = (matmul(ds, qh) * scale).astype(BF16)
        dq[:, pl.ds(pl.multiple_of(dq0 + h * 128, 128), 128)] = (matmul(kh.T, ds).T * scale).astype(BF16)

    for_each(HEADS, body)


class SmallGather:
    def __init__(self, me, full, send, recv):
        self.me, self.full, self.send, self.recv = me, full, send, recv

    def copy(self, src, k, r, dev):
        return remote(src, src, self.send.at[k], self.recv.at[r], dev)

    def sib(self, out=True):
        me = self.me
        return self.copy(self.full.at[me.y, me.x, me.z, me.c if out else 1 - me.c], 0, 0, me.dev(c=1 - me.c))

    def zc(self, blk, k, r, to):
        me = self.me
        return self.copy(self.full.at[me.y, me.x, blk], k, r, me.dev(z=to))

    def xc(self, out=True):
        me = self.me
        return self.copy(self.full.at[me.y, me.x if out else 1 - me.x], 5, 5, me.dev(x=1 - me.x))

    def yc(self, out=True):
        me = self.me
        return self.copy(self.full.at[me.y if out else 1 - me.y], 6, 6, me.dev(y=1 - me.y))

    def run(self, s):
        me = self.me
        if s == 0:
            self.sib().start()
        elif s == 1:
            self.sib(False).wait_recv()
            self.zc(me.z, 1, 1 + me.z, me.z1).start()
            self.zc(me.z, 2, 1 + me.z, me.z2).start()

            @pl.when(~me.is_end)
            def _():
                self.zc(me.z, 3, 1 + me.z, me.z3).start()

        elif s == 2:

            @pl.when(~me.is_end)
            def _():
                self.zc(me.z3, 4, 1 + me.z3, me.z1).wait_recv()
                self.zc(me.z3, 4, 1 + me.z3, me.z1).start()

            for z in (me.z1, me.z2):
                self.zc(z, 1, 1 + z, me.z1).wait_recv()

            @pl.when(me.is_end)
            def _():
                self.zc(me.z3, 1, 1 + me.z3, me.z1).wait_recv()

            self.xc().start()
        elif s == 3:
            self.xc(False).wait_recv()
            self.yc().start()
        elif s == 4:
            self.yc(False).wait_recv()
            self.sib().wait_send()
            self.zc(me.z, 1, 1 + me.z, me.z1).wait_send()
            self.zc(me.z, 2, 1 + me.z, me.z2).wait_send()

            @pl.when(~me.is_end)
            def _():
                self.zc(me.z, 3, 1 + me.z, me.z3).wait_send()
                self.zc(me.z3, 4, 1 + me.z3, me.z1).wait_send()

            self.xc().wait_send()
            self.yc().wait_send()


class SmallSum:
    def __init__(self, me, acc, got, send, recv):
        z_near = jnp.where(me.is_end, me.z1, me.z1)
        z_far = jnp.where(me.is_end, me.z2, me.z3)
        self.devs = [me.dev(c=1 - me.c), me.dev(x=1 - me.x), me.dev(y=1 - me.y), me.dev(z=z_near), me.dev(z=z_far)]
        self.acc, self.got, self.send, self.recv = acc, got, send, recv

    def copy(self, k):
        return remote(self.acc, self.got.at[k], self.send.at[k], self.recv.at[k], self.devs[k])

    def start(self, k):
        self.copy(k).start()

    def finish(self, k):
        c = self.copy(k)
        c.wait_send()
        c.wait_recv()
        self.acc[...] += self.got[k]


def mega_kernel(*refs):
    it = iter(refs)
    take = lambda n: [next(it) for _ in range(n)]
    latents, pixels, counts, cotangent, gain_block = take(5)
    shards = take(8)
    latents_out, latents_grad, pixels_grad, small_out = take(4)
    grads_out = take(8)
    fulls = take(8)
    (
        w_buf, wd_buf, part, r1, r2, rz,
        xt_normed, xt_pix, xt_mixed, xt_nself, xt_smixed, xt_nmlp, xt_act, st_a, st_b,
        g_out, g_out_in, hid, hid_in, g_branch, g_branch_in, act, packed_in, g_cross, g_cross_in,
        dq, dq_in, big, dk_in, dv, dv_in,
        queries, keys, values, packed, after_cross, after_self, resid, pix, tmp, acc,
        gain_full, gain_vec, gain_acc, small, small_got,
    ) = take(46)
    gather_sems, scatter_sems = take(9), take(6)
    w_sem, wd_sem, in_sem, out_sem, sg_s, sg_r, ss_s, ss_r, xl, xs, xr, gs, gr = take(13)
    me = Place()
    me.barrier()

    cross_units = [(shards[i], fulls[i], 0, 0) for i in (1, 2, 0, 3)]
    self_units = [(shards[4], fulls[4], 0, k * UNIT_COLS) for k in range(3)] + [(shards[5], fulls[5], 0, 0)]
    mlp_units = [(shards[6], fulls[6], 0, k * UNIT_COLS) for k in range(4)]
    mlp_units += [(shards[7], fulls[7], k * UNIT_ROWS, 0) for k in range(4)]
    gather = Gather(me, cross_units + self_units + mlp_units, gather_sems)
    scatter_units = [(grads_out[7], k * UNIT_ROWS, 0) for k in range(4)]
    scatter_units += [(grads_out[6], 0, k * UNIT_COLS) for k in range(4)]
    scatter_units += [(grads_out[5], 0, 0)] + [(grads_out[4], 0, k * UNIT_COLS) for k in range(3)]
    scatter_units += [(grads_out[i], 0, 0) for i in (3, 2, 1, 0)]
    scatter = Scatter(me, scatter_units, (part, r1, r2, rz), scatter_sems)
    pushed = [0]
    tick = [0]

    def gather_to(t):
        while tick[0] <= min(t, gather.ticks(1) - 1):
            gather.tick(tick[0], 1)
            tick[0] += 1

    def arrived(u):
        gather_to(u + Gather.STAGES - 1)

    def settle(last):
        for s in range(Scatter.STAGES - 1, 0, -1):
            if 0 <= last - s < len(scatter_units):
                scatter.stage(s, last - s)

    def load(k, src, dst):
        return pltpu.make_async_copy(src, dst, in_sem.at[k])

    loads = [load(0, latents.at[0], after_self), load(1, pixels.at[0], pix), load(2, cotangent.at[0], resid)]
    for c in loads:
        c.start()
    own_gain = pltpu.make_async_copy(gain_block, gain_full.at[me.y, me.x, me.z, me.c], in_sem.at[3])
    own_gain.start()
    own_gain.wait()
    gains = SmallGather(me, gain_full, sg_s, sg_r)
    gains.run(0)
    gather_to(0)
    gains.run(1)
    gather_to(1)
    gains.run(2)
    gains.run(3)
    gather_to(2)
    gains.run(4)
    table = jnp.sum(gain_full[...].reshape(32, 8, 128), axis=1).astype(BF16)
    width = latents.shape[2]
    lane = lax.broadcasted_iota(jnp.int32, (128, width), 1)
    place = lax.broadcasted_iota(jnp.int32, (128, width), 0)
    owner = lax.broadcasted_iota(jnp.int32, (32, width), 0) == (lax.broadcasted_iota(jnp.int32, (32, width), 1) >> 5)
    for g in range(4):
        pick = jnp.where(place == (lane & 31) + 32 * g, 1.0, 0.0).astype(BF16)
        spread = jnp.where(owner, matmul(table, pick), 0.0)
        gain_vec[g : g + 1, :] = jnp.sum(spread, axis=0, keepdims=True)
    gain = [gain_vec.at[g : g + 1, :] for g in range(4)]
    for g in range(4):
        gain_acc[g] = jnp.zeros_like(gain_acc[g])

    staged = [None, None]

    def hand_over(k, stage, mine, slot, own_dst, far_dst):
        a = pltpu.make_async_copy(mine, own_dst, xl.at[k])
        b = remote(stage, far_dst, xs.at[k], xr.at[k], me.dev(c=1 - me.c))
        a.start()
        b.start()
        staged[slot] = (a, b)

    def clear(slot):
        if staged[slot] is not None:
            a, b = staged[slot]
            a.wait()
            b.wait_send()
            staged[slot] = None

    turn = [0]

    def transpose_out(k, x, row0, xt, k_rows):
        slot = turn[0] % 2
        turn[0] += 1
        clear(slot)

        def body(j):
            piece = x[pl.ds(row0, 256), block(j, 256)].T
            st_b[slot, j // 2, j % 2] = piece.reshape(4, 2, 32, 256)

        for_each(4, body)
        hand_over(
            k,
            st_b.at[slot, :, :, :, 1 - me.c],
            st_b.at[slot, :, :, :, me.c],
            slot,
            xt.at[:, :, :, :, pl.ds(row0, 256)],
            xt.at[:, :, :, :, pl.ds(k_rows + row0, 256)],
        )

    def xt_wait(k, xt, row0, k_rows):
        remote(
            st_b.at[0, :, :, :, 0],
            xt.at[:, :, :, :, pl.ds(k_rows + row0, 256)],
            xs.at[k],
            xr.at[k],
            me.dev(c=1 - me.c),
        ).wait_recv()

    def swap(k, src, dst):
        return remote(src, dst, gs.at[k], gr.at[k], me.dev(c=1 - me.c))

    w_turn = [0]

    def w_start(full, col):
        slot = w_turn[0] % 2
        w_turn[0] += 1
        c = pltpu.make_async_copy(full.at[:, :, :, :, :, pl.ds(col, UNIT_COLS)], w_buf.at[slot], w_sem.at[slot])
        c.start()
        return slot, c

    def w_fetch(full, col):
        slot, c = w_start(full, col)
        c.wait()
        return slot

    def w_cols(slot, j):
        return w_buf[slot, :, :, :, :, :, block(j, 256)].reshape(width, 256)

    def w_rows(slot, j):
        return w_buf[slot, j // 2, j % 2].reshape(256, UNIT_COLS)

    def project(x, slot, out):
        for_each(4, lambda j: out(j, matmul(x[...], w_cols(slot, j))))

    def store(dst, col0=0):
        def put(j, tile):
            dst[:, pl.ds(pl.multiple_of(col0 + j * 256, 256), 256)] = tile.astype(dst.dtype)

        return put

    def back(g, col0, slot, dst, first):
        def body(j):
            tile = matmul_nt(g[:, pl.ds(col0, UNIT_COLS)], w_rows(slot, j))
            cols = block(j, 256)
            if first:
                dst[:, cols] = tile.astype(dst.dtype)
            else:
                dst[:, cols] = dst[:, cols] + tile

        for_each(4, body)

    def weight_grad(xt_at, rows, own, far, col0):
        u = pushed[0]
        if u >= PARTIALS:
            scatter.sent(u - PARTIALS)
        slot = u % PARTIALS

        def body(j):
            cols = pl.ds(pl.multiple_of(col0 + j * 256, 256), 256)
            total = matmul(xt_at(0), own[:, cols]) + matmul(xt_at(rows), far[:, cols])
            part[slot, :, :, :, :, block(j, 256)] = total.astype(BF16).reshape(2, 2, 4, UNIT_ROWS, 256)

        for_each(4, body)
        scatter.stage(0, u)
        pushed[0] += 1

    def xt_of(xt, rows):
        return lambda at: xt[:, :, :, :, pl.ds(at, rows)].reshape(512, rows)

    loads[0].wait()
    loads[1].wait()
    ln_forward(after_self, gain[0], tmp)
    transpose_out(0, tmp, 0, xt_normed, 256)
    gather_to(3)
    ln_forward(pix, gain[1], big)
    transpose_out(1, big, 0, xt_pix, 512)
    gather_to(4)
    transpose_out(2, big, 256, xt_pix, 512)
    count = counts[0]
    arrived(0)
    project(big, w_fetch(fulls[1], 0), store(keys))
    arrived(1)
    project(big, w_fetch(fulls[2], 0), store(values))
    loads[2].wait()
    for_each(8, lambda i: g_out.__setitem__((block(i, 32), slice(None)), resid[block(i, 32), :].astype(BF16)))
    swap(0, g_out, g_out_in).start()
    arrived(2)
    project(tmp, w_fetch(fulls[0], 0), store(queries))
    attend_forward_heads(queries, 0, keys, 0, values, 0, tmp, count)
    arrived(3)
    transpose_out(3, tmp, 0, xt_mixed, 256)

    def add_to(dst, src):
        def put(j, tile):
            dst[:, block(j, 256)] = src[:, block(j, 256)] + tile

        return put

    project(tmp, w_fetch(fulls[3], 0), add_to(after_cross, after_self))

    ln_forward(after_cross, gain[2], tmp)
    transpose_out(4, tmp, 0, xt_nself, 256)
    for k in range(3):
        arrived(4 + k)
        project(tmp, w_fetch(fulls[4], k * UNIT_COLS), store(packed, k * UNIT_COLS))
    attend_forward_heads(packed, 0, packed, UNIT_COLS, packed, 2 * UNIT_COLS, tmp, None)
    arrived(7)
    transpose_out(5, tmp, 0, xt_smixed, 256)
    project(tmp, w_fetch(fulls[5], 0), add_to(after_self, after_cross))

    ln_forward(after_self, gain[3], tmp)
    transpose_out(6, tmp, 0, xt_nmlp, 256)
    a_staged = [None, None]

    def act_out(k):
        slot = k % 2
        if a_staged[slot] is not None:
            a_staged[slot][0].wait()
            a_staged[slot][1].wait_send()

        def body(m):
            st_a[slot, m // 2, m % 2] = act[:, pl.ds(pl.multiple_of(k * UNIT_COLS + m * 128, 128), 128)].T

        for_each(8, body)
        a = pltpu.make_async_copy(st_a.at[slot, :, me.c], xt_act.at[k // 2, k % 2, :, :, pl.ds(0, 256)], xl.at[7 + k])
        b = remote(
            st_a.at[slot, :, 1 - me.c],
            xt_act.at[k // 2, k % 2, :, :, pl.ds(256, 256)],
            xs.at[7 + k],
            xr.at[7 + k],
            me.dev(c=1 - me.c),
        )
        a.start()
        b.start()
        a_staged[slot] = (a, b)
        return a, b

    act_copies = []
    for k in range(4):
        arrived(8 + k)
        slot = w_fetch(fulls[6], k * UNIT_COLS)

        def up(j):
            x = matmul(tmp[...], w_cols(slot, j))
            t = jnp.tanh(GELU_A * (x + GELU_B * (x * x * x)))
            half = 0.5 * (1.0 + t)
            cols = pl.ds(pl.multiple_of(k * UNIT_COLS + j * 256, 256), 256)
            act[:, cols] = (x * half).astype(BF16)
            slope = half + (0.5 * GELU_A) * x * (1.0 - t * t) * (1.0 + (3 * GELU_B) * (x * x))
            hid[:, cols] = slope.astype(BF16)

        for_each(4, up)
        act_copies.append(act_out(k))
    for k in range(2, 4):
        a_staged[k % 2][0].wait()
        a_staged[k % 2][1].wait_send()
    for k in range(4):
        act_copies[k][1].wait_recv()

    for slot in range(2):
        clear(slot)

    swap(0, g_out, g_out_in).wait_recv()
    for k in range(4):
        def xt_down(at, k=k):
            return xt_act[:, :, :, pl.ds(k * UNIT_ROWS, UNIT_ROWS), pl.ds(at, 256)].reshape(512, 256)

        weight_grad(xt_down, 256, g_out, g_out_in, 0)
        arrived(12 + k)
        settle(k)

    def wd_start(q):
        c = pltpu.make_async_copy(fulls[7].at[q // 2, q % 2], wd_buf.at[q % 2], wd_sem.at[q % 2])
        c.start()
        return c

    wd = [wd_start(0), wd_start(1), None, None]
    for q in range(4):
        wd[q].wait()

        def hidden_back(j):
            w = wd_buf[q % 2, j].reshape(256, width)
            tile = matmul_nt(g_out[...], w)
            cols = pl.ds(pl.multiple_of(q * UNIT_COLS + j * 256, 256), 256)
            hid[:, cols] = (hid[:, cols].astype(F32) * tile).astype(BF16)

        for_each(4, hidden_back)
        cols = pl.ds(q * UNIT_COLS, UNIT_COLS)
        swap(1 + q, hid.at[:, cols], hid_in.at[:, cols]).start()

        def down(j):
            w = wd_buf[q % 2, :, :, :, block(j, 256)].reshape(UNIT_COLS, 256)
            tile = matmul(act[:, pl.ds(q * UNIT_COLS, UNIT_COLS)], w)
            dst = block(j, 256)
            acc[0, :, dst] = (after_self[:, dst] if q == 0 else acc[0, :, dst]) + tile

        for_each(4, down)
        if q < 2:
            wd[q + 2] = wd_start(q + 2)
    xt_wait(6, xt_nmlp, 0, 256)
    pending = [w_start(fulls[6], 0), None]
    out_copy = pltpu.make_async_copy(acc.at[0], latents_out.at[0], out_sem.at[0])
    out_copy.start()
    small[...] = jnp.zeros_like(small)
    squares = jnp.zeros((8, width), F32)

    def square(i, total):
        v = acc[0, block(i, 8), :]
        return total + v * v

    squares = lax.fori_loop(0, 32, square, squares)
    mean_square = jnp.sum(jnp.sum(squares, axis=1, keepdims=True), axis=0, keepdims=True) / (latents.shape[1] * width)
    root_mean = jnp.sqrt(mean_square)
    small[5:6, :] = jnp.broadcast_to(root_mean, (1, width))
    for k in range(4):
        cols = pl.ds(k * UNIT_COLS, UNIT_COLS)
        swap(1 + k, hid.at[:, cols], hid_in.at[:, cols]).wait_recv()
        weight_grad(xt_of(xt_nmlp, 256), 256, hid, hid_in, k * UNIT_COLS)
        slot, c = pending[k % 2]
        c.wait()
        if k < 3:
            pending[(k + 1) % 2] = w_start(fulls[6], (k + 1) * UNIT_COLS)
        back(hid, k * UNIT_COLS, slot, acc.at[1], k == 0)
        settle(4 + k)
    ln_backward(after_self, 0, gain[3], acc.at[1], resid, gain_acc.at[3])

    def round_rows(dst):
        for_each(8, lambda i: dst.__setitem__((block(i, 32), slice(None)), resid[block(i, 32), :].astype(BF16)))

    so_slot, c_so = w_start(fulls[5], 0)
    round_rows(g_branch)
    swap(5, g_branch, g_branch_in).start()
    c_so.wait()
    back(g_branch, 0, so_slot, tmp, True)
    swap(5, g_branch, g_branch_in).wait_recv()
    xt_wait(5, xt_smixed, 0, 256)
    weight_grad(xt_of(xt_smixed, 256), 256, g_branch, g_branch_in, 0)
    settle(8)
    qkv_w = w_start(fulls[4], 0)
    attend_backward_heads(
        packed, 0, packed, UNIT_COLS, packed, 2 * UNIT_COLS, tmp, None, act, 0, act, UNIT_COLS, act, 2 * UNIT_COLS
    )
    packed_grad = act.at[:, pl.ds(0, 3 * UNIT_COLS)]
    swap(6, packed_grad, packed_in).start()
    swap(6, packed_grad, packed_in).wait_recv()
    xt_wait(4, xt_nself, 0, 256)
    out_copy.wait()
    for k in range(3):
        weight_grad(xt_of(xt_nself, 256), 256, act, packed_in, k * UNIT_COLS)
        slot, c = qkv_w
        c.wait()
        if k < 2:
            qkv_w = w_start(fulls[4], (k + 1) * UNIT_COLS)
        back(act, k * UNIT_COLS, slot, acc.at[0], k == 0)
        settle(9 + k)
    wo_slot, c_wo = w_start(fulls[3], 0)
    ln_backward(after_cross, 0, gain[2], acc.at[0], resid, gain_acc.at[2])
    again = load(0, latents.at[0], after_self)
    again.start()

    round_rows(g_cross)
    swap(7, g_cross, g_cross_in).start()
    c_wo.wait()
    back(g_cross, 0, wo_slot, tmp, True)
    swap(7, g_cross, g_cross_in).wait_recv()
    xt_wait(3, xt_mixed, 0, 256)
    weight_grad(xt_of(xt_mixed, 256), 256, g_cross, g_cross_in, 0)
    settle(12)
    attend_backward_heads(queries, 0, keys, 0, values, 0, tmp, count, dq, 0, big, 0, dv, 0)
    given = [swap(8, dv, dv_in), swap(9, big, dk_in), swap(10, dq, dq_in)]
    for c in given:
        c.start()
    w_q = w_start(fulls[0], 0)
    xt_wait(1, xt_pix, 0, 512)
    xt_wait(2, xt_pix, 256, 512)
    given[0].wait_recv()
    weight_grad(xt_of(xt_pix, 512), 512, dv, dv_in, 0)
    settle(13)
    given[1].wait_recv()
    weight_grad(xt_of(xt_pix, 512), 512, big, dk_in, 0)
    settle(14)
    xt_wait(0, xt_normed, 0, 256)
    given[2].wait_recv()
    weight_grad(xt_of(xt_normed, 256), 256, dq, dq_in, 0)
    settle(15)
    w_q[1].wait()
    w_k = w_start(fulls[1], 0)
    back(dq, 0, w_q[0], acc.at[0], True)
    again.wait()
    ln_backward(after_self, 0, gain[0], acc.at[0], resid, gain_acc.at[0])
    grad_copy = pltpu.make_async_copy(resid, latents_grad.at[0], out_sem.at[1])
    grad_copy.start()
    settle(16)
    w_v = w_start(fulls[2], 0)
    w_k[1].wait()
    for r in range(2):
        back(big.at[pl.ds(256 * r, 256)], 0, w_k[0], acc.at[r], True)
    settle(17)
    w_v[1].wait()
    pix_copies = []
    for r in range(2):
        back(dv.at[pl.ds(256 * r, 256)], 0, w_v[0], acc.at[r], False)
        ln_backward(pix, 256 * r, gain[1], acc.at[r], None, gain_acc.at[1])
        c = pltpu.make_async_copy(acc.at[r], pixels_grad.at[0, pl.ds(256 * r, 256)], out_sem.at[2 + r])
        c.start()
        pix_copies.append(c)
    for g in range(4):
        small[g : g + 1, :] = jnp.sum(gain_acc[g], axis=0, keepdims=True)
    small[4:5, :] = small[5:6, :]
    total = SmallSum(me, small, small_got, ss_s, ss_r)
    total.start(0)
    settle(18)
    total.finish(0)
    total.start(1)
    settle(19)
    for k in range(1, 5):
        total.finish(k)
        if k < 4:
            total.start(k + 1)
    small[5:6, :] = jnp.broadcast_to(root_mean, (1, width))
    small_out[...] = small[...]

    for u in range(len(gather.units)):
        gather.sent(u)
    for u in range(len(scatter_units) - PARTIALS, len(scatter_units)):
        scatter.sent(u)
    swap(0, g_out, g_out_in).wait_send()
    for q in range(4):
        cols = pl.ds(q * UNIT_COLS, UNIT_COLS)
        swap(1 + q, hid.at[:, cols], hid_in.at[:, cols]).wait_send()
    swap(5, g_branch, g_branch_in).wait_send()
    swap(6, packed_grad, packed_in).wait_send()
    swap(7, g_cross, g_cross_in).wait_send()
    for c in given:
        c.wait_send()
    grad_copy.wait()
    for c in pix_copies:
        c.wait()


def mega(latents, pixels, counts, cotangent, gain_block, shards):
    rows, slots, width = latents.shape[1], pixels.shape[1], latents.shape[2]
    hidden = shards[6].shape[1]
    vm = pltpu.VMEM
    xt = lambda k: vm((2, 2, 4, UNIT_ROWS, k), BF16)
    wide = lambda n: vm((rows, n), BF16)
    scratch = [
        vm((2, 2, 2, 4, 2, UNIT_ROWS, UNIT_COLS), BF16),
        vm((2, 4, 2, 128, UNIT_COLS), BF16),
        vm((PARTIALS, 2, 2, 4, UNIT_ROWS, UNIT_COLS), BF16),
        vm((RING, 2, 4, UNIT_ROWS, UNIT_COLS), BF16),
        vm((RING, 4, UNIT_ROWS, UNIT_COLS), BF16),
        vm((RING, 4, 2, UNIT_ROWS, UNIT_COLS), BF16),
        xt(2 * rows), xt(2 * slots), xt(2 * rows), xt(2 * rows), xt(2 * rows), xt(2 * rows),
        vm((2, 2, 4, 128, 2 * rows), BF16),
        vm((2, 4, 2, 128, rows), BF16),
        vm((2, 2, 2, 4, 2, UNIT_ROWS, 256), BF16),
        wide(width), wide(width), wide(hidden), wide(hidden), wide(width), wide(width), wide(hidden), wide(3 * width),
        wide(width), wide(width),
        wide(width), wide(width), vm((slots, width), BF16), vm((slots, width), BF16), vm((slots, width), BF16), vm((slots, width), BF16),
        wide(width), vm((slots, width), BF16), vm((slots, width), BF16), wide(3 * width),
        vm((rows, width), F32), vm((rows, width), F32), vm((rows, width), F32), vm((slots, width), BF16), wide(width), vm((2, rows, width), F32),
        vm((2, 2, 4, 2, 8, 128), F32), vm((8, width), F32), vm((4, 8, width), F32), vm((8, width), F32), vm((5, 8, width), F32),
    ]
    sems = Gather.sems(16) + Scatter.sems(16)
    sems += [DMA((2,)), DMA((2,)), DMA((4,)), DMA((4,)), DMA((7,)), DMA((7,)), DMA((5,)), DMA((5,))]
    sems += [DMA((11,))] * 3 + [DMA((11,))] * 2
    outs = [
        jax.ShapeDtypeStruct(latents.shape, F32),
        jax.ShapeDtypeStruct(latents.shape, F32),
        jax.ShapeDtypeStruct(pixels.shape, F32),
        jax.ShapeDtypeStruct((8, width), F32),
    ]
    outs += [jax.ShapeDtypeStruct(s.shape, F32) for s in shards]
    outs += [jax.ShapeDtypeStruct((2, 2, 4, 2) + s.shape, s.dtype) for s in shards]
    hbm, vmem = pl.BlockSpec(memory_space=pl.ANY), pl.BlockSpec(memory_space=pltpu.VMEM)
    smem = pl.BlockSpec(memory_space=pltpu.SMEM)
    results = pl.pallas_call(
        mega_kernel,
        out_shape=outs,
        in_specs=[hbm, hbm, smem, hbm, hbm] + [hbm] * 8,
        out_specs=[hbm] * 3 + [vmem] + [vmem] * 8 + [hbm] * 8,
        scratch_shapes=scratch + sems,
        compiler_params=pltpu.CompilerParams(collective_id=0, has_side_effects=True, vmem_limit_bytes=63 * 2**20),
    )(latents, pixels, counts, cotangent, gain_block, *shards)
    return results[:4], results[4:12]


def layer_norm(inputs, gain):
    center = inputs - jnp.mean(inputs, axis=-1, keepdims=True)
    spread = jnp.mean(center * center, axis=-1, keepdims=True)
    return center * lax.rsqrt(spread + EPS) * gain


def project(inputs, matrix):
    return jnp.einsum("gld,de->gle", inputs, matrix, preferred_element_type=jnp.float32)


def project_back(grad_rows, matrix):
    return jnp.einsum("gle,de->gld", grad_rows, matrix, preferred_element_type=jnp.float32)


def weight_grad(inputs, grad_rows):
    return jnp.einsum("gld,gle->de", inputs, grad_rows, preferred_element_type=jnp.float32)


def split_heads(tensor):
    return tensor.reshape(tensor.shape[0], tensor.shape[1], HEADS, -1)


def merge_heads(tensor):
    return tensor.reshape(tensor.shape[0], tensor.shape[1], -1)


def scores_of(queries, key_rows, visible):
    scores = jnp.einsum("glhd,gshd->ghls", queries, key_rows, preferred_element_type=jnp.float32)
    scores = scores * queries.shape[-1] ** (-0.5)
    if visible is not None:
        scores = jnp.where(visible[:, None, None, :], scores, -1e30)
    return scores


def attend_forward(queries, key_rows, value_rows, visible):
    scores = scores_of(queries, key_rows, visible)
    largest = jnp.max(scores, axis=-1, keepdims=True)
    exp_scores = jnp.exp(scores - largest)
    totals = jnp.sum(exp_scores, axis=-1, keepdims=True)
    attn_probs = exp_scores / totals
    log_total = largest + jnp.log(totals)
    mixed = jnp.einsum(
        "ghls,gshd->glhd",
        attn_probs.astype(jnp.bfloat16),
        value_rows,
        preferred_element_type=jnp.float32,
    ).astype(jnp.bfloat16)
    return (mixed, log_total)


def attend_backward(queries, key_rows, value_rows, visible, log_total, mixed_grad):
    scale = queries.shape[-1] ** (-0.5)
    attn_probs = jnp.exp(scores_of(queries, key_rows, visible) - log_total)
    probs_grad = jnp.einsum(
        "glhd,gshd->ghls", mixed_grad, value_rows, preferred_element_type=jnp.float32
    )
    value_grad = jnp.einsum(
        "ghls,glhd->gshd",
        attn_probs.astype(jnp.bfloat16),
        mixed_grad,
        preferred_element_type=jnp.float32,
    ).astype(jnp.bfloat16)
    score_grad = attn_probs * (
        probs_grad - jnp.sum(probs_grad * attn_probs, axis=-1, keepdims=True)
    )
    score_grad = score_grad.astype(jnp.bfloat16)
    query_grad = (
        jnp.einsum("ghls,gshd->glhd", score_grad, key_rows, preferred_element_type=jnp.float32)
        * scale
    ).astype(jnp.bfloat16)
    key_grad = (
        jnp.einsum("ghls,glhd->gshd", score_grad, queries, preferred_element_type=jnp.float32)
        * scale
    ).astype(jnp.bfloat16)
    return (query_grad, key_grad, value_grad)


def local_plain(
    latents,
    pixels,
    slot_index,
    counts,
    cotangent,
    gain_q,
    gain_kv,
    w_query,
    w_key,
    w_value,
    w_out,
    gain_self,
    w_qkv,
    w_self_out,
    gain_mlp,
    w_up,
    w_down,
):
    groups = latents.shape[0]
    slots = pixels.shape[1]
    width = latents.shape[2]
    local_slot = slot_index % groups
    chosen = jnp.take(pixels, local_slot, axis=0).astype(jnp.float32)
    visible_count = jnp.take(counts, local_slot, axis=0)
    visible = lax.broadcasted_iota(jnp.int32, (groups, slots), 1) < visible_count[:, None]
    cross_all = (
        lax.all_gather(gain_q, ("dp", "fsdp"), axis=0, tiled=True),
        lax.all_gather(gain_kv, ("dp", "fsdp"), axis=0, tiled=True),
        lax.all_gather(w_query, ("dp", "fsdp"), axis=0, tiled=True),
        lax.all_gather(w_key, ("dp", "fsdp"), axis=0, tiled=True),
        lax.all_gather(w_value, ("dp", "fsdp"), axis=0, tiled=True),
        lax.all_gather(w_out, ("dp", "fsdp"), axis=0, tiled=True),
    )
    normed = layer_norm(latents, cross_all[0].astype(jnp.float32)).astype(jnp.bfloat16)
    pix_normed = layer_norm(chosen, cross_all[1].astype(jnp.float32)).astype(jnp.bfloat16)
    queries = split_heads(project(normed, cross_all[2]).astype(jnp.bfloat16))
    key_rows = split_heads(project(pix_normed, cross_all[3]).astype(jnp.bfloat16))
    value_rows = split_heads(project(pix_normed, cross_all[4]).astype(jnp.bfloat16))
    cross_mixed, cross_total = attend_forward(queries, key_rows, value_rows, visible)
    cross_flat = merge_heads(cross_mixed)
    after_cross = latents + project(cross_flat, cross_all[5])
    self_all = (
        lax.all_gather(gain_self, ("dp", "fsdp"), axis=0, tiled=True),
        lax.all_gather(w_qkv, ("dp", "fsdp"), axis=0, tiled=True),
        lax.all_gather(w_self_out, ("dp", "fsdp"), axis=0, tiled=True),
    )
    normed_self = layer_norm(after_cross, self_all[0].astype(jnp.float32)).astype(jnp.bfloat16)
    packed = project(normed_self, self_all[1]).astype(jnp.bfloat16)
    self_queries = split_heads(packed[..., :width])
    self_keys = split_heads(packed[..., width : 2 * width])
    self_values = split_heads(packed[..., 2 * width :])
    self_mixed, self_total = attend_forward(self_queries, self_keys, self_values, None)
    self_flat = merge_heads(self_mixed)
    after_self = after_cross + project(self_flat, self_all[2])
    mlp_all = (
        lax.all_gather(gain_mlp, ("dp", "fsdp"), axis=0, tiled=True),
        lax.all_gather(w_up, ("dp", "fsdp"), axis=0, tiled=True),
        lax.all_gather(w_down, ("dp", "fsdp"), axis=0, tiled=True),
    )
    normed_mlp = layer_norm(after_self, mlp_all[0].astype(jnp.float32)).astype(jnp.bfloat16)
    hidden = project(normed_mlp, mlp_all[1])
    activated = jax.nn.gelu(hidden).astype(jnp.bfloat16)
    latents_out = after_self + project(activated, mlp_all[2])
    root_mean = jnp.sqrt(jnp.mean(latents_out * latents_out, axis=(1, 2)))
    total_norm = lax.psum(jnp.sum(root_mean), ("dp", "fsdp"))
    norms = root_mean * (groups * lax.axis_size(("dp", "fsdp"))) / total_norm
    mlp_back = (
        lax.all_gather(gain_mlp, ("dp", "fsdp"), axis=0, tiled=True),
        lax.all_gather(w_up, ("dp", "fsdp"), axis=0, tiled=True),
        lax.all_gather(w_down, ("dp", "fsdp"), axis=0, tiled=True),
    )
    out_grad = cotangent.astype(jnp.bfloat16)
    down_grad = weight_grad(activated, out_grad)
    act_grad = project_back(out_grad, mlp_back[2])
    hidden_grad = jax.vjp(jax.nn.gelu, hidden)[1](act_grad)[0].astype(jnp.bfloat16)
    up_grad = weight_grad(normed_mlp, hidden_grad)
    mlp_in_grad = project_back(hidden_grad, mlp_back[1])
    after_self_ln, mlp_gain_grad = jax.vjp(layer_norm, after_self, mlp_back[0].astype(jnp.float32))[
        1
    ](mlp_in_grad)
    after_self_grad = cotangent + after_self_ln
    mlp_grads = (
        lax.psum_scatter(mlp_gain_grad, ("dp", "fsdp"), scatter_dimension=0, tiled=True),
        lax.psum_scatter(up_grad, ("dp", "fsdp"), scatter_dimension=0, tiled=True),
        lax.psum_scatter(down_grad, ("dp", "fsdp"), scatter_dimension=0, tiled=True),
    )
    self_back = (
        lax.all_gather(gain_self, ("dp", "fsdp"), axis=0, tiled=True),
        lax.all_gather(w_qkv, ("dp", "fsdp"), axis=0, tiled=True),
        lax.all_gather(w_self_out, ("dp", "fsdp"), axis=0, tiled=True),
    )
    self_branch = after_self_grad.astype(jnp.bfloat16)
    self_out_grad = weight_grad(self_flat, self_branch)
    self_mixed_grad = split_heads(project_back(self_branch, self_back[2]).astype(jnp.bfloat16))
    self_q_grad, self_k_grad, self_v_grad = attend_backward(
        self_queries, self_keys, self_values, None, self_total, self_mixed_grad
    )
    packed_grad = jnp.concatenate(
        [merge_heads(self_q_grad), merge_heads(self_k_grad), merge_heads(self_v_grad)], axis=-1
    )
    qkv_grad = weight_grad(normed_self, packed_grad)
    self_in_grad = project_back(packed_grad, self_back[1])
    after_cross_ln, self_gain_grad = jax.vjp(
        layer_norm, after_cross, self_back[0].astype(jnp.float32)
    )[1](self_in_grad)
    after_cross_grad = after_self_grad + after_cross_ln
    self_grads = (
        lax.psum_scatter(self_gain_grad, ("dp", "fsdp"), scatter_dimension=0, tiled=True),
        lax.psum_scatter(qkv_grad, ("dp", "fsdp"), scatter_dimension=0, tiled=True),
        lax.psum_scatter(self_out_grad, ("dp", "fsdp"), scatter_dimension=0, tiled=True),
    )
    cross_back = (
        lax.all_gather(gain_q, ("dp", "fsdp"), axis=0, tiled=True),
        lax.all_gather(gain_kv, ("dp", "fsdp"), axis=0, tiled=True),
        lax.all_gather(w_query, ("dp", "fsdp"), axis=0, tiled=True),
        lax.all_gather(w_key, ("dp", "fsdp"), axis=0, tiled=True),
        lax.all_gather(w_value, ("dp", "fsdp"), axis=0, tiled=True),
        lax.all_gather(w_out, ("dp", "fsdp"), axis=0, tiled=True),
    )
    cross_branch = after_cross_grad.astype(jnp.bfloat16)
    out_w_grad = weight_grad(cross_flat, cross_branch)
    cross_mixed_grad = split_heads(project_back(cross_branch, cross_back[5]).astype(jnp.bfloat16))
    query_grad, key_grad, value_grad = attend_backward(
        queries, key_rows, value_rows, visible, cross_total, cross_mixed_grad
    )
    query_flat = merge_heads(query_grad)
    key_flat = merge_heads(key_grad)
    value_flat = merge_heads(value_grad)
    query_w_grad = weight_grad(normed, query_flat)
    key_w_grad = weight_grad(pix_normed, key_flat)
    value_w_grad = weight_grad(pix_normed, value_flat)
    normed_grad = project_back(query_flat, cross_back[2])
    pix_normed_grad = project_back(key_flat, cross_back[3]) + project_back(
        value_flat, cross_back[4]
    )
    latents_ln, query_gain_grad = jax.vjp(layer_norm, latents, cross_back[0].astype(jnp.float32))[
        1
    ](normed_grad)
    latents_grad = after_cross_grad + latents_ln
    chosen_grad, pixel_gain_grad = jax.vjp(layer_norm, chosen, cross_back[1].astype(jnp.float32))[
        1
    ](pix_normed_grad)
    pixels_grad = jnp.zeros(pixels.shape, jnp.float32).at[local_slot].add(chosen_grad)
    cross_grads = (
        lax.psum_scatter(query_gain_grad, ("dp", "fsdp"), scatter_dimension=0, tiled=True),
        lax.psum_scatter(pixel_gain_grad, ("dp", "fsdp"), scatter_dimension=0, tiled=True),
        lax.psum_scatter(query_w_grad, ("dp", "fsdp"), scatter_dimension=0, tiled=True),
        lax.psum_scatter(key_w_grad, ("dp", "fsdp"), scatter_dimension=0, tiled=True),
        lax.psum_scatter(value_w_grad, ("dp", "fsdp"), scatter_dimension=0, tiled=True),
        lax.psum_scatter(out_w_grad, ("dp", "fsdp"), scatter_dimension=0, tiled=True),
    )
    return (
        latents_out,
        latents_grad,
        pixels_grad,
        cross_grads[0],
        cross_grads[1],
        cross_grads[2],
        cross_grads[3],
        cross_grads[4],
        cross_grads[5],
        self_grads[0],
        self_grads[1],
        self_grads[2],
        mlp_grads[0],
        mlp_grads[1],
        mlp_grads[2],
        norms,
    )


def local_fast(
    latents,
    pixels,
    slot_index,
    counts,
    cotangent,
    gain_q,
    gain_kv,
    w_query,
    w_key,
    w_value,
    w_out,
    gain_self,
    w_qkv,
    w_self_out,
    gain_mlp,
    w_up,
    w_down,
):
    gains = jnp.concatenate([gain_q, gain_kv, gain_self, gain_mlp]).astype(jnp.float32)
    gain_block = jnp.pad(gains[None, :], ((0, 7), (0, 0)))
    shards = (w_query, w_key, w_value, w_out, w_qkv, w_self_out, w_up, w_down)
    (latents_out, latents_grad, pixels_grad, small), grads = mega(latents, pixels, counts, cotangent, gain_block, shards)
    rows = gain_q.shape[0]
    devices = lax.axis_size(("dp", "fsdp"))
    mine = lax.dynamic_slice(small[:4], (0, lax.axis_index(("dp", "fsdp")) * rows), (4, rows))
    norms = small[5, :1] * devices / small[4, :1]
    g_query, g_key, g_value, g_out, g_qkv, g_self_out, g_up, g_down = grads
    return (
        latents_out,
        latents_grad,
        pixels_grad,
        mine[0],
        mine[1],
        g_query,
        g_key,
        g_value,
        g_out,
        mine[2],
        g_qkv,
        g_self_out,
        mine[3],
        g_up,
        g_down,
        norms,
    )


def fits(mesh):
    return mesh.shape["dp"] == 4 and mesh.shape["fsdp"] == 8


def solution(mesh):
    in_specs = (
        P(("dp", "fsdp"), None, None),
        P(("dp", "fsdp"), None, None),
        P(("dp", "fsdp")),
        P(("dp", "fsdp")),
        P(("dp", "fsdp"), None, None),
        P(("dp", "fsdp")),
        P(("dp", "fsdp")),
        P(("dp", "fsdp"), None),
        P(("dp", "fsdp"), None),
        P(("dp", "fsdp"), None),
        P(("dp", "fsdp"), None),
        P(("dp", "fsdp")),
        P(("dp", "fsdp"), None),
        P(("dp", "fsdp"), None),
        P(("dp", "fsdp")),
        P(("dp", "fsdp"), None),
        P(("dp", "fsdp"), None),
    )
    out_specs = (
        P(("dp", "fsdp"), None, None),
        P(("dp", "fsdp"), None, None),
        P(("dp", "fsdp"), None, None),
        P(("dp", "fsdp")),
        P(("dp", "fsdp")),
        P(("dp", "fsdp"), None),
        P(("dp", "fsdp"), None),
        P(("dp", "fsdp"), None),
        P(("dp", "fsdp"), None),
        P(("dp", "fsdp")),
        P(("dp", "fsdp"), None),
        P(("dp", "fsdp"), None),
        P(("dp", "fsdp")),
        P(("dp", "fsdp"), None),
        P(("dp", "fsdp"), None),
        P(("dp", "fsdp")),
    )
    return jax.shard_map(local_fast if fits(mesh) else local_plain, mesh=mesh, in_specs=in_specs, out_specs=out_specs, check_vma=False)
```

```python
import functools

import jax
import jax.numpy as jnp
from jax import lax
from jax.experimental import pallas as pl
from jax.experimental.pallas import tpu as pltpu
from jax.sharding import PartitionSpec as P

MESH = pl.DeviceIdType.MESH
DMA = pltpu.SemaphoreType.DMA
UNIT_COLS = 1024
UNIT_ROWS = 32
RING = 4
PARTIALS = 8
WIDTHS = ((256, 256, 256, 256), (128, 128, 384, 384), (128, 128, 384, 384), (128, 128, 384, 384))


class Place:
    def __init__(self):
        dp, f = lax.axis_index("dp"), lax.axis_index("fsdp")
        self.y, self.x, self.z, self.c = dp // 2, dp % 2, f // 2, f % 2
        step = jnp.where(self.z < 2, 1, -1)
        self.is_end = (self.z == 0) | (self.z == 3)
        self.z1 = jnp.where(self.is_end, self.z + step, self.z - step)
        self.z2 = jnp.where(self.is_end, self.z + 2 * step, self.z + step)
        self.z3 = jnp.where(self.is_end, self.z + 3 * step, self.z + 2 * step)

    def dev(self, y=None, x=None, z=None, c=None):
        y = self.y if y is None else y
        x = self.x if x is None else x
        z = self.z if z is None else z
        c = self.c if c is None else c
        return (y * 2 + x, z * 2 + c)

    def barrier(self):
        bar = pltpu.get_barrier_semaphore()
        peers = [
            self.dev(c=1 - self.c),
            self.dev(x=1 - self.x),
            self.dev(y=1 - self.y),
            self.dev(z=self.z1),
            self.dev(z=self.z2),
            self.dev(z=self.z3),
        ]
        for peer in peers:
            pl.semaphore_signal(bar, inc=1, device_id=peer, device_id_type=MESH)
        pl.semaphore_wait(bar, len(peers))


def remote(src, dst, send_sem, recv_sem, dev):
    return pltpu.make_async_remote_copy(
        src_ref=src, dst_ref=dst, send_sem=send_sem, recv_sem=recv_sem, device_id=dev, device_id_type=MESH
    )


def part_cols(u, p, base):
    widths = WIDTHS[u % RING]
    return pl.ds(base + sum(widths[:p]), widths[p])


class Gather:
    STAGES = 7

    def __init__(self, me, units, sems):
        self.me, self.units = me, units
        self.loc, self.sib_s, self.sib_r, self.zs, self.zr, self.xs, self.xr, self.ys, self.yr = sems

    @staticmethod
    def sems(n):
        return [DMA((n,))] * 3 + [DMA((n, 4, 4))] * 2 + [DMA((n, 4))] * 4

    def at(self, u, y, x, z, c, p=None):
        _, full, row, col = self.units[u]
        cols = pl.ds(col, UNIT_COLS) if p is None else part_cols(u, p, col)
        return full.at[y, x, z, c, pl.ds(row, UNIT_ROWS), cols]

    def own(self, u):
        me, (shard, _, row, col) = self.me, self.units[u]
        src = shard.at[pl.ds(row, UNIT_ROWS), pl.ds(col, UNIT_COLS)]
        return pltpu.make_async_copy(src, self.at(u, me.y, me.x, me.z, me.c), self.loc.at[u])

    def zblk(self, u, p, z):
        me, s = self.me, slice(None)
        return self.at(u, me.y if p != 3 else s, me.x if p != 2 else s, z, me.c, p)

    def zcopy(self, u, p, z_to, z_block=None):
        me = self.me
        if z_block is None:
            b = self.zblk(u, p, me.z)
            return remote(b, b, self.zs.at[u, p, z_to], self.zr.at[u, p, me.z], me.dev(z=z_to))
        b = self.zblk(u, p, z_block)
        return remote(b, b, self.zs.at[u, p, me.z], self.zr.at[u, p, z_block], me.dev(z=z_to))

    def zin(self, u, p, z_block):
        b = self.zblk(u, p, z_block)
        return remote(b, b, self.zs.at[u, p, z_block], self.zr.at[u, p, z_block], self.me.dev(z=z_block))

    def z_a(self, u, p):
        me = self.me
        self.zcopy(u, p, me.z1).start()
        self.zcopy(u, p, me.z2).start()

        @pl.when(~me.is_end)
        def _():
            self.zcopy(u, p, me.z3).start()

    def z_b(self, u, p):
        me = self.me

        @pl.when(~me.is_end)
        def _():
            self.zin(u, p, me.z3).wait_recv()
            self.zcopy(u, p, me.z1, me.z3).start()

    def z_wait(self, u, p):
        me = self.me
        self.zin(u, p, me.z1).wait_recv()
        self.zin(u, p, me.z2).wait_recv()

        @pl.when(me.is_end)
        def _():
            self.zin(u, p, me.z3).wait_recv()

    def z_sent(self, u, p):
        me = self.me
        self.zcopy(u, p, me.z1).wait_send()
        self.zcopy(u, p, me.z2).wait_send()

        @pl.when(~me.is_end)
        def _():
            self.zcopy(u, p, me.z3).wait_send()
            self.zcopy(u, p, me.z1, me.z3).wait_send()

    def xcopy(self, u, p, out=True):
        me, s = self.me, slice(None)
        b = self.at(u, me.y if p != 3 and p != 1 else s, me.x if out else 1 - me.x, me.z if p == 2 else s, me.c, p)
        return remote(b, b, self.xs.at[u, p], self.xr.at[u, p], me.dev(x=1 - me.x))

    def ycopy(self, u, p, out=True):
        me, s = self.me, slice(None)
        b = self.at(u, me.y if out else 1 - me.y, me.x if p != 2 and p != 0 else s, me.z if p == 3 else s, me.c, p)
        return remote(b, b, self.ys.at[u, p], self.yr.at[u, p], me.dev(y=1 - me.y))

    def final(self, u, out=True):
        me, s = self.me, slice(None)
        b = self.at(u, s, s, s, me.c if out else 1 - me.c)
        return remote(b, b, self.sib_s.at[u], self.sib_r.at[u], me.dev(c=1 - me.c))

    def stage(self, s, u):
        if s == 1:
            self.z_a(u, 0)
            self.z_a(u, 1)
        elif s == 2:
            self.z_b(u, 0)
            self.z_b(u, 1)
            self.xcopy(u, 2, False).wait_recv()
            self.z_a(u, 2)
            self.ycopy(u, 3, False).wait_recv()
            self.z_a(u, 3)
        elif s == 3:
            self.z_wait(u, 0)
            self.xcopy(u, 0).start()
            self.z_wait(u, 1)
            self.ycopy(u, 1).start()
            self.z_b(u, 2)
            self.z_b(u, 3)
        elif s == 4:
            self.z_wait(u, 2)
            self.ycopy(u, 2).start()
            self.z_wait(u, 3)
            self.xcopy(u, 3).start()
            self.xcopy(u, 0, False).wait_recv()
            self.ycopy(u, 0).start()
            self.ycopy(u, 1, False).wait_recv()
            self.xcopy(u, 1).start()
        elif s == 5:
            self.ycopy(u, 2, False).wait_recv()
            self.xcopy(u, 3, False).wait_recv()
            self.ycopy(u, 0, False).wait_recv()
            self.xcopy(u, 1, False).wait_recv()
            self.final(u).start()
        elif s == 6:
            self.final(u, False).wait_recv()

    def early(self, u):
        self.own(u).wait()
        self.xcopy(u, 2).start()
        self.ycopy(u, 3).start()

    def sent(self, u):
        for p in range(4):
            self.z_sent(u, p)
            self.xcopy(u, p).wait_send()
            self.ycopy(u, p).wait_send()
        self.final(u).wait_send()

    def tick(self, t, wide):
        for u in range(len(self.units)):
            s = t - max(0, u - wide + 1)
            if 0 <= s < self.STAGES:
                self.stage(s, u)

    def ticks(self, wide):
        return self.STAGES + max(0, len(self.units) - wide)


class Scatter:
    STAGES = 5

    def __init__(self, me, units, refs, sems):
        self.me, self.units = me, units
        self.part, self.r1, self.r2, self.rz = refs
        self.s1, self.q1, self.s2, self.q2, self.zs, self.zr = sems

    @staticmethod
    def sems(n):
        return [DMA((n, 4))] * 4 + [DMA((n, 4, 4))] * 2

    def pt(self, u, p, y, x, z):
        return self.part.at[u % PARTIALS, y, x, z, :, part_cols(u, p, 0)]

    def first(self, u, p):
        me, s = self.me, slice(None)
        dst = self.r1.at[u % PARTIALS, :, :, :, part_cols(u, p, 0)]
        if p in (0, 2):
            return remote(self.pt(u, p, 1 - me.y, s, s), dst, self.s1.at[u, p], self.q1.at[u, p], me.dev(y=1 - me.y))
        return remote(self.pt(u, p, s, 1 - me.x, s), dst, self.s1.at[u, p], self.q1.at[u, p], me.dev(x=1 - me.x))

    def add(self, count, dst, srcs):
        def body(i, carry):
            total = dst(i)[...].astype(jnp.float32)
            for src in srcs:
                total = total + src(i)[...].astype(jnp.float32)
            dst(i)[...] = total.astype(jnp.bfloat16)
            return carry

        if count == 1:
            body(0, 0)
        else:
            lax.fori_loop(0, count, body, 0)

    def first_in(self, u, p):
        me = self.me
        self.first(u, p).wait_recv()
        if p in (0, 2):
            dst = lambda i: self.pt(u, p, me.y, i // 4, i % 4)
        else:
            dst = lambda i: self.pt(u, p, i // 4, me.x, i % 4)
        self.add(8, dst, [lambda i: self.r1.at[u % PARTIALS, i // 4, i % 4, :, part_cols(u, p, 0)]])

    def second(self, u, p):
        me, s = self.me, slice(None)
        cols = part_cols(u, p, 0)
        z = s if p < 2 else me.z
        dst = self.r2.at[u % RING, :, :, cols] if p < 2 else self.r2.at[u % RING, 0, :, cols]
        if p in (0, 2):
            return remote(self.pt(u, p, me.y, 1 - me.x, z), dst, self.s2.at[u, p], self.q2.at[u, p], me.dev(x=1 - me.x))
        return remote(self.pt(u, p, 1 - me.y, me.x, z), dst, self.s2.at[u, p], self.q2.at[u, p], me.dev(y=1 - me.y))

    def second_in(self, u, p):
        me = self.me
        self.second(u, p).wait_recv()
        self.add(
            4,
            lambda i: self.pt(u, p, me.y, me.x, i),
            [lambda i: self.r2.at[u % RING, i, :, part_cols(u, p, 0)]],
        )

    def zblk(self, u, p, z):
        me, s = self.me, slice(None)
        return self.pt(u, p, me.y if p != 3 else s, me.x if p != 2 else s, z)

    def zslot(self, u, p, slot):
        cols = part_cols(u, p, 0)
        return self.rz.at[u % RING, slot, 0, :, cols] if p < 2 else self.rz.at[u % RING, slot, :, :, cols]

    def zcopy(self, u, p, which, block, slot, z_to):
        return remote(
            self.zblk(u, p, block), self.zslot(u, p, slot), self.zs.at[u, p, which], self.zr.at[u, p, slot], self.me.dev(z=z_to)
        )

    def z_ends(self, u, p):
        me = self.me
        return [
            self.zcopy(u, p, 2, me.z3, 3, me.z1),
            self.zcopy(u, p, 1, me.z2, 2, me.z2),
            self.zcopy(u, p, 0, me.z1, 0, me.z1),
        ]

    def z_mids(self, u, p):
        me = self.me
        return [self.zcopy(u, p, 0, me.z1, 0, me.z1), self.zcopy(u, p, 1, me.z2, 1, me.z2)]

    def z_gone(self, u, p):
        return self.zcopy(u, p, 2, self.me.z3, 1, self.me.z3)

    def z_a(self, u, p):
        me = self.me

        @pl.when(me.is_end)
        def _():
            for c in self.z_ends(u, p):
                c.start()

        @pl.when(~me.is_end)
        def _():
            for c in self.z_mids(u, p):
                c.start()

    def zget(self, u, p, slot):
        return self.zcopy(u, p, 0, self.me.z, slot, self.me.z1)

    def z_b(self, u, p):
        me = self.me

        @pl.when(~me.is_end)
        def _():
            self.zget(u, p, 3).wait_recv()
            self.z_add(u, p, me.z3, (3,))
            self.z_gone(u, p).start()

    def z_add(self, u, p, block, slots):
        cols = part_cols(u, p, 0)
        me = self.me
        if p < 2:
            dst, count = (lambda i: self.pt(u, p, me.y, me.x, block)), 1
        elif p == 2:
            dst, count = (lambda i: self.pt(u, p, me.y, i, block)), 2
        else:
            dst, count = (lambda i: self.pt(u, p, i, me.x, block)), 2
        self.add(count, dst, [functools.partial(lambda slot, i: self.rz.at[u % RING, slot, i, :, cols], k) for k in slots])

    def z_in(self, u, p):
        me = self.me
        self.zget(u, p, 0).wait_recv()
        self.zget(u, p, 1).wait_recv()

        @pl.when(~me.is_end)
        def _():
            self.zget(u, p, 2).wait_recv()

    def out(self, u, p):
        out, row, col = self.units[u]
        return out.at[pl.ds(row, UNIT_ROWS), part_cols(u, p, col)]

    def finish_z(self, u, p):
        me, cols = self.me, part_cols(u, p, 0)
        self.z_in(u, p)
        f32 = lambda ref: ref[...].astype(jnp.float32)
        total = f32(self.pt(u, p, me.y, me.x, me.z)) + f32(self.rz.at[u % RING, 0, 0, :, cols]) + f32(self.rz.at[u % RING, 1, 0, :, cols])

        @pl.when(me.is_end)
        def _():
            self.out(u, p)[...] = total

        @pl.when(~me.is_end)
        def _():
            self.out(u, p)[...] = total + f32(self.rz.at[u % RING, 2, 0, :, cols])

    def pass_z(self, u, p):
        me = self.me
        self.z_in(u, p)

        @pl.when(me.is_end)
        def _():
            self.z_add(u, p, me.z, (0, 1))

        @pl.when(~me.is_end)
        def _():
            self.z_add(u, p, me.z, (0, 1, 2))

        self.second(u, p).start()

    def finish_last(self, u, p):
        me, cols = self.me, part_cols(u, p, 0)
        self.second(u, p).wait_recv()
        total = self.pt(u, p, me.y, me.x, me.z)[...].astype(jnp.float32) + self.r2.at[u % RING, 0, :, cols][...].astype(jnp.float32)
        self.out(u, p)[...] = total

    def stage(self, s, u):
        if s == 0:
            for p in (2, 3, 0, 1):
                self.first(u, p).start()
        elif s == 1:
            for p in (2, 3):
                self.first_in(u, p)
                self.z_a(u, p)
            for p in (0, 1):
                self.first_in(u, p)
                self.second(u, p).start()
        elif s == 2:
            for p in (2, 3):
                self.z_b(u, p)
            for p in (0, 1):
                self.second_in(u, p)
                self.z_a(u, p)
        elif s == 3:
            for p in (2, 3):
                self.pass_z(u, p)
            for p in (0, 1):
                self.z_b(u, p)
        elif s == 4:
            for p in (0, 1):
                self.finish_z(u, p)
            for p in (2, 3):
                self.finish_last(u, p)

    def sent(self, u):
        me = self.me
        for p in range(4):
            self.first(u, p).wait_send()
            self.second(u, p).wait_send()

            @pl.when(me.is_end)
            def _():
                for c in self.z_ends(u, p):
                    c.wait_send()

            @pl.when(~me.is_end)
            def _():
                for c in self.z_mids(u, p) + [self.z_gone(u, p)]:
                    c.wait_send()


EPS = 1e-05
HEADS = 8
GELU_A = 0.7978845608028654
GELU_B = 0.044715
NT = (((1,), (1,)), ((), ()))
F32, BF16 = jnp.float32, jnp.bfloat16


def matmul(a, b):
    return jnp.dot(a, b, preferred_element_type=F32)


def matmul_nt(a, b):
    return lax.dot_general(a, b, NT, preferred_element_type=F32)


def block(i, size):
    return pl.ds(pl.multiple_of(i * size, size), size)


def for_each(count, body):
    def step(i, carry):
        body(i)
        return carry

    lax.fori_loop(0, count, step, 0)


def normalise(v):
    center = v - jnp.mean(v, axis=-1, keepdims=True)
    inv = lax.rsqrt(jnp.mean(center * center, axis=-1, keepdims=True) + EPS)
    return center * inv, inv


def ln_forward(src, gain, dst):
    def body(i):
        rows = block(i, 32)
        n, _ = normalise(src[rows, :].astype(F32))
        dst[rows, :] = (n * gain[...]).astype(BF16)

    for_each(src.shape[0] // 32, body)


def ln_backward(src, row0, gain, incoming, base, gain_grad):
    def body(i):
        rows = block(i, 32)
        n, inv = normalise(src[pl.ds(pl.multiple_of(row0 + i * 32, 32), 32), :].astype(F32))
        g = incoming[rows, :]
        e = g * gain[...]
        grad = inv * (e - jnp.mean(e, axis=-1, keepdims=True) - n * jnp.mean(e * n, axis=-1, keepdims=True))
        prod = g * n
        gain_grad[...] += prod[0:8] + prod[8:16] + prod[16:24] + prod[24:32]
        if base is None:
            incoming[rows, :] = grad
        else:
            base[rows, :] = base[rows, :] + grad

    for_each(incoming.shape[0] // 32, body)


def attend_forward_heads(first, heads, q, q0, k, k0, v, v0, out, count):
    def body(i):
        h = first + i

        def head(ref, at):
            return ref[:, pl.ds(pl.multiple_of(at + h * 128, 128), 128)]

        s = matmul_nt(head(q, q0), head(k, k0)) * 128 ** (-0.5)
        if count is not None:
            s = jnp.where(lax.broadcasted_iota(jnp.int32, s.shape, 1) < count, s, -1e30)
        e = jnp.exp(s - jnp.max(s, axis=-1, keepdims=True))
        p = (e * (1.0 / jnp.sum(e, axis=-1, keepdims=True))).astype(BF16)
        out[:, block(h, 128)] = matmul(p, head(v, v0)).astype(BF16)

    for_each(heads, body)


def attend_backward_heads(first, heads, q, q0, k, k0, v, v0, mixed_grad, count, dq, dq0, dk, dk0, dv, dv0):
    scale = 128 ** (-0.5)

    def body(i):
        h = first + i

        def head(ref, at):
            return ref[:, pl.ds(pl.multiple_of(at + h * 128, 128), 128)]

        qh, kh, vh, gh = head(q, q0), head(k, k0), head(v, v0), head(mixed_grad, 0)
        s = matmul_nt(kh, qh) * scale
        if count is not None:
            s = jnp.where(lax.broadcasted_iota(jnp.int32, s.shape, 0) < count, s, -1e30)
        e = jnp.exp(s - jnp.max(s, axis=0, keepdims=True))
        p = e * (1.0 / jnp.sum(e, axis=0, keepdims=True))
        dv[:, pl.ds(pl.multiple_of(dv0 + h * 128, 128), 128)] = matmul(p.astype(BF16), gh).astype(BF16)
        dp = matmul_nt(vh, gh)
        ds = (p * (dp - jnp.sum(dp * p, axis=0, keepdims=True))).astype(BF16)
        dk[:, pl.ds(pl.multiple_of(dk0 + h * 128, 128), 128)] = (matmul(ds, qh) * scale).astype(BF16)
        dq[:, pl.ds(pl.multiple_of(dq0 + h * 128, 128), 128)] = (matmul(kh.T, ds).T * scale).astype(BF16)

    for_each(heads, body)


class SmallGather:
    def __init__(self, me, full, send, recv):
        self.me, self.full, self.send, self.recv = me, full, send, recv

    def copy(self, src, k, r, dev):
        return remote(src, src, self.send.at[k], self.recv.at[r], dev)

    def sib(self, out=True):
        me = self.me
        return self.copy(self.full.at[me.y, me.x, me.z, me.c if out else 1 - me.c], 0, 0, me.dev(c=1 - me.c))

    def zc(self, blk, k, r, to):
        me = self.me
        return self.copy(self.full.at[me.y, me.x, blk], k, r, me.dev(z=to))

    def xc(self, out=True):
        me = self.me
        return self.copy(self.full.at[me.y, me.x if out else 1 - me.x], 5, 5, me.dev(x=1 - me.x))

    def yc(self, out=True):
        me = self.me
        return self.copy(self.full.at[me.y if out else 1 - me.y], 6, 6, me.dev(y=1 - me.y))

    def run(self, s):
        me = self.me
        if s == 0:
            self.sib().start()
        elif s == 1:
            self.sib(False).wait_recv()
            self.zc(me.z, 1, 1 + me.z, me.z1).start()
            self.zc(me.z, 2, 1 + me.z, me.z2).start()

            @pl.when(~me.is_end)
            def _():
                self.zc(me.z, 3, 1 + me.z, me.z3).start()

        elif s == 2:

            @pl.when(~me.is_end)
            def _():
                self.zc(me.z3, 4, 1 + me.z3, me.z1).wait_recv()
                self.zc(me.z3, 4, 1 + me.z3, me.z1).start()

            for z in (me.z1, me.z2):
                self.zc(z, 1, 1 + z, me.z1).wait_recv()

            @pl.when(me.is_end)
            def _():
                self.zc(me.z3, 1, 1 + me.z3, me.z1).wait_recv()

            self.xc().start()
        elif s == 3:
            self.xc(False).wait_recv()
            self.yc().start()
        elif s == 4:
            self.yc(False).wait_recv()
            self.sib().wait_send()
            self.zc(me.z, 1, 1 + me.z, me.z1).wait_send()
            self.zc(me.z, 2, 1 + me.z, me.z2).wait_send()

            @pl.when(~me.is_end)
            def _():
                self.zc(me.z, 3, 1 + me.z, me.z3).wait_send()
                self.zc(me.z3, 4, 1 + me.z3, me.z1).wait_send()

            self.xc().wait_send()
            self.yc().wait_send()


class SmallSum:
    def __init__(self, me, acc, got, send, recv):
        z_near = jnp.where(me.is_end, me.z1, me.z1)
        z_far = jnp.where(me.is_end, me.z2, me.z3)
        self.devs = [me.dev(c=1 - me.c), me.dev(x=1 - me.x), me.dev(y=1 - me.y), me.dev(z=z_near), me.dev(z=z_far)]
        self.acc, self.got, self.send, self.recv = acc, got, send, recv

    def copy(self, k):
        return remote(self.acc, self.got.at[k], self.send.at[k], self.recv.at[k], self.devs[k])

    def start(self, k):
        self.copy(k).start()

    def finish(self, k):
        c = self.copy(k)
        c.wait_send()
        c.wait_recv()
        self.acc[...] += self.got[k]


def mega_kernel(*refs):
    it = iter(refs)
    take = lambda n: [next(it) for _ in range(n)]
    latents, pixels, counts, cotangent, gain_block = take(5)
    shards = take(8)
    latents_out, latents_grad, pixels_grad, small_out = take(4)
    grads_out = take(8)
    fulls = take(8)
    (
        w_buf, wd_buf, part, r1, r2, rz,
        xt_normed, xt_pix, xt_mixed, xt_nself, xt_smixed, xt_nmlp, xt_act, st_a, st_b,
        g_out, g_out_in, hid, hid_in, g_branch, g_branch_in, act, packed_in, g_cross, g_cross_in,
        dq, dq_in, big, dk_in, dv, dv_in,
        queries, keys, values, packed, after_cross, after_self, resid, pix, tmp, acc,
        gain_full, gain_vec, gain_acc, small, small_got,
    ) = take(46)
    gather_sems, scatter_sems = take(9), take(6)
    w_sem, wd_sem, in_sem, out_sem, sg_s, sg_r, ss_s, ss_r, xl, xs, xr, gs, gr = take(13)
    me = Place()
    me.barrier()

    cross_units = [(shards[i], fulls[i], 0, 0) for i in (1, 2, 0, 3)]
    self_units = [(shards[4], fulls[4], 0, k * UNIT_COLS) for k in range(3)] + [(shards[5], fulls[5], 0, 0)]
    mlp_units = [(shards[6], fulls[6], 0, k * UNIT_COLS) for k in range(4)]
    mlp_units += [(shards[7], fulls[7], k * UNIT_ROWS, 0) for k in range(4)]
    gather = Gather(me, cross_units + self_units + mlp_units, gather_sems)
    scatter_units = [(grads_out[7], k * UNIT_ROWS, 0) for k in range(4)]
    scatter_units += [(grads_out[6], 0, k * UNIT_COLS) for k in range(4)]
    scatter_units += [(grads_out[5], 0, 0)] + [(grads_out[4], 0, k * UNIT_COLS) for k in range(3)]
    scatter_units += [(grads_out[i], 0, 0) for i in (3, 2, 1, 0)]
    scatter = Scatter(me, scatter_units, (part, r1, r2, rz), scatter_sems)
    pushed = [0]
    tick = [0]

    clock = [0.0]
    settled = [-1]
    ready = []

    def tick_ready(t):
        return 13 + 3.7 * min(t, 6) + 7.35 * max(0, t - 6)

    def settle_ready(k):
        return ready[k] if k < len(ready) else ready[-1] + 4.0 * (k - len(ready) + 1)

    def next_tick():
        clock[0] = max(clock[0], tick_ready(tick[0])) + 0.5
        gather.tick(tick[0], 1)
        tick[0] += 1

    def next_settle():
        settled[0] += 1
        last = settled[0]
        clock[0] = max(clock[0], settle_ready(last)) + 1.0
        for s in range(Scatter.STAGES - 1, 0, -1):
            if 0 <= last - s < len(scatter_units):
                scatter.stage(s, last - s)

    def spend(us):
        clock[0] += us
        while True:
            k = settled[0] + 1
            if tick[0] < gather.ticks(1) and tick_ready(tick[0]) <= clock[0]:
                next_tick()
            elif pushed[0] and k <= pushed[0] and k < len(scatter_units) + 4 and settle_ready(k) <= clock[0]:
                next_settle()
            else:
                break

    def arrived(u):
        while tick[0] < gather.ticks(1) and tick[0] <= u + Gather.STAGES - 1:
            next_tick()

    def gather_to(t):
        while tick[0] <= t:
            next_tick()

    def settle_to(last):
        while settled[0] < last:
            next_settle()

    def load(k, src, dst):
        return pltpu.make_async_copy(src, dst, in_sem.at[k])

    for u in range(len(gather.units)):
        gather.own(u).start()
    loads = [load(0, latents.at[0], after_self), load(1, pixels.at[0], pix), load(2, cotangent.at[0], resid)]
    for c in loads:
        c.start()
    own_gain = pltpu.make_async_copy(gain_block, gain_full.at[me.y, me.x, me.z, me.c], in_sem.at[3])
    own_gain.start()
    own_gain.wait()
    gains = SmallGather(me, gain_full, sg_s, sg_r)
    gains.run(0)
    gather.early(0)
    gather_to(1)
    for u in range(1, len(gather.units)):
        gather.early(u)
    gains.run(1)
    gather_to(2)
    gains.run(2)
    gather_to(3)
    gains.run(3)
    gains.run(4)
    table = jnp.sum(gain_full[...].reshape(32, 8, 128), axis=1).astype(BF16)
    width = latents.shape[2]
    lane = lax.broadcasted_iota(jnp.int32, (128, width), 1)
    place = lax.broadcasted_iota(jnp.int32, (128, width), 0)
    owner = lax.broadcasted_iota(jnp.int32, (32, width), 0) == (lax.broadcasted_iota(jnp.int32, (32, width), 1) >> 5)
    for g in range(4):
        pick = jnp.where(place == (lane & 31) + 32 * g, 1.0, 0.0).astype(BF16)
        spread = jnp.where(owner, matmul(table, pick), 0.0)
        gain_vec[g : g + 1, :] = jnp.sum(spread, axis=0, keepdims=True)
    gain = [gain_vec.at[g : g + 1, :] for g in range(4)]
    for g in range(4):
        gain_acc[g] = jnp.zeros_like(gain_acc[g])

    staged = [None, None]

    def hand_over(k, stage, mine, slot, own_dst, far_dst):
        a = pltpu.make_async_copy(mine, own_dst, xl.at[k])
        b = remote(stage, far_dst, xs.at[k], xr.at[k], me.dev(c=1 - me.c))
        a.start()
        b.start()
        staged[slot] = (a, b)

    def clear(slot):
        if staged[slot] is not None:
            a, b = staged[slot]
            a.wait()
            b.wait_send()
            staged[slot] = None

    turn = [0]

    def transpose_out(k, x, row0, xt, k_rows):
        slot = turn[0] % 2
        turn[0] += 1
        clear(slot)

        def body(j):
            piece = x[pl.ds(row0, 256), block(j, 256)].T
            st_b[slot, j // 2, j % 2] = piece.reshape(4, 2, 32, 256)

        for_each(4, body)
        hand_over(
            k,
            st_b.at[slot, :, :, :, 1 - me.c],
            st_b.at[slot, :, :, :, me.c],
            slot,
            xt.at[:, :, :, :, pl.ds(row0, 256)],
            xt.at[:, :, :, :, pl.ds(k_rows + row0, 256)],
        )

    def xt_wait(k, xt, row0, k_rows):
        remote(
            st_b.at[0, :, :, :, 0],
            xt.at[:, :, :, :, pl.ds(k_rows + row0, 256)],
            xs.at[k],
            xr.at[k],
            me.dev(c=1 - me.c),
        ).wait_recv()

    def swap(k, src, dst):
        return remote(src, dst, gs.at[k], gr.at[k], me.dev(c=1 - me.c))

    w_turn = [0]

    def w_start(full, col):
        slot = w_turn[0] % 2
        w_turn[0] += 1
        c = pltpu.make_async_copy(full.at[:, :, :, :, :, pl.ds(col, UNIT_COLS)], w_buf.at[slot], w_sem.at[slot])
        c.start()
        return slot, c

    def w_fetch(full, col):
        slot, c = w_start(full, col)
        c.wait()
        return slot

    def w_cols(slot, j):
        return w_buf[slot, :, :, :, :, :, block(j, 256)].reshape(width, 256)

    def w_rows(slot, j):
        return w_buf[slot, j // 2, j % 2].reshape(256, UNIT_COLS)

    def project(x, slot, out):
        for_each(4, lambda j: out(j, matmul(x[...], w_cols(slot, j))))

    def store(dst, col0=0):
        def put(j, tile):
            dst[:, pl.ds(pl.multiple_of(col0 + j * 256, 256), 256)] = tile.astype(dst.dtype)

        return put

    def back(g, col0, slot, dst, first):
        def body(j):
            tile = matmul_nt(g[:, pl.ds(col0, UNIT_COLS)], w_rows(slot, j))
            cols = block(j, 256)
            if first:
                dst[:, cols] = tile.astype(dst.dtype)
            else:
                dst[:, cols] = dst[:, cols] + tile

        for_each(4, body)

    def weight_grad(xt_at, rows, own, far, col0):
        u = pushed[0]
        settle_to(u - 3)
        if u >= PARTIALS:
            scatter.sent(u - PARTIALS)
        slot = u % PARTIALS

        def body(j):
            cols = pl.ds(pl.multiple_of(col0 + j * 256, 256), 256)
            total = matmul(xt_at(0), own[:, cols]) + matmul(xt_at(rows), far[:, cols])
            part[slot, :, :, :, :, block(j, 256)] = total.astype(BF16).reshape(2, 2, 4, UNIT_ROWS, 256)

        for_each(4, body)
        scatter.stage(0, u)
        pushed[0] += 1
        clock[0] += 1.7 if rows > 256 else 1.2
        gap = 7.35 if tick[0] >= gather.ticks(1) else 14.7
        ready.append(max(clock[0] + 9, (ready[-1] if ready else 0) + gap))
        spend(0)

    def xt_of(xt, rows):
        return lambda at: xt[:, :, :, :, pl.ds(at, rows)].reshape(512, rows)

    loads[0].wait()
    loads[1].wait()
    ln_forward(after_self, gain[0], tmp)
    transpose_out(0, tmp, 0, xt_normed, 256)
    spend(2)
    ln_forward(pix, gain[1], big)
    transpose_out(1, big, 0, xt_pix, 512)
    spend(3.3)
    transpose_out(2, big, 256, xt_pix, 512)
    count = counts[0]
    loads[2].wait()
    for_each(8, lambda i: g_out.__setitem__((block(i, 32), slice(None)), resid[block(i, 32), :].astype(BF16)))
    swap(0, g_out, g_out_in).start()
    arrived(0)
    project(big, w_fetch(fulls[1], 0), store(keys))
    spend(3.3)
    arrived(1)
    project(big, w_fetch(fulls[2], 0), store(values))
    spend(3.3)
    arrived(2)
    project(tmp, w_fetch(fulls[0], 0), store(queries))
    spend(2.7)
    for half in range(2):
        attend_forward_heads(4 * half, 4, queries, 0, keys, 0, values, 0, tmp, count)
        spend(2.3)
    arrived(3)
    transpose_out(3, tmp, 0, xt_mixed, 256)

    def add_to(dst, src):
        def put(j, tile):
            dst[:, block(j, 256)] = src[:, block(j, 256)] + tile

        return put

    project(tmp, w_fetch(fulls[3], 0), add_to(after_cross, after_self))
    spend(3)

    ln_forward(after_cross, gain[2], tmp)
    transpose_out(4, tmp, 0, xt_nself, 256)
    spend(1.8)
    for k in range(3):
        arrived(4 + k)
        project(tmp, w_fetch(fulls[4], k * UNIT_COLS), store(packed, k * UNIT_COLS))
        spend(2.7)
    for half in range(2):
        attend_forward_heads(4 * half, 4, packed, 0, packed, UNIT_COLS, packed, 2 * UNIT_COLS, tmp, None)
        spend(2.2)
    arrived(7)
    transpose_out(5, tmp, 0, xt_smixed, 256)
    project(tmp, w_fetch(fulls[5], 0), add_to(after_self, after_cross))
    spend(3)

    ln_forward(after_self, gain[3], tmp)
    transpose_out(6, tmp, 0, xt_nmlp, 256)
    spend(1.8)
    a_staged = [None, None]

    def act_out(k):
        slot = k % 2
        if a_staged[slot] is not None:
            a_staged[slot][0].wait()
            a_staged[slot][1].wait_send()

        def body(m):
            st_a[slot, m // 2, m % 2] = act[:, pl.ds(pl.multiple_of(k * UNIT_COLS + m * 128, 128), 128)].T

        for_each(8, body)
        a = pltpu.make_async_copy(st_a.at[slot, :, me.c], xt_act.at[k // 2, k % 2, :, :, pl.ds(0, 256)], xl.at[7 + k])
        b = remote(
            st_a.at[slot, :, 1 - me.c],
            xt_act.at[k // 2, k % 2, :, :, pl.ds(256, 256)],
            xs.at[7 + k],
            xr.at[7 + k],
            me.dev(c=1 - me.c),
        )
        a.start()
        b.start()
        a_staged[slot] = (a, b)
        return a, b

    act_copies = []
    for k in range(4):
        arrived(8 + k)
        slot = w_fetch(fulls[6], k * UNIT_COLS)

        def up(j):
            x = matmul(tmp[...], w_cols(slot, j))
            t = jnp.tanh(GELU_A * (x + GELU_B * (x * x * x)))
            half = 0.5 * (1.0 + t)
            cols = pl.ds(pl.multiple_of(k * UNIT_COLS + j * 256, 256), 256)
            act[:, cols] = (x * half).astype(BF16)
            slope = half + (0.5 * GELU_A) * x * (1.0 - t * t) * (1.0 + (3 * GELU_B) * (x * x))
            hid[:, cols] = slope.astype(BF16)

        for_each(4, up)
        act_copies.append(act_out(k))
        spend(3.2)
    for k in range(2, 4):
        a_staged[k % 2][0].wait()
        a_staged[k % 2][1].wait_send()
    for k in range(4):
        act_copies[k][1].wait_recv()
    for slot in range(2):
        clear(slot)
    spend(2)

    swap(0, g_out, g_out_in).wait_recv()

    def down_grad(k):
        def xt_down(at):
            return xt_act[:, :, :, pl.ds(k * UNIT_ROWS, UNIT_ROWS), pl.ds(at, 256)].reshape(512, 256)

        weight_grad(xt_down, 256, g_out, g_out_in, 0)

    down_grad(0)
    arrived(13)
    down_grad(1)
    arrived(15)

    wd_turn = [0]

    def wd_start(q):
        slot = wd_turn[0] % 2
        wd_turn[0] += 1
        c = pltpu.make_async_copy(fulls[7].at[q // 2, q % 2], wd_buf.at[slot], wd_sem.at[slot])
        c.start()
        return slot, c

    pending = w_start(fulls[6], 0)
    wd = [wd_start(0), wd_start(1), None, None]
    for q in range(4):
        slot, c = wd[q]
        c.wait()

        def hidden_back(j):
            w = wd_buf[slot, j].reshape(256, width)
            tile = matmul_nt(g_out[...], w)
            cols = pl.ds(pl.multiple_of(q * UNIT_COLS + j * 256, 256), 256)
            hid[:, cols] = (hid[:, cols].astype(F32) * tile).astype(BF16)

        for_each(4, hidden_back)
        cols = pl.ds(q * UNIT_COLS, UNIT_COLS)
        swap(1 + q, hid.at[:, cols], hid_in.at[:, cols]).start()
        spend(1.5)
        if q < 2:
            wd[q + 2] = wd_start(q + 2)
            down_grad(2 + q)
    xt_wait(6, xt_nmlp, 0, 256)
    wd = [wd_start(0), wd_start(1), None, None]
    for k in range(4):
        slot, c = pending
        c.wait()
        if k < 3:
            pending = w_start(fulls[6], (k + 1) * UNIT_COLS)
        back(hid, k * UNIT_COLS, slot, acc.at[1], k == 0)
        spend(1.4)
        cols = pl.ds(k * UNIT_COLS, UNIT_COLS)
        swap(1 + k, hid.at[:, cols], hid_in.at[:, cols]).wait_recv()
        weight_grad(xt_of(xt_nmlp, 256), 256, hid, hid_in, k * UNIT_COLS)
    so_slot, c_so = w_start(fulls[5], 0)
    ln_backward(after_self, 0, gain[3], acc.at[1], resid, gain_acc.at[3])
    spend(2.3)

    def round_rows(dst):
        for_each(8, lambda i: dst.__setitem__((block(i, 32), slice(None)), resid[block(i, 32), :].astype(BF16)))

    round_rows(g_branch)
    swap(5, g_branch, g_branch_in).start()
    c_so.wait()
    qkv_w = w_start(fulls[4], 0)
    back(g_branch, 0, so_slot, tmp, True)
    spend(1.8)
    swap(5, g_branch, g_branch_in).wait_recv()
    xt_wait(5, xt_smixed, 0, 256)
    weight_grad(xt_of(xt_smixed, 256), 256, g_branch, g_branch_in, 0)
    for q in range(4):
        cols = pl.ds(q * UNIT_COLS, UNIT_COLS)
        swap(1 + q, hid.at[:, cols], hid_in.at[:, cols]).wait_send()
    for half in range(2):
        attend_backward_heads(
            4 * half, 4, packed, 0, packed, UNIT_COLS, packed, 2 * UNIT_COLS, tmp, None,
            hid, 0, hid, UNIT_COLS, hid, 2 * UNIT_COLS,
        )
        spend(3.4)
    packed_grad = hid.at[:, pl.ds(0, 3 * UNIT_COLS)]
    swap(6, packed_grad, packed_in).start()
    for k in range(3):
        slot, c = qkv_w
        c.wait()
        if k < 2:
            qkv_w = w_start(fulls[4], (k + 1) * UNIT_COLS)
        back(hid, k * UNIT_COLS, slot, acc.at[0], k == 0)
        spend(1.3)
        if k == 0:
            swap(6, packed_grad, packed_in).wait_recv()
            xt_wait(4, xt_nself, 0, 256)
        weight_grad(xt_of(xt_nself, 256), 256, hid, packed_in, k * UNIT_COLS)
    wo_slot, c_wo = w_start(fulls[3], 0)
    ln_backward(after_cross, 0, gain[2], acc.at[0], resid, gain_acc.at[2])
    spend(2.3)

    round_rows(g_cross)
    swap(7, g_cross, g_cross_in).start()
    c_wo.wait()
    back(g_cross, 0, wo_slot, tmp, True)
    spend(1.8)
    swap(7, g_cross, g_cross_in).wait_recv()
    xt_wait(3, xt_mixed, 0, 256)
    weight_grad(xt_of(xt_mixed, 256), 256, g_cross, g_cross_in, 0)

    for q in range(4):
        slot, c = wd[q]
        c.wait()

        def down(j):
            w = wd_buf[slot, :, :, :, block(j, 256)].reshape(UNIT_COLS, 256)
            tile = matmul(act[:, pl.ds(q * UNIT_COLS, UNIT_COLS)], w)
            dst = block(j, 256)
            acc[0, :, dst] = (after_self[:, dst] if q == 0 else acc[0, :, dst]) + tile

        for_each(4, down)
        if q < 2:
            wd[q + 2] = wd_start(q + 2)
        spend(1.3)
    again = load(0, latents.at[0], after_self)
    again.start()
    out_copy = pltpu.make_async_copy(acc.at[0], latents_out.at[0], out_sem.at[0])
    out_copy.start()
    small[...] = jnp.zeros_like(small)

    def square(i, total):
        v = acc[0, block(i, 8), :]
        return total + v * v

    squares = lax.fori_loop(0, 32, square, jnp.zeros((8, width), F32))
    mean_square = jnp.sum(jnp.sum(squares, axis=1, keepdims=True), axis=0, keepdims=True) / (latents.shape[1] * width)
    root_mean = jnp.sqrt(mean_square)
    small[4:5, :] = jnp.broadcast_to(root_mean, (1, width))
    spend(1)

    for half in range(2):
        attend_backward_heads(4 * half, 4, queries, 0, keys, 0, values, 0, tmp, count, dq, 0, big, 0, dv, 0)
        spend(3.2)
    given = [swap(8, dv, dv_in), swap(9, big, dk_in), swap(10, dq, dq_in)]
    for c in given:
        c.start()
    w_v = w_start(fulls[2], 0)
    w_k = w_start(fulls[1], 0)
    xt_wait(1, xt_pix, 0, 512)
    xt_wait(2, xt_pix, 256, 512)
    given[0].wait_recv()
    weight_grad(xt_of(xt_pix, 512), 512, dv, dv_in, 0)
    given[1].wait_recv()
    weight_grad(xt_of(xt_pix, 512), 512, big, dk_in, 0)
    xt_wait(0, xt_normed, 0, 256)
    given[2].wait_recv()
    weight_grad(xt_of(xt_normed, 256), 256, dq, dq_in, 0)
    out_copy.wait()
    w_v[1].wait()
    for r in range(2):
        back(dv.at[pl.ds(256 * r, 256)], 0, w_v[0], acc.at[r], True)
        spend(1.3)
    w_q = w_start(fulls[0], 0)
    w_k[1].wait()
    pix_copies = []
    for r in range(2):
        back(big.at[pl.ds(256 * r, 256)], 0, w_k[0], acc.at[r], False)
        spend(1.3)
        ln_backward(pix, 256 * r, gain[1], acc.at[r], None, gain_acc.at[1])
        c = pltpu.make_async_copy(acc.at[r], pixels_grad.at[0, pl.ds(256 * r, 256)], out_sem.at[2 + r])
        c.start()
        pix_copies.append(c)
        spend(2.3)
    w_q[1].wait()
    back(dq, 0, w_q[0], after_cross, True)
    spend(1.3)
    again.wait()
    ln_backward(after_self, 0, gain[0], after_cross, resid, gain_acc.at[0])
    grad_copy = pltpu.make_async_copy(resid, latents_grad.at[0], out_sem.at[1])
    grad_copy.start()
    spend(2.3)
    for g in range(4):
        small[g : g + 1, :] = jnp.sum(gain_acc[g], axis=0, keepdims=True)
    total = SmallSum(me, small, small_got, ss_s, ss_r)
    for k in range(5):
        total.start(k)
        if settled[0] < len(scatter_units) + 3:
            next_settle()
        total.finish(k)
    settle_to(len(scatter_units) + 3)
    small[5:6, :] = jnp.broadcast_to(root_mean, (1, width))
    small_out[...] = small[...]

    for u in range(len(gather.units)):
        gather.sent(u)
    for u in range(len(scatter_units) - PARTIALS, len(scatter_units)):
        scatter.sent(u)
    swap(0, g_out, g_out_in).wait_send()
    swap(5, g_branch, g_branch_in).wait_send()
    swap(6, packed_grad, packed_in).wait_send()
    swap(7, g_cross, g_cross_in).wait_send()
    for c in given:
        c.wait_send()
    grad_copy.wait()
    for c in pix_copies:
        c.wait()


def mega(latents, pixels, counts, cotangent, gain_block, shards):
    rows, slots, width = latents.shape[1], pixels.shape[1], latents.shape[2]
    hidden = shards[6].shape[1]
    vm = pltpu.VMEM
    xt = lambda k: vm((2, 2, 4, UNIT_ROWS, k), BF16)
    wide = lambda n: vm((rows, n), BF16)
    scratch = [
        vm((2, 2, 2, 4, 2, UNIT_ROWS, UNIT_COLS), BF16),
        vm((2, 4, 2, 128, UNIT_COLS), BF16),
        vm((PARTIALS, 2, 2, 4, UNIT_ROWS, UNIT_COLS), BF16),
        vm((PARTIALS, 2, 4, UNIT_ROWS, UNIT_COLS), BF16),
        vm((RING, 4, UNIT_ROWS, UNIT_COLS), BF16),
        vm((RING, 4, 2, UNIT_ROWS, UNIT_COLS), BF16),
        xt(2 * rows), xt(2 * slots), xt(2 * rows), xt(2 * rows), xt(2 * rows), xt(2 * rows),
        vm((2, 2, 4, 128, 2 * rows), BF16),
        vm((2, 4, 2, 128, rows), BF16),
        vm((2, 2, 2, 4, 2, UNIT_ROWS, 256), BF16),
        wide(width), wide(width), wide(hidden), wide(hidden), wide(width), wide(width), wide(hidden), wide(3 * width),
        wide(width), wide(width),
        wide(width), wide(width), vm((slots, width), BF16), vm((slots, width), BF16), vm((slots, width), BF16), vm((slots, width), BF16),
        wide(width), vm((slots, width), BF16), vm((slots, width), BF16), wide(3 * width),
        vm((rows, width), F32), vm((rows, width), F32), vm((rows, width), F32), vm((slots, width), BF16), wide(width), vm((2, rows, width), F32),
        vm((2, 2, 4, 2, 8, 128), F32), vm((8, width), F32), vm((4, 8, width), F32), vm((8, width), F32), vm((5, 8, width), F32),
    ]
    sems = Gather.sems(16) + Scatter.sems(16)
    sems += [DMA((2,)), DMA((2,)), DMA((4,)), DMA((4,)), DMA((7,)), DMA((7,)), DMA((5,)), DMA((5,))]
    sems += [DMA((11,))] * 3 + [DMA((11,))] * 2
    outs = [
        jax.ShapeDtypeStruct(latents.shape, F32),
        jax.ShapeDtypeStruct(latents.shape, F32),
        jax.ShapeDtypeStruct(pixels.shape, F32),
        jax.ShapeDtypeStruct((8, width), F32),
    ]
    outs += [jax.ShapeDtypeStruct(s.shape, F32) for s in shards]
    outs += [jax.ShapeDtypeStruct((2, 2, 4, 2) + s.shape, s.dtype) for s in shards]
    hbm, vmem = pl.BlockSpec(memory_space=pl.ANY), pl.BlockSpec(memory_space=pltpu.VMEM)
    smem = pl.BlockSpec(memory_space=pltpu.SMEM)
    results = pl.pallas_call(
        mega_kernel,
        out_shape=outs,
        in_specs=[hbm, hbm, smem, hbm, hbm] + [vmem] * 8,
        out_specs=[hbm] * 3 + [vmem] + [vmem] * 8 + [hbm] * 8,
        scratch_shapes=scratch + sems,
        compiler_params=pltpu.CompilerParams(collective_id=0, has_side_effects=True, vmem_limit_bytes=63 * 2**20),
    )(latents, pixels, counts, cotangent, gain_block, *shards)
    return results[:4], results[4:12]


def layer_norm(inputs, gain):
    center = inputs - jnp.mean(inputs, axis=-1, keepdims=True)
    spread = jnp.mean(center * center, axis=-1, keepdims=True)
    return center * lax.rsqrt(spread + EPS) * gain


def project(inputs, matrix):
    return jnp.einsum("gld,de->gle", inputs, matrix, preferred_element_type=jnp.float32)


def project_back(grad_rows, matrix):
    return jnp.einsum("gle,de->gld", grad_rows, matrix, preferred_element_type=jnp.float32)


def weight_grad(inputs, grad_rows):
    return jnp.einsum("gld,gle->de", inputs, grad_rows, preferred_element_type=jnp.float32)


def split_heads(tensor):
    return tensor.reshape(tensor.shape[0], tensor.shape[1], HEADS, -1)


def merge_heads(tensor):
    return tensor.reshape(tensor.shape[0], tensor.shape[1], -1)


def scores_of(queries, key_rows, visible):
    scores = jnp.einsum("glhd,gshd->ghls", queries, key_rows, preferred_element_type=jnp.float32)
    scores = scores * queries.shape[-1] ** (-0.5)
    if visible is not None:
        scores = jnp.where(visible[:, None, None, :], scores, -1e30)
    return scores


def attend_forward(queries, key_rows, value_rows, visible):
    scores = scores_of(queries, key_rows, visible)
    largest = jnp.max(scores, axis=-1, keepdims=True)
    exp_scores = jnp.exp(scores - largest)
    totals = jnp.sum(exp_scores, axis=-1, keepdims=True)
    attn_probs = exp_scores / totals
    log_total = largest + jnp.log(totals)
    mixed = jnp.einsum(
        "ghls,gshd->glhd",
        attn_probs.astype(jnp.bfloat16),
        value_rows,
        preferred_element_type=jnp.float32,
    ).astype(jnp.bfloat16)
    return (mixed, log_total)


def attend_backward(queries, key_rows, value_rows, visible, log_total, mixed_grad):
    scale = queries.shape[-1] ** (-0.5)
    attn_probs = jnp.exp(scores_of(queries, key_rows, visible) - log_total)
    probs_grad = jnp.einsum(
        "glhd,gshd->ghls", mixed_grad, value_rows, preferred_element_type=jnp.float32
    )
    value_grad = jnp.einsum(
        "ghls,glhd->gshd",
        attn_probs.astype(jnp.bfloat16),
        mixed_grad,
        preferred_element_type=jnp.float32,
    ).astype(jnp.bfloat16)
    score_grad = attn_probs * (
        probs_grad - jnp.sum(probs_grad * attn_probs, axis=-1, keepdims=True)
    )
    score_grad = score_grad.astype(jnp.bfloat16)
    query_grad = (
        jnp.einsum("ghls,gshd->glhd", score_grad, key_rows, preferred_element_type=jnp.float32)
        * scale
    ).astype(jnp.bfloat16)
    key_grad = (
        jnp.einsum("ghls,glhd->gshd", score_grad, queries, preferred_element_type=jnp.float32)
        * scale
    ).astype(jnp.bfloat16)
    return (query_grad, key_grad, value_grad)


def local_plain(
    latents,
    pixels,
    slot_index,
    counts,
    cotangent,
    gain_q,
    gain_kv,
    w_query,
    w_key,
    w_value,
    w_out,
    gain_self,
    w_qkv,
    w_self_out,
    gain_mlp,
    w_up,
    w_down,
):
    groups = latents.shape[0]
    slots = pixels.shape[1]
    width = latents.shape[2]
    local_slot = slot_index % groups
    chosen = jnp.take(pixels, local_slot, axis=0).astype(jnp.float32)
    visible_count = jnp.take(counts, local_slot, axis=0)
    visible = lax.broadcasted_iota(jnp.int32, (groups, slots), 1) < visible_count[:, None]
    cross_all = (
        lax.all_gather(gain_q, ("dp", "fsdp"), axis=0, tiled=True),
        lax.all_gather(gain_kv, ("dp", "fsdp"), axis=0, tiled=True),
        lax.all_gather(w_query, ("dp", "fsdp"), axis=0, tiled=True),
        lax.all_gather(w_key, ("dp", "fsdp"), axis=0, tiled=True),
        lax.all_gather(w_value, ("dp", "fsdp"), axis=0, tiled=True),
        lax.all_gather(w_out, ("dp", "fsdp"), axis=0, tiled=True),
    )
    normed = layer_norm(latents, cross_all[0].astype(jnp.float32)).astype(jnp.bfloat16)
    pix_normed = layer_norm(chosen, cross_all[1].astype(jnp.float32)).astype(jnp.bfloat16)
    queries = split_heads(project(normed, cross_all[2]).astype(jnp.bfloat16))
    key_rows = split_heads(project(pix_normed, cross_all[3]).astype(jnp.bfloat16))
    value_rows = split_heads(project(pix_normed, cross_all[4]).astype(jnp.bfloat16))
    cross_mixed, cross_total = attend_forward(queries, key_rows, value_rows, visible)
    cross_flat = merge_heads(cross_mixed)
    after_cross = latents + project(cross_flat, cross_all[5])
    self_all = (
        lax.all_gather(gain_self, ("dp", "fsdp"), axis=0, tiled=True),
        lax.all_gather(w_qkv, ("dp", "fsdp"), axis=0, tiled=True),
        lax.all_gather(w_self_out, ("dp", "fsdp"), axis=0, tiled=True),
    )
    normed_self = layer_norm(after_cross, self_all[0].astype(jnp.float32)).astype(jnp.bfloat16)
    packed = project(normed_self, self_all[1]).astype(jnp.bfloat16)
    self_queries = split_heads(packed[..., :width])
    self_keys = split_heads(packed[..., width : 2 * width])
    self_values = split_heads(packed[..., 2 * width :])
    self_mixed, self_total = attend_forward(self_queries, self_keys, self_values, None)
    self_flat = merge_heads(self_mixed)
    after_self = after_cross + project(self_flat, self_all[2])
    mlp_all = (
        lax.all_gather(gain_mlp, ("dp", "fsdp"), axis=0, tiled=True),
        lax.all_gather(w_up, ("dp", "fsdp"), axis=0, tiled=True),
        lax.all_gather(w_down, ("dp", "fsdp"), axis=0, tiled=True),
    )
    normed_mlp = layer_norm(after_self, mlp_all[0].astype(jnp.float32)).astype(jnp.bfloat16)
    hidden = project(normed_mlp, mlp_all[1])
    activated = jax.nn.gelu(hidden).astype(jnp.bfloat16)
    latents_out = after_self + project(activated, mlp_all[2])
    root_mean = jnp.sqrt(jnp.mean(latents_out * latents_out, axis=(1, 2)))
    total_norm = lax.psum(jnp.sum(root_mean), ("dp", "fsdp"))
    norms = root_mean * (groups * lax.axis_size(("dp", "fsdp"))) / total_norm
    mlp_back = (
        lax.all_gather(gain_mlp, ("dp", "fsdp"), axis=0, tiled=True),
        lax.all_gather(w_up, ("dp", "fsdp"), axis=0, tiled=True),
        lax.all_gather(w_down, ("dp", "fsdp"), axis=0, tiled=True),
    )
    out_grad = cotangent.astype(jnp.bfloat16)
    down_grad = weight_grad(activated, out_grad)
    act_grad = project_back(out_grad, mlp_back[2])
    hidden_grad = jax.vjp(jax.nn.gelu, hidden)[1](act_grad)[0].astype(jnp.bfloat16)
    up_grad = weight_grad(normed_mlp, hidden_grad)
    mlp_in_grad = project_back(hidden_grad, mlp_back[1])
    after_self_ln, mlp_gain_grad = jax.vjp(layer_norm, after_self, mlp_back[0].astype(jnp.float32))[
        1
    ](mlp_in_grad)
    after_self_grad = cotangent + after_self_ln
    mlp_grads = (
        lax.psum_scatter(mlp_gain_grad, ("dp", "fsdp"), scatter_dimension=0, tiled=True),
        lax.psum_scatter(up_grad, ("dp", "fsdp"), scatter_dimension=0, tiled=True),
        lax.psum_scatter(down_grad, ("dp", "fsdp"), scatter_dimension=0, tiled=True),
    )
    self_back = (
        lax.all_gather(gain_self, ("dp", "fsdp"), axis=0, tiled=True),
        lax.all_gather(w_qkv, ("dp", "fsdp"), axis=0, tiled=True),
        lax.all_gather(w_self_out, ("dp", "fsdp"), axis=0, tiled=True),
    )
    self_branch = after_self_grad.astype(jnp.bfloat16)
    self_out_grad = weight_grad(self_flat, self_branch)
    self_mixed_grad = split_heads(project_back(self_branch, self_back[2]).astype(jnp.bfloat16))
    self_q_grad, self_k_grad, self_v_grad = attend_backward(
        self_queries, self_keys, self_values, None, self_total, self_mixed_grad
    )
    packed_grad = jnp.concatenate(
        [merge_heads(self_q_grad), merge_heads(self_k_grad), merge_heads(self_v_grad)], axis=-1
    )
    qkv_grad = weight_grad(normed_self, packed_grad)
    self_in_grad = project_back(packed_grad, self_back[1])
    after_cross_ln, self_gain_grad = jax.vjp(
        layer_norm, after_cross, self_back[0].astype(jnp.float32)
    )[1](self_in_grad)
    after_cross_grad = after_self_grad + after_cross_ln
    self_grads = (
        lax.psum_scatter(self_gain_grad, ("dp", "fsdp"), scatter_dimension=0, tiled=True),
        lax.psum_scatter(qkv_grad, ("dp", "fsdp"), scatter_dimension=0, tiled=True),
        lax.psum_scatter(self_out_grad, ("dp", "fsdp"), scatter_dimension=0, tiled=True),
    )
    cross_back = (
        lax.all_gather(gain_q, ("dp", "fsdp"), axis=0, tiled=True),
        lax.all_gather(gain_kv, ("dp", "fsdp"), axis=0, tiled=True),
        lax.all_gather(w_query, ("dp", "fsdp"), axis=0, tiled=True),
        lax.all_gather(w_key, ("dp", "fsdp"), axis=0, tiled=True),
        lax.all_gather(w_value, ("dp", "fsdp"), axis=0, tiled=True),
        lax.all_gather(w_out, ("dp", "fsdp"), axis=0, tiled=True),
    )
    cross_branch = after_cross_grad.astype(jnp.bfloat16)
    out_w_grad = weight_grad(cross_flat, cross_branch)
    cross_mixed_grad = split_heads(project_back(cross_branch, cross_back[5]).astype(jnp.bfloat16))
    query_grad, key_grad, value_grad = attend_backward(
        queries, key_rows, value_rows, visible, cross_total, cross_mixed_grad
    )
    query_flat = merge_heads(query_grad)
    key_flat = merge_heads(key_grad)
    value_flat = merge_heads(value_grad)
    query_w_grad = weight_grad(normed, query_flat)
    key_w_grad = weight_grad(pix_normed, key_flat)
    value_w_grad = weight_grad(pix_normed, value_flat)
    normed_grad = project_back(query_flat, cross_back[2])
    pix_normed_grad = project_back(key_flat, cross_back[3]) + project_back(
        value_flat, cross_back[4]
    )
    latents_ln, query_gain_grad = jax.vjp(layer_norm, latents, cross_back[0].astype(jnp.float32))[
        1
    ](normed_grad)
    latents_grad = after_cross_grad + latents_ln
    chosen_grad, pixel_gain_grad = jax.vjp(layer_norm, chosen, cross_back[1].astype(jnp.float32))[
        1
    ](pix_normed_grad)
    pixels_grad = jnp.zeros(pixels.shape, jnp.float32).at[local_slot].add(chosen_grad)
    cross_grads = (
        lax.psum_scatter(query_gain_grad, ("dp", "fsdp"), scatter_dimension=0, tiled=True),
        lax.psum_scatter(pixel_gain_grad, ("dp", "fsdp"), scatter_dimension=0, tiled=True),
        lax.psum_scatter(query_w_grad, ("dp", "fsdp"), scatter_dimension=0, tiled=True),
        lax.psum_scatter(key_w_grad, ("dp", "fsdp"), scatter_dimension=0, tiled=True),
        lax.psum_scatter(value_w_grad, ("dp", "fsdp"), scatter_dimension=0, tiled=True),
        lax.psum_scatter(out_w_grad, ("dp", "fsdp"), scatter_dimension=0, tiled=True),
    )
    return (
        latents_out,
        latents_grad,
        pixels_grad,
        cross_grads[0],
        cross_grads[1],
        cross_grads[2],
        cross_grads[3],
        cross_grads[4],
        cross_grads[5],
        self_grads[0],
        self_grads[1],
        self_grads[2],
        mlp_grads[0],
        mlp_grads[1],
        mlp_grads[2],
        norms,
    )


def local_fast(
    latents,
    pixels,
    slot_index,
    counts,
    cotangent,
    gain_q,
    gain_kv,
    w_query,
    w_key,
    w_value,
    w_out,
    gain_self,
    w_qkv,
    w_self_out,
    gain_mlp,
    w_up,
    w_down,
):
    gains = jnp.concatenate([gain_q, gain_kv, gain_self, gain_mlp]).astype(jnp.float32)
    gain_block = jnp.pad(gains[None, :], ((0, 7), (0, 0)))
    shards = (w_query, w_key, w_value, w_out, w_qkv, w_self_out, w_up, w_down)
    (latents_out, latents_grad, pixels_grad, small), grads = mega(latents, pixels, counts, cotangent, gain_block, shards)
    latents_out, latents_grad, pixels_grad, *grads = hand_out([latents_out, latents_grad, pixels_grad] + list(grads))
    rows = gain_q.shape[0]
    devices = lax.axis_size(("dp", "fsdp"))
    mine = lax.dynamic_slice(small[:4], (0, lax.axis_index(("dp", "fsdp")) * rows), (4, rows))
    norms = small[5, :1] * devices / small[4, :1]
    g_query, g_key, g_value, g_out, g_qkv, g_self_out, g_up, g_down = grads
    return (
        latents_out,
        latents_grad,
        pixels_grad,
        mine[0],
        mine[1],
        g_query,
        g_key,
        g_value,
        g_out,
        mine[2],
        g_qkv,
        g_self_out,
        mine[3],
        g_up,
        g_down,
        norms,
    )


def hand_out(arrays):
    n = len(arrays)

    def kernel(*refs):
        sems = refs[3 * n]
        fetch = [pltpu.make_async_copy(refs[k], refs[2 * n + k], sems.at[0, k]) for k in range(n)]
        put = [pltpu.make_async_copy(refs[2 * n + k], refs[n + k], sems.at[1, k]) for k in range(n)]
        for c in fetch:
            c.start()
        for k in range(n):
            fetch[k].wait()
            put[k].start()
        for c in put:
            c.wait()

    return pl.pallas_call(
        kernel,
        out_shape=[jax.ShapeDtypeStruct(a.shape, a.dtype) for a in arrays],
        in_specs=[pl.BlockSpec(memory_space=pl.ANY)] * n,
        out_specs=[pl.BlockSpec(memory_space=pl.ANY)] * n,
        scratch_shapes=[pltpu.VMEM(a.shape, a.dtype) for a in arrays] + [DMA((2, n))],
        compiler_params=pltpu.CompilerParams(vmem_limit_bytes=63 * 2**20),
    )(*arrays)


def fits(mesh):
    return mesh.shape["dp"] == 4 and mesh.shape["fsdp"] == 8


def solution(mesh):
    in_specs = (
        P(("dp", "fsdp"), None, None),
        P(("dp", "fsdp"), None, None),
        P(("dp", "fsdp")),
        P(("dp", "fsdp")),
        P(("dp", "fsdp"), None, None),
        P(("dp", "fsdp")),
        P(("dp", "fsdp")),
        P(("dp", "fsdp"), None),
        P(("dp", "fsdp"), None),
        P(("dp", "fsdp"), None),
        P(("dp", "fsdp"), None),
        P(("dp", "fsdp")),
        P(("dp", "fsdp"), None),
        P(("dp", "fsdp"), None),
        P(("dp", "fsdp")),
        P(("dp", "fsdp"), None),
        P(("dp", "fsdp"), None),
    )
    out_specs = (
        P(("dp", "fsdp"), None, None),
        P(("dp", "fsdp"), None, None),
        P(("dp", "fsdp"), None, None),
        P(("dp", "fsdp")),
        P(("dp", "fsdp")),
        P(("dp", "fsdp"), None),
        P(("dp", "fsdp"), None),
        P(("dp", "fsdp"), None),
        P(("dp", "fsdp"), None),
        P(("dp", "fsdp")),
        P(("dp", "fsdp"), None),
        P(("dp", "fsdp"), None),
        P(("dp", "fsdp")),
        P(("dp", "fsdp"), None),
        P(("dp", "fsdp"), None),
        P(("dp", "fsdp")),
    )
    return jax.shard_map(local_fast if fits(mesh) else local_plain, mesh=mesh, in_specs=in_specs, out_specs=out_specs, check_vma=False)
```

```python
import functools

import jax
import jax.numpy as jnp
from jax import lax
from jax.experimental import pallas as pl
from jax.experimental.pallas import tpu as pltpu
from jax.sharding import PartitionSpec as P

MESH = pl.DeviceIdType.MESH
DMA = pltpu.SemaphoreType.DMA
UNIT_COLS = 1024
UNIT_ROWS = 32
RING = 4
PARTIALS = 8
SCATTER_WIDTHS = ((256, 256, 256, 256),) * RING
GATHER_WIDTHS = ((256, 256, 256, 256),)
WHOLE = (0, 0, UNIT_COLS, 0)


class Place:
    def __init__(self):
        dp, f = lax.axis_index("dp"), lax.axis_index("fsdp")
        self.y, self.x, self.z, self.c = dp // 2, dp % 2, f // 2, f % 2
        step = jnp.where(self.z < 2, 1, -1)
        self.is_end = (self.z == 0) | (self.z == 3)
        self.z1 = jnp.where(self.is_end, self.z + step, self.z - step)
        self.z2 = jnp.where(self.is_end, self.z + 2 * step, self.z + step)
        self.z3 = jnp.where(self.is_end, self.z + 3 * step, self.z + 2 * step)

    def dev(self, y=None, x=None, z=None, c=None):
        y = self.y if y is None else y
        x = self.x if x is None else x
        z = self.z if z is None else z
        c = self.c if c is None else c
        return (y * 2 + x, z * 2 + c)

    def barrier(self):
        bar = pltpu.get_barrier_semaphore()
        peers = [
            self.dev(c=1 - self.c),
            self.dev(x=1 - self.x),
            self.dev(y=1 - self.y),
            self.dev(z=self.z1),
            self.dev(z=self.z2),
            self.dev(z=self.z3),
        ]
        for peer in peers:
            pl.semaphore_signal(bar, inc=1, device_id=peer, device_id_type=MESH)
        pl.semaphore_wait(bar, len(peers))


def remote(src, dst, send_sem, recv_sem, dev):
    return pltpu.make_async_remote_copy(
        src_ref=src, dst_ref=dst, send_sem=send_sem, recv_sem=recv_sem, device_id=dev, device_id_type=MESH
    )


def columns(widths, p, base):
    return pl.ds(base + sum(widths[:p]), widths[p])


class Unit:
    def __init__(self, kind, shard, full, row=0, col=0, rows=UNIT_ROWS):
        self.kind, self.shard, self.full, self.row, self.col, self.rows = kind, shard, full, row, col, rows


class Gather:
    STAGES = 7

    def __init__(self, me, units, sems):
        self.me, self.units = me, units
        self.loc, self.sib_s, self.sib_r, self.zs, self.zr, self.xs, self.xr, self.ys, self.yr = sems
        self.widths, plain = [], 0
        for unit in units:
            self.widths.append(GATHER_WIDTHS[plain % len(GATHER_WIDTHS)] if unit.kind == "all" else WHOLE)
            plain += unit.kind == "all"

    @staticmethod
    def sems(n):
        return [DMA((n,))] * 3 + [DMA((n, 4, 4))] * 2 + [DMA((n, 4))] * 4

    def at(self, u, y, x, z, c, p=None):
        unit = self.units[u]
        cols = pl.ds(unit.col, UNIT_COLS) if p is None else columns(self.widths[u], p, unit.col)
        rows = pl.ds(unit.row, unit.rows)
        if unit.kind == "down":
            return unit.full.at[y, z, c, rows, cols]
        return unit.full.at[y, x, z, c, rows, cols]

    def parts(self, u, *which):
        return [p for p in which if self.widths[u][p]]

    def half(self, u, x):
        unit = self.units[u]
        col = pl.multiple_of(2 * unit.col + x * UNIT_COLS, UNIT_COLS)
        return unit.shard.at[pl.ds(unit.row, unit.rows), pl.ds(col, UNIT_COLS)]

    def own(self, u):
        me, unit = self.me, self.units[u]
        if unit.kind == "up":
            src = self.half(u, me.x)
        else:
            src = unit.shard.at[pl.ds(unit.row, unit.rows), pl.ds(unit.col, UNIT_COLS)]
        return pltpu.make_async_copy(src, self.at(u, me.y, me.x, me.z, me.c), self.loc.at[u])

    def zblk(self, u, p, z):
        me, s = self.me, slice(None)
        return self.at(u, me.y if p != 3 else s, me.x if p != 2 else s, z, me.c, p)

    def zcopy(self, u, p, z_to, z_block=None):
        me = self.me
        if z_block is None:
            b = self.zblk(u, p, me.z)
            return remote(b, b, self.zs.at[u, p, z_to], self.zr.at[u, p, me.z], me.dev(z=z_to))
        b = self.zblk(u, p, z_block)
        return remote(b, b, self.zs.at[u, p, me.z], self.zr.at[u, p, z_block], me.dev(z=z_to))

    def zin(self, u, p, z_block):
        b = self.zblk(u, p, z_block)
        return remote(b, b, self.zs.at[u, p, z_block], self.zr.at[u, p, z_block], self.me.dev(z=z_block))

    def z_a(self, u, p):
        me = self.me
        self.zcopy(u, p, me.z1).start()
        self.zcopy(u, p, me.z2).start()

        @pl.when(~me.is_end)
        def _():
            self.zcopy(u, p, me.z3).start()

    def z_b(self, u, p):
        me = self.me

        @pl.when(~me.is_end)
        def _():
            self.zin(u, p, me.z3).wait_recv()
            self.zcopy(u, p, me.z1, me.z3).start()

    def z_wait(self, u, p):
        me = self.me
        self.zin(u, p, me.z1).wait_recv()
        self.zin(u, p, me.z2).wait_recv()

        @pl.when(me.is_end)
        def _():
            self.zin(u, p, me.z3).wait_recv()

    def z_sent(self, u, p):
        me = self.me
        self.zcopy(u, p, me.z1).wait_send()
        self.zcopy(u, p, me.z2).wait_send()

        @pl.when(~me.is_end)
        def _():
            self.zcopy(u, p, me.z3).wait_send()
            self.zcopy(u, p, me.z1, me.z3).wait_send()

    def xcopy(self, u, p, out=True):
        me, s = self.me, slice(None)
        b = self.at(u, me.y if p != 3 and p != 1 else s, me.x if out else 1 - me.x, me.z if p == 2 else s, me.c, p)
        if self.units[u].kind == "up" and out:
            return remote(self.half(u, 1 - me.x), b, self.xs.at[u, p], self.xr.at[u, p], me.dev(x=1 - me.x))
        return remote(b, b, self.xs.at[u, p], self.xr.at[u, p], me.dev(x=1 - me.x))

    def ycopy(self, u, p, out=True):
        me, s = self.me, slice(None)
        b = self.at(u, me.y if out else 1 - me.y, me.x if p != 2 and p != 0 else s, me.z if p == 3 else s, me.c, p)
        return remote(b, b, self.ys.at[u, p], self.yr.at[u, p], me.dev(y=1 - me.y))

    def final(self, u, out=True):
        me, s = self.me, slice(None)
        b = self.at(u, s, s, s, me.c if out else 1 - me.c)
        return remote(b, b, self.sib_s.at[u], self.sib_r.at[u], me.dev(c=1 - me.c))

    def stage(self, s, u):
        kind = self.units[u].kind
        if s == 1:
            for p in self.parts(u, 0, 1):
                self.z_a(u, p)
        elif s == 2:
            for p in self.parts(u, 0, 1):
                self.z_b(u, p)
            for p in self.parts(u, 2, 3):
                if kind != "down":
                    (self.xcopy if p == 2 else self.ycopy)(u, p, False).wait_recv()
                self.z_a(u, p)
        elif s == 3:
            for p in self.parts(u, 0, 1):
                self.z_wait(u, p)
                (self.xcopy if p == 0 else self.ycopy)(u, p).start()
            for p in self.parts(u, 2, 3):
                self.z_b(u, p)
        elif s == 4:
            for p in self.parts(u, 2, 3):
                self.z_wait(u, p)
                (self.ycopy if p == 2 else self.xcopy)(u, p).start()
            for p in self.parts(u, 0, 1):
                (self.xcopy if p == 0 else self.ycopy)(u, p, False).wait_recv()
                (self.ycopy if p == 0 else self.xcopy)(u, p).start()
        elif s == 5:
            for p in self.parts(u, 2, 3, 0, 1):
                (self.ycopy if p in (0, 2) else self.xcopy)(u, p, False).wait_recv()
            self.final(u).start()
        elif s == 6:
            self.final(u, False).wait_recv()

    def early(self, u):
        self.own(u).wait()
        for p in self.parts(u, 2, 3):
            if self.units[u].kind != "down":
                (self.xcopy if p == 2 else self.ycopy)(u, p).start()

    def sent(self, u):
        for p in self.parts(u, 0, 1, 2, 3):
            self.z_sent(u, p)
            if self.units[u].kind != "down":
                self.xcopy(u, p).wait_send()
            self.ycopy(u, p).wait_send()
        self.final(u).wait_send()

    def tick(self, t, wide):
        for u in range(len(self.units)):
            s = t - max(0, u - wide + 1)
            if 0 <= s < self.STAGES:
                self.stage(s, u)

    def ticks(self, wide):
        return self.STAGES + max(0, len(self.units) - wide)


class Scatter:
    STAGES = 5

    def __init__(self, me, units, refs, sems):
        self.me, self.units = me, units
        self.part, self.r1, self.r2, self.rz = refs
        self.s1, self.q1, self.s2, self.q2, self.zs, self.zr = sems

    @staticmethod
    def sems(n):
        return [DMA((n, 4))] * 4 + [DMA((n, 4, 4))] * 2

    def kind(self, u):
        return self.units[u][0]

    def widths(self, u):
        return SCATTER_WIDTHS[u % RING] if self.kind(u) == "all" else WHOLE

    def cols(self, u, p):
        return columns(self.widths(u), p, 0)

    def parts(self, u, *which):
        return [p for p in which if self.widths(u)[p]]

    def slot2(self, u):
        return u % RING if self.kind(u) == "all" else RING + u % 2

    def pt(self, u, p, y, x, z):
        return self.part.at[u % PARTIALS, y, x, z, :, self.cols(u, p)]

    def first(self, u, p):
        me, s = self.me, slice(None)
        dst = self.r1.at[u % PARTIALS, :, :, :, self.cols(u, p)]
        if p in (0, 2):
            return remote(self.pt(u, p, 1 - me.y, s, s), dst, self.s1.at[u, p], self.q1.at[u, p], me.dev(y=1 - me.y))
        return remote(self.pt(u, p, s, 1 - me.x, s), dst, self.s1.at[u, p], self.q1.at[u, p], me.dev(x=1 - me.x))

    def add(self, count, dst, srcs):
        def body(i, carry):
            total = dst(i)[...].astype(jnp.float32)
            for src in srcs:
                total = total + src(i)[...].astype(jnp.float32)
            dst(i)[...] = total.astype(jnp.bfloat16)
            return carry

        if count == 1:
            body(0, 0)
        else:
            lax.fori_loop(0, count, body, 0)

    def first_in(self, u, p):
        me = self.me
        self.first(u, p).wait_recv()
        if p in (0, 2):
            dst = lambda i: self.pt(u, p, me.y, i // 4, i % 4)
        else:
            dst = lambda i: self.pt(u, p, i // 4, me.x, i % 4)
        self.add(8, dst, [lambda i: self.r1.at[u % PARTIALS, i // 4, i % 4, :, self.cols(u, p)]])

    def second(self, u, p):
        me, s = self.me, slice(None)
        cols = self.cols(u, p)
        z = s if p < 2 else me.z
        dst = self.r2.at[self.slot2(u), :, :, cols] if p < 2 else self.r2.at[self.slot2(u), 0, :, cols]
        if p in (0, 2):
            return remote(self.pt(u, p, me.y, 1 - me.x, z), dst, self.s2.at[u, p], self.q2.at[u, p], me.dev(x=1 - me.x))
        return remote(self.pt(u, p, 1 - me.y, me.x, z), dst, self.s2.at[u, p], self.q2.at[u, p], me.dev(y=1 - me.y))

    def second_in(self, u, p):
        me = self.me
        self.second(u, p).wait_recv()
        self.add(
            4,
            lambda i: self.pt(u, p, me.y, me.x, i),
            [lambda i: self.r2.at[self.slot2(u), i, :, self.cols(u, p)]],
        )

    def zblk(self, u, p, z):
        me, s = self.me, slice(None)
        return self.pt(u, p, me.y if p != 3 else s, me.x if p != 2 else s, z)

    def zslot(self, u, p, slot):
        cols = self.cols(u, p)
        return self.rz.at[u % RING, slot, 0, :, cols] if p < 2 else self.rz.at[u % RING, slot, :, :, cols]

    def zcopy(self, u, p, which, block, slot, z_to):
        return remote(
            self.zblk(u, p, block), self.zslot(u, p, slot), self.zs.at[u, p, which], self.zr.at[u, p, slot], self.me.dev(z=z_to)
        )

    def z_ends(self, u, p):
        me = self.me
        return [
            self.zcopy(u, p, 2, me.z3, 3, me.z1),
            self.zcopy(u, p, 1, me.z2, 2, me.z2),
            self.zcopy(u, p, 0, me.z1, 0, me.z1),
        ]

    def z_mids(self, u, p):
        me = self.me
        return [self.zcopy(u, p, 0, me.z1, 0, me.z1), self.zcopy(u, p, 1, me.z2, 1, me.z2)]

    def z_gone(self, u, p):
        return self.zcopy(u, p, 2, self.me.z3, 1, self.me.z3)

    def z_a(self, u, p):
        me = self.me

        @pl.when(me.is_end)
        def _():
            for c in self.z_ends(u, p):
                c.start()

        @pl.when(~me.is_end)
        def _():
            for c in self.z_mids(u, p):
                c.start()

    def zget(self, u, p, slot):
        return self.zcopy(u, p, 0, self.me.z, slot, self.me.z1)

    def z_b(self, u, p):
        me = self.me

        @pl.when(~me.is_end)
        def _():
            self.zget(u, p, 3).wait_recv()
            self.z_add(u, p, me.z3, (3,))
            self.z_gone(u, p).start()

    def z_add(self, u, p, block, slots):
        cols = self.cols(u, p)
        me = self.me
        if p < 2:
            dst, count = (lambda i: self.pt(u, p, me.y, me.x, block)), 1
        elif p == 2:
            dst, count = (lambda i: self.pt(u, p, me.y, i, block)), 2
        else:
            dst, count = (lambda i: self.pt(u, p, i, me.x, block)), 2
        self.add(count, dst, [functools.partial(lambda slot, i: self.rz.at[u % RING, slot, i, :, cols], k) for k in slots])

    def z_in(self, u, p):
        me = self.me
        self.zget(u, p, 0).wait_recv()
        self.zget(u, p, 1).wait_recv()

        @pl.when(~me.is_end)
        def _():
            self.zget(u, p, 2).wait_recv()

    def out(self, u, p):
        _, out, row, col = self.units[u]
        return out.at[pl.ds(row, UNIT_ROWS), columns(self.widths(u), p, col)]

    def finish_z(self, u, p):
        me, cols = self.me, self.cols(u, p)
        self.z_in(u, p)
        f32 = lambda ref: ref[...].astype(jnp.float32)
        total = f32(self.pt(u, p, me.y, me.x, me.z)) + f32(self.rz.at[u % RING, 0, 0, :, cols]) + f32(self.rz.at[u % RING, 1, 0, :, cols])

        @pl.when(me.is_end)
        def _():
            self.out(u, p)[...] = total

        @pl.when(~me.is_end)
        def _():
            self.out(u, p)[...] = total + f32(self.rz.at[u % RING, 2, 0, :, cols])

    def finish_down(self, u):
        me = self.me
        _, out, row, col = self.units[u]
        self.z_in(u, 2)
        f32 = lambda ref: ref[...].astype(jnp.float32)
        for r in range(2):
            dst = out.at[pl.ds(row + r * UNIT_ROWS, UNIT_ROWS), pl.ds(col, UNIT_COLS)]
            dst[...] = f32(self.pt(u, 2, me.y, r, me.z)) + f32(self.rz.at[u % RING, 0, r]) + f32(self.rz.at[u % RING, 1, r])

            @pl.when(~me.is_end)
            def _():
                dst[...] = dst[...] + f32(self.rz.at[u % RING, 2, r])

    def finish_up(self, u):
        me = self.me
        _, out, row, col = self.units[u]
        self.second(u, 2).wait_recv()
        rows = pl.ds(row, UNIT_ROWS)
        for x, ref in ((me.x, self.pt(u, 2, me.y, me.x, me.z)), (1 - me.x, self.r2.at[self.slot2(u), 0])):
            cols = pl.ds(pl.multiple_of(2 * col + x * UNIT_COLS, UNIT_COLS), UNIT_COLS)
            out[rows, cols] = ref[...].astype(jnp.float32)

    def pass_z(self, u, p):
        me = self.me
        self.z_in(u, p)

        @pl.when(me.is_end)
        def _():
            self.z_add(u, p, me.z, (0, 1))

        @pl.when(~me.is_end)
        def _():
            self.z_add(u, p, me.z, (0, 1, 2))

        self.second(u, p).start()

    def finish_last(self, u, p):
        me, cols = self.me, self.cols(u, p)
        self.second(u, p).wait_recv()
        total = self.pt(u, p, me.y, me.x, me.z)[...].astype(jnp.float32) + self.r2.at[self.slot2(u), 0, :, cols][...].astype(jnp.float32)
        self.out(u, p)[...] = total

    def stage(self, s, u):
        kind = self.kind(u)
        if s == 0:
            for p in self.parts(u, 2, 3, 0, 1):
                self.first(u, p).start()
        elif s == 1:
            for p in self.parts(u, 2, 3):
                self.first_in(u, p)
                self.z_a(u, p)
            for p in self.parts(u, 0, 1):
                self.first_in(u, p)
                self.second(u, p).start()
        elif s == 2:
            for p in self.parts(u, 2, 3):
                self.z_b(u, p)
            for p in self.parts(u, 0, 1):
                self.second_in(u, p)
                self.z_a(u, p)
        elif s == 3:
            if kind == "down":
                self.finish_down(u)
            else:
                for p in self.parts(u, 2, 3):
                    self.pass_z(u, p)
            for p in self.parts(u, 0, 1):
                self.z_b(u, p)
        elif s == 4:
            if kind == "up":
                self.finish_up(u)
            elif kind == "all":
                for p in (0, 1):
                    self.finish_z(u, p)
                for p in (2, 3):
                    self.finish_last(u, p)

    def sent(self, u):
        me = self.me
        for p in self.parts(u, 0, 1, 2, 3):
            self.first(u, p).wait_send()
            if self.kind(u) != "down":
                self.second(u, p).wait_send()

            @pl.when(me.is_end)
            def _():
                for c in self.z_ends(u, p):
                    c.wait_send()

            @pl.when(~me.is_end)
            def _():
                for c in self.z_mids(u, p) + [self.z_gone(u, p)]:
                    c.wait_send()


EPS = 1e-05
HEADS = 8
GELU_A = 0.7978845608028654
GELU_B = 0.044715
NT = (((1,), (1,)), ((), ()))
F32, BF16 = jnp.float32, jnp.bfloat16


def matmul(a, b):
    return jnp.dot(a, b, preferred_element_type=F32)


def matmul_nt(a, b):
    return lax.dot_general(a, b, NT, preferred_element_type=F32)


def block(i, size):
    return pl.ds(pl.multiple_of(i * size, size), size)


def for_each(count, body):
    def step(i, carry):
        body(i)
        return carry

    lax.fori_loop(0, count, step, 0)


def normalise(v):
    center = v - jnp.mean(v, axis=-1, keepdims=True)
    inv = lax.rsqrt(jnp.mean(center * center, axis=-1, keepdims=True) + EPS)
    return center * inv, inv


def ln_forward(src, gain, dst):
    def body(i):
        rows = block(i, 32)
        n, _ = normalise(src[rows, :].astype(F32))
        dst[rows, :] = (n * gain[...]).astype(BF16)

    for_each(src.shape[0] // 32, body)


def ln_backward(src, row0, gain, incoming, base, gain_grad):
    def body(i):
        rows = block(i, 32)
        n, inv = normalise(src[pl.ds(pl.multiple_of(row0 + i * 32, 32), 32), :].astype(F32))
        g = incoming[rows, :]
        e = g * gain[...]
        grad = inv * (e - jnp.mean(e, axis=-1, keepdims=True) - n * jnp.mean(e * n, axis=-1, keepdims=True))
        prod = g * n
        gain_grad[...] += prod[0:8] + prod[8:16] + prod[16:24] + prod[24:32]
        if base is None:
            incoming[rows, :] = grad
        else:
            base[rows, :] = base[rows, :] + grad

    for_each(incoming.shape[0] // 32, body)


def attend_forward_heads(first, heads, q, q0, k, k0, v, v0, out, count):
    def body(i):
        h = first + i

        def head(ref, at):
            return ref[:, pl.ds(pl.multiple_of(at + h * 128, 128), 128)]

        s = matmul_nt(head(q, q0), head(k, k0)) * 128 ** (-0.5)
        if count is not None:
            s = jnp.where(lax.broadcasted_iota(jnp.int32, s.shape, 1) < count, s, -1e30)
        e = jnp.exp(s - jnp.max(s, axis=-1, keepdims=True))
        p = (e * (1.0 / jnp.sum(e, axis=-1, keepdims=True))).astype(BF16)
        out[:, block(h, 128)] = matmul(p, head(v, v0)).astype(BF16)

    for_each(heads, body)


def attend_backward_heads(first, heads, q, q0, k, k0, v, v0, mixed_grad, count, dq, dq0, dk, dk0, dv, dv0):
    scale = 128 ** (-0.5)

    def body(i):
        h = first + i

        def head(ref, at):
            return ref[:, pl.ds(pl.multiple_of(at + h * 128, 128), 128)]

        qh, kh, vh, gh = head(q, q0), head(k, k0), head(v, v0), head(mixed_grad, 0)
        s = matmul_nt(kh, qh) * scale
        if count is not None:
            s = jnp.where(lax.broadcasted_iota(jnp.int32, s.shape, 0) < count, s, -1e30)
        e = jnp.exp(s - jnp.max(s, axis=0, keepdims=True))
        p = e * (1.0 / jnp.sum(e, axis=0, keepdims=True))
        dv[:, pl.ds(pl.multiple_of(dv0 + h * 128, 128), 128)] = matmul(p.astype(BF16), gh).astype(BF16)
        dp = matmul_nt(vh, gh)
        ds = (p * (dp - jnp.sum(dp * p, axis=0, keepdims=True))).astype(BF16)
        dk[:, pl.ds(pl.multiple_of(dk0 + h * 128, 128), 128)] = (matmul(ds, qh) * scale).astype(BF16)
        dq[:, pl.ds(pl.multiple_of(dq0 + h * 128, 128), 128)] = (matmul(kh.T, ds).T * scale).astype(BF16)

    for_each(heads, body)


class SmallGather:
    def __init__(self, me, full, send, recv):
        self.me, self.full, self.send, self.recv = me, full, send, recv

    def copy(self, src, k, r, dev):
        return remote(src, src, self.send.at[k], self.recv.at[r], dev)

    def sib(self, out=True):
        me = self.me
        return self.copy(self.full.at[me.y, me.x, me.z, me.c if out else 1 - me.c], 0, 0, me.dev(c=1 - me.c))

    def zc(self, blk, k, r, to):
        me = self.me
        return self.copy(self.full.at[me.y, me.x, blk], k, r, me.dev(z=to))

    def xc(self, out=True):
        me = self.me
        return self.copy(self.full.at[me.y, me.x if out else 1 - me.x], 5, 5, me.dev(x=1 - me.x))

    def yc(self, out=True):
        me = self.me
        return self.copy(self.full.at[me.y if out else 1 - me.y], 6, 6, me.dev(y=1 - me.y))

    def run(self, s):
        me = self.me
        if s == 0:
            self.sib().start()
        elif s == 1:
            self.sib(False).wait_recv()
            self.zc(me.z, 1, 1 + me.z, me.z1).start()
            self.zc(me.z, 2, 1 + me.z, me.z2).start()

            @pl.when(~me.is_end)
            def _():
                self.zc(me.z, 3, 1 + me.z, me.z3).start()

        elif s == 2:

            @pl.when(~me.is_end)
            def _():
                self.zc(me.z3, 4, 1 + me.z3, me.z1).wait_recv()
                self.zc(me.z3, 4, 1 + me.z3, me.z1).start()

        elif s == 3:
            for z in (me.z1, me.z2):
                self.zc(z, 1, 1 + z, me.z1).wait_recv()

            @pl.when(me.is_end)
            def _():
                self.zc(me.z3, 1, 1 + me.z3, me.z1).wait_recv()

            self.xc().start()
        elif s == 4:
            self.xc(False).wait_recv()
            self.yc().start()
        elif s == 5:
            self.yc(False).wait_recv()
            self.sib().wait_send()
            self.zc(me.z, 1, 1 + me.z, me.z1).wait_send()
            self.zc(me.z, 2, 1 + me.z, me.z2).wait_send()

            @pl.when(~me.is_end)
            def _():
                self.zc(me.z, 3, 1 + me.z, me.z3).wait_send()
                self.zc(me.z3, 4, 1 + me.z3, me.z1).wait_send()

            self.xc().wait_send()
            self.yc().wait_send()


class SmallSum:
    def __init__(self, me, acc, got, send, recv):
        z_near = jnp.where(me.is_end, me.z1, me.z1)
        z_far = jnp.where(me.is_end, me.z2, me.z3)
        self.devs = [me.dev(c=1 - me.c), me.dev(x=1 - me.x), me.dev(y=1 - me.y), me.dev(z=z_near), me.dev(z=z_far)]
        self.acc, self.got, self.send, self.recv = acc, got, send, recv

    def copy(self, k):
        return remote(self.acc, self.got.at[k], self.send.at[k], self.recv.at[k], self.devs[k])

    def start(self, k):
        self.copy(k).start()

    def finish(self, k):
        c = self.copy(k)
        c.wait_send()
        c.wait_recv()
        self.acc[...] += self.got[k]


def mega_kernel(*refs):
    it = iter(refs)
    take = lambda n: [next(it) for _ in range(n)]
    latents, pixels, counts, cotangent, gain_block = take(5)
    shards = take(8)
    latents_out, latents_grad, pixels_grad, small_out = take(4)
    grads_out = take(8)
    fulls = take(8)
    (
        w_buf, wd_buf, part, r1, r2, rz,
        xt_normed, xt_pix, xt_mixed, xt_nself, xt_smixed, xt_nmlp, xt_act, st_a, st_b,
        g_out, g_out_in, hid, hid_in, g_branch, g_branch_in, act, packed_in,
        dq, dq_in, big, dk_in, dv, dv_in,
        queries, keys, values, packed, after_cross, after_self, resid, pix, tmp, acc,
        gain_full, gain_vec, gain_acc, small, small_got,
    ) = take(44)
    gather_sems, scatter_sems = take(9), take(6)
    w_sem, wd_sem, in_sem, out_sem, sg_s, sg_r, ss_s, ss_r, xl, xs, xr, gs, gr, across_s, across_r = take(15)
    me = Place()

    plain = lambda i, k: Unit("all", shards[i], fulls[i], 0, k * UNIT_COLS)
    up_unit = lambda k: Unit("up", shards[6], fulls[6], 0, k * UNIT_COLS)
    down_unit = lambda k: Unit("down", shards[7], fulls[7], 2 * k * UNIT_ROWS, 0, 2 * UNIT_ROWS)
    order = ["key", "value", "query", "out", "qkv0", "qkv1", "qkv2", "self", "up0", "up1", "down0", "down1"]
    made = {"query": plain(0, 0), "key": plain(1, 0), "value": plain(2, 0), "out": plain(3, 0), "self": plain(5, 0)}
    made.update({f"qkv{k}": plain(4, k) for k in range(3)})
    made.update({f"up{k}": up_unit(k) for k in range(2)})
    made.update({f"down{k}": down_unit(k) for k in range(2)})
    gather = Gather(me, [made[name] for name in order], gather_sems)
    scatter_units = [("down", grads_out[7], 2 * k * UNIT_ROWS, 0) for k in range(2)]
    scatter_units += [("up", grads_out[6], 0, k * UNIT_COLS) for k in range(2)]
    scatter_units += [("all", grads_out[5], 0, 0)] + [("all", grads_out[4], 0, k * UNIT_COLS) for k in range(3)]
    scatter_units += [("all", grads_out[i], 0, 0) for i in (3, 2, 1, 0)]
    scatter = Scatter(me, scatter_units, (part, r1, r2, rz), scatter_sems)
    pushed = [0]
    tick = [0]

    clock = [0.0]
    settled = [-1]
    ready = []

    def tick_ready(t):
        return 17 + 3.7 * min(t, 6) + 8.4 * min(max(0, t - 6), 8) + 11.5 * max(0, t - 14)

    def settle_ready(k):
        return ready[k] if k < len(ready) else ready[-1] + 4.0 * (k - len(ready) + 1)

    def next_tick():
        clock[0] = max(clock[0], tick_ready(tick[0])) + 0.5
        gather.tick(tick[0], 1)
        tick[0] += 1

    def next_settle():
        settled[0] += 1
        last = settled[0]
        clock[0] = max(clock[0], settle_ready(last)) + 1.0
        for s in range(Scatter.STAGES - 1, 0, -1):
            if 0 <= last - s < len(scatter_units):
                scatter.stage(s, last - s)

    def spend(us):
        clock[0] += us
        while True:
            k = settled[0] + 1
            if tick[0] < gather.ticks(1) and tick_ready(tick[0]) <= clock[0]:
                next_tick()
            elif pushed[0] and k <= pushed[0] and k < len(scatter_units) + 4 and settle_ready(k) <= clock[0]:
                next_settle()
            else:
                break

    def arrived(name):
        u = order.index(name)
        while tick[0] < gather.ticks(1) and tick[0] <= u + Gather.STAGES - 1:
            next_tick()

    def gather_to(t):
        while tick[0] <= t:
            next_tick()

    def settle_to(last):
        while settled[0] < last:
            next_settle()

    def load(k, src, dst):
        return pltpu.make_async_copy(src, dst, in_sem.at[k])

    def across(k, src, dst):
        return remote(src, dst, across_s.at[k], across_r.at[k], me.dev(x=1 - me.x))

    mine, theirs = pl.ds(0, 256), pl.ds(256, 256)
    loads = [load(0, latents.at[0], after_self), load(1, pixels.at[0], pix), load(2, cotangent.at[0], resid)]
    own_gain = load(3, gain_block, gain_full.at[me.y, me.x, me.z, me.c])
    own_gain.start()
    loads[2].start()
    for u in range(len(gather.units)):
        gather.own(u).start()
    loads[0].start()
    loads[1].start()
    loads[2].wait()
    for_each(8, lambda i: g_out.__setitem__((block(i, 32), slice(None)), resid[block(i, 32), :].astype(BF16)))
    own_gain.wait()
    gains = SmallGather(me, gain_full, sg_s, sg_r)
    me.barrier()
    gains.run(0)
    gather.early(0)
    gather_to(1)
    for u in range(1, len(gather.units)):
        gather.early(u)
    across(0, g_out.at[mine], g_out.at[theirs]).start()
    gains.run(1)
    for s in range(2, 6):
        gather_to(s)
        gains.run(s)
    table = jnp.sum(gain_full[...].reshape(32, 8, 128), axis=1).astype(BF16)
    width = latents.shape[2]
    lane = lax.broadcasted_iota(jnp.int32, (128, width), 1)
    place = lax.broadcasted_iota(jnp.int32, (128, width), 0)
    owner = lax.broadcasted_iota(jnp.int32, (32, width), 0) == (lax.broadcasted_iota(jnp.int32, (32, width), 1) >> 5)
    for g in range(4):
        pick = jnp.where(place == (lane & 31) + 32 * g, 1.0, 0.0).astype(BF16)
        spread = jnp.where(owner, matmul(table, pick), 0.0)
        gain_vec[g : g + 1, :] = jnp.sum(spread, axis=0, keepdims=True)
    gain = [gain_vec.at[g : g + 1, :] for g in range(4)]
    for g in range(4):
        gain_acc[g] = jnp.zeros_like(gain_acc[g])

    staged = [None, None]

    def hand_over(k, stage, mine, slot, own_dst, far_dst):
        a = pltpu.make_async_copy(mine, own_dst, xl.at[k])
        b = remote(stage, far_dst, xs.at[k], xr.at[k], me.dev(c=1 - me.c))
        a.start()
        b.start()
        staged[slot] = (a, b)

    def clear(slot):
        if staged[slot] is not None:
            a, b = staged[slot]
            a.wait()
            b.wait_send()
            staged[slot] = None

    turn = [0]

    def transpose_out(k, x, row0, xt, k_rows):
        slot = turn[0] % 2
        turn[0] += 1
        clear(slot)

        def body(j):
            piece = x[pl.ds(row0, 256), block(j, 256)].T
            st_b[slot, j // 2, j % 2] = piece.reshape(4, 2, 32, 256)

        for_each(4, body)
        hand_over(
            k,
            st_b.at[slot, :, :, :, 1 - me.c],
            st_b.at[slot, :, :, :, me.c],
            slot,
            xt.at[:, :, :, :, pl.ds(row0, 256)],
            xt.at[:, :, :, :, pl.ds(k_rows + row0, 256)],
        )

    def xt_wait(k, xt, row0, k_rows):
        remote(
            st_b.at[0, :, :, :, 0],
            xt.at[:, :, :, :, pl.ds(k_rows + row0, 256)],
            xs.at[k],
            xr.at[k],
            me.dev(c=1 - me.c),
        ).wait_recv()

    def swap(k, src, dst):
        return remote(src, dst, gs.at[k], gr.at[k], me.dev(c=1 - me.c))

    w_turn = [0]

    def w_start(full, col):
        slot = w_turn[0] % 2
        w_turn[0] += 1
        c = pltpu.make_async_copy(full.at[:, :, :, :, :, pl.ds(col, UNIT_COLS)], w_buf.at[slot], w_sem.at[slot])
        c.start()
        return slot, c

    def w_fetch(full, col):
        slot, c = w_start(full, col)
        c.wait()
        return slot

    def w_cols(slot, j):
        return w_buf[slot, :, :, :, :, :, block(j, 256)].reshape(width, 256)

    def w_rows(slot, j):
        return w_buf[slot, j // 2, j % 2].reshape(256, UNIT_COLS)

    def project(x, slot, out):
        for_each(4, lambda j: out(j, matmul(x[...], w_cols(slot, j))))

    def store(dst, col0=0):
        def put(j, tile):
            dst[:, pl.ds(pl.multiple_of(col0 + j * 256, 256), 256)] = tile.astype(dst.dtype)

        return put

    def back(g, col0, slot, dst, first):
        def body(j):
            tile = matmul_nt(g[:, pl.ds(col0, UNIT_COLS)], w_rows(slot, j))
            cols = block(j, 256)
            if first:
                dst[:, cols] = tile.astype(dst.dtype)
            else:
                dst[:, cols] = dst[:, cols] + tile

        for_each(4, body)

    def partial_sums(us, body):
        u = pushed[0]
        settle_to(u - 3)
        if u >= PARTIALS:
            scatter.sent(u - PARTIALS)
        body(u % PARTIALS)
        scatter.stage(0, u)
        pushed[0] += 1
        clock[0] += us
        lag, gap = (18, 10) if scatter.kind(u) == "all" else (24, 12)
        ready.append(max(clock[0] + lag, (ready[-1] if ready else 0) + gap))
        spend(0)

    def weight_grad(xt_at, rows, own, far, col0):
        def fill(slot):
            def body(j):
                cols = pl.ds(pl.multiple_of(col0 + j * 256, 256), 256)
                total = matmul(xt_at(0), own[:, cols]) + matmul(xt_at(rows), far[:, cols])
                part[slot, :, :, :, :, block(j, 256)] = total.astype(BF16).reshape(2, 2, 4, UNIT_ROWS, 256)

            for_each(4, body)

        partial_sums(1.7 if rows > 256 else 1.2, fill)

    def xt_of(xt, rows):
        return lambda at: xt[:, :, :, :, pl.ds(at, rows)].reshape(512, rows)

    loads[0].wait()
    loads[1].wait()
    ln_forward(after_self, gain[0], tmp)
    transpose_out(0, tmp, 0, xt_normed, 256)
    spend(2)
    ln_forward(pix, gain[1], big)
    transpose_out(1, big, 0, xt_pix, 512)
    spend(3.3)
    transpose_out(2, big, 256, xt_pix, 512)
    count = counts[0]
    arrived("key")
    project(big, w_fetch(fulls[1], 0), store(keys))
    spend(3.3)
    arrived("value")
    project(big, w_fetch(fulls[2], 0), store(values))
    spend(3.3)
    arrived("query")
    project(tmp, w_fetch(fulls[0], 0), store(queries))
    spend(2.7)
    for half in range(2):
        attend_forward_heads(4 * half, 4, queries, 0, keys, 0, values, 0, tmp, count)
        spend(2.3)
    arrived("out")
    transpose_out(3, tmp, 0, xt_mixed, 256)

    def add_to(dst, src):
        def put(j, tile):
            dst[:, block(j, 256)] = src[:, block(j, 256)] + tile

        return put

    project(tmp, w_fetch(fulls[3], 0), add_to(after_cross, after_self))
    spend(3)

    ln_forward(after_cross, gain[2], tmp)
    transpose_out(4, tmp, 0, xt_nself, 256)
    spend(1.8)
    for k in range(3):
        arrived(f"qkv{k}")
        project(tmp, w_fetch(fulls[4], k * UNIT_COLS), store(packed, k * UNIT_COLS))
        spend(2.7)
    for half in range(2):
        attend_forward_heads(4 * half, 4, packed, 0, packed, UNIT_COLS, packed, 2 * UNIT_COLS, tmp, None)
        spend(2.2)
    arrived("self")
    transpose_out(5, tmp, 0, xt_smixed, 256)
    project(tmp, w_fetch(fulls[5], 0), add_to(after_self, after_cross))
    spend(3)

    across(0, g_out.at[mine], g_out.at[theirs]).wait_recv()
    swap(0, g_out, g_out_in).start()
    ln_forward(after_self, gain[3], big.at[mine])
    across(1, big.at[mine], big.at[theirs]).start()
    transpose_out(6, big, 0, xt_nmlp, 512)
    spend(1.8)

    def up_rows(slot, k, rows):
        def up(j):
            x = matmul(big[rows, :], w_cols(slot, j))
            t = jnp.tanh(GELU_A * (x + GELU_B * (x * x * x)))
            half = 0.5 * (1.0 + t)
            cols = pl.ds(pl.multiple_of(k * UNIT_COLS + j * 256, 256), 256)
            act[rows, cols] = (x * half).astype(BF16)
            slope = half + (0.5 * GELU_A) * x * (1.0 - t * t) * (1.0 + (3 * GELU_B) * (x * x))
            hid[rows, cols] = slope.astype(BF16)

        for_each(4, up)

    a_staged = [None, None]
    act_copies = []

    def act_out(k, row0):
        n = len(act_copies)
        slot = n % 2
        if n >= 2:
            act_copies[n - 2][0].wait()
            act_copies[n - 2][1].wait_send()

        def body(m):
            st_a[slot, m // 2, m % 2] = act[pl.ds(row0, 256), pl.ds(pl.multiple_of(k * UNIT_COLS + m * 128, 128), 128)].T

        for_each(8, body)
        a = pltpu.make_async_copy(st_a.at[slot, :, me.c], xt_act.at[k, :, :, pl.ds(row0, 256)], xl.at[8 + n])
        b = remote(
            st_a.at[slot, :, 1 - me.c],
            xt_act.at[k, :, :, pl.ds(512 + row0, 256)],
            xs.at[8 + n],
            xr.at[8 + n],
            me.dev(c=1 - me.c),
        )
        a.start()
        b.start()
        act_copies.append((a, b))

    up_slots = []
    for k in range(2):
        arrived(f"up{k}")
        up_slots.append(w_fetch(fulls[6], k * UNIT_COLS))
        up_rows(up_slots[k], k, mine)
        spend(2.8)
        act_out(k, 0)
        spend(0.5)
    across(1, big.at[mine], big.at[theirs]).wait_recv()
    for k in range(2):
        up_rows(up_slots[k], k, theirs)
        spend(1.3)
        act_out(k, 256)
        spend(0.5)
    transpose_out(7, big, 256, xt_nmlp, 512)
    for a, b in act_copies[2:]:
        a.wait()
        b.wait_send()
    for _, b in act_copies:
        b.wait_recv()
    for slot in range(2):
        clear(slot)
    spend(2)

    swap(0, g_out, g_out_in).wait_recv()

    def down_grad(k):
        def fill(slot):
            def body(i):
                r, cols = i // 4, block(i % 4, 256)
                rows = pl.ds(pl.multiple_of((2 * k + r) * UNIT_ROWS, UNIT_ROWS), UNIT_ROWS)
                near = xt_act[:, :, rows, pl.ds(0, 512)].reshape(256, 512)
                far = xt_act[:, :, rows, pl.ds(512, 512)].reshape(256, 512)
                total = matmul(near, g_out[:, cols]) + matmul(far, g_out_in[:, cols])
                part[slot, :, r, :, :, cols] = total.astype(BF16).reshape(2, 4, UNIT_ROWS, 256)

            for_each(8, body)

        partial_sums(2, fill)

    down_grad(0)
    arrived("down1")

    wd_turn = [0]

    def wd_start(q):
        slot = wd_turn[0] % 2
        wd_turn[0] += 1
        c = pltpu.make_async_copy(fulls[7].at[q], wd_buf.at[slot], wd_sem.at[slot])
        c.start()
        return slot, c

    wd = [wd_start(0), wd_start(1)]
    for q in range(2):
        slot, c = wd[q]
        c.wait()

        def hidden_back(j):
            w = wd_buf[slot, j].reshape(256, width)
            tile = matmul_nt(g_out[...], w)
            cols = pl.ds(pl.multiple_of(q * UNIT_COLS + j * 256, 256), 256)
            hid[:, cols] = (hid[:, cols].astype(F32) * tile).astype(BF16)

        for_each(4, hidden_back)
        cols = pl.ds(q * UNIT_COLS, UNIT_COLS)
        swap(1 + q, hid.at[:, cols], hid_in.at[:, cols]).start()
        spend(2)
    for k in range(2):
        back(hid.at[theirs], k * UNIT_COLS, up_slots[k], acc.at[0], k == 0)
        spend(1.3)
    across(1, big.at[mine], big.at[theirs]).wait_send()
    for_each(8, lambda i: big.__setitem__((block(i, 32), slice(None)), acc[0, block(i, 32), :].astype(BF16)))
    across(2, big.at[mine], tmp).start()
    down_grad(1)
    for k in range(2):
        back(hid.at[mine], k * UNIT_COLS, up_slots[k], acc.at[1], k == 0)
        spend(1.3)
    xt_wait(6, xt_nmlp, 0, 512)
    xt_wait(7, xt_nmlp, 256, 512)
    for k in range(2):
        cols = pl.ds(k * UNIT_COLS, UNIT_COLS)
        swap(1 + k, hid.at[:, cols], hid_in.at[:, cols]).wait_recv()
        weight_grad(xt_of(xt_nmlp, 512), 512, hid, hid_in, k * UNIT_COLS)
    across(2, big.at[mine], tmp).wait_recv()

    def add_theirs(i):
        rows = block(i, 32)
        acc[1, rows, :] = acc[1, rows, :] + tmp[rows, :].astype(F32)

    for_each(8, add_theirs)
    so_slot, c_so = w_start(fulls[5], 0)
    ln_backward(after_self, 0, gain[3], acc.at[1], resid, gain_acc.at[3])
    spend(2.3)

    def round_rows(dst):
        for_each(8, lambda i: dst.__setitem__((block(i, 32), slice(None)), resid[block(i, 32), :].astype(BF16)))

    round_rows(g_branch)
    swap(3, g_branch, g_branch_in).start()
    c_so.wait()
    qkv_w = w_start(fulls[4], 0)
    back(g_branch, 0, so_slot, tmp, True)
    spend(1.8)
    swap(3, g_branch, g_branch_in).wait_recv()
    xt_wait(5, xt_smixed, 0, 256)
    weight_grad(xt_of(xt_smixed, 256), 256, g_branch, g_branch_in, 0)
    for q in range(2):
        cols = pl.ds(q * UNIT_COLS, UNIT_COLS)
        swap(1 + q, hid.at[:, cols], hid_in.at[:, cols]).wait_send()
    corner = [hid.at[mine, pl.ds(0, UNIT_COLS)], hid.at[mine, pl.ds(UNIT_COLS, UNIT_COLS)], hid.at[theirs, pl.ds(0, UNIT_COLS)]]
    for half in range(2):
        attend_backward_heads(
            4 * half, 4, packed, 0, packed, UNIT_COLS, packed, 2 * UNIT_COLS, tmp, None,
            corner[0], 0, corner[1], 0, corner[2], 0,
        )
        spend(3.4)
    packed_swaps = [swap(4 + k, corner[k], packed_in.at[k]) for k in range(3)]
    for c in packed_swaps:
        c.start()
    for k in range(3):
        slot, c = qkv_w
        c.wait()
        if k < 2:
            qkv_w = w_start(fulls[4], (k + 1) * UNIT_COLS)
        back(corner[k], 0, slot, acc.at[0], k == 0)
        spend(1.3)
        packed_swaps[k].wait_recv()
        if k == 0:
            xt_wait(4, xt_nself, 0, 256)
        weight_grad(xt_of(xt_nself, 256), 256, corner[k], packed_in.at[k], 0)
    wo_slot, c_wo = w_start(fulls[3], 0)
    ln_backward(after_cross, 0, gain[2], acc.at[0], resid, gain_acc.at[2])
    spend(2.3)

    swap(3, g_branch, g_branch_in).wait_send()
    round_rows(g_branch)
    swap(7, g_branch, g_branch_in).start()
    c_wo.wait()
    back(g_branch, 0, wo_slot, tmp, True)
    spend(1.8)
    swap(7, g_branch, g_branch_in).wait_recv()
    xt_wait(3, xt_mixed, 0, 256)
    weight_grad(xt_of(xt_mixed, 256), 256, g_branch, g_branch_in, 0)

    across(2, big.at[mine], tmp).wait_send()
    for half in range(2):
        attend_backward_heads(4 * half, 4, queries, 0, keys, 0, values, 0, tmp, count, dq, 0, big, 0, dv, 0)
        spend(3.2)
    given = [swap(8, dv, dv_in), swap(9, big, dk_in), swap(10, dq, dq_in)]
    for c in given:
        c.start()
    w_v = w_start(fulls[2], 0)
    w_k = w_start(fulls[1], 0)
    xt_wait(1, xt_pix, 0, 512)
    xt_wait(2, xt_pix, 256, 512)
    given[0].wait_recv()
    weight_grad(xt_of(xt_pix, 512), 512, dv, dv_in, 0)
    given[1].wait_recv()
    weight_grad(xt_of(xt_pix, 512), 512, big, dk_in, 0)
    xt_wait(0, xt_normed, 0, 256)
    given[2].wait_recv()
    weight_grad(xt_of(xt_normed, 256), 256, dq, dq_in, 0)
    def down(rows, slot, q, dst, base):
        def body(j):
            w = wd_buf[slot, :, :, :, block(j, 256)].reshape(UNIT_COLS, 256)
            tile = matmul(act[rows, pl.ds(q * UNIT_COLS, UNIT_COLS)], w)
            cols = block(j, 256)
            if base is None:
                dst[:, cols] = tile
            else:
                dst[:, cols] = base[:, cols] + tile

        for_each(4, body)
        spend(1.3)

    outer = hid.at[theirs, pl.ds(UNIT_COLS, UNIT_COLS)]
    down(theirs, wd[0][0], 0, after_cross, None)
    down(theirs, wd[1][0], 1, after_cross, after_cross)
    for_each(8, lambda i: tmp.__setitem__((block(i, 32), slice(None)), after_cross[block(i, 32), :].astype(BF16)))
    across(3, tmp, outer).start()
    w_v[1].wait()
    for r in range(2):
        back(dv.at[pl.ds(256 * r, 256)], 0, w_v[0], acc.at[r], True)
        spend(1.3)
    w_q = w_start(fulls[0], 0)
    w_k[1].wait()
    pix_copies = []
    for r in range(2):
        back(big.at[pl.ds(256 * r, 256)], 0, w_k[0], acc.at[r], False)
        spend(1.3)
        ln_backward(pix, 256 * r, gain[1], acc.at[r], None, gain_acc.at[1])
        c = pltpu.make_async_copy(acc.at[r], pixels_grad.at[0, pl.ds(256 * r, 256)], out_sem.at[2 + r])
        c.start()
        pix_copies.append(c)
        spend(2.3)
    down(mine, wd[0][0], 0, after_cross, after_self)
    down(mine, wd[1][0], 1, after_cross, after_cross)
    again = load(0, latents.at[0], after_self)
    again.start()
    across(3, tmp, outer).wait_recv()
    small[...] = jnp.zeros_like(small)

    def add_output(i, total):
        rows = block(i, 32)
        v = after_cross[rows, :] + outer[rows, :].astype(F32)
        after_cross[rows, :] = v
        v = v * v
        return total + v[0:8] + v[8:16] + v[16:24] + v[24:32]

    squares = lax.fori_loop(0, 8, add_output, jnp.zeros((8, width), F32))
    out_copy = pltpu.make_async_copy(after_cross, latents_out.at[0], out_sem.at[0])
    out_copy.start()
    mean_square = jnp.sum(jnp.sum(squares, axis=1, keepdims=True), axis=0, keepdims=True) / (latents.shape[1] * width)
    root_mean = jnp.sqrt(mean_square)
    small[4:5, :] = jnp.broadcast_to(root_mean, (1, width))
    spend(1)
    pix_copies[0].wait()
    w_q[1].wait()
    back(dq, 0, w_q[0], acc.at[0], True)
    spend(1.3)
    again.wait()
    ln_backward(after_self, 0, gain[0], acc.at[0], resid, gain_acc.at[0])
    grad_copy = pltpu.make_async_copy(resid, latents_grad.at[0], out_sem.at[1])
    grad_copy.start()
    spend(2.3)
    for g in range(4):
        small[g : g + 1, :] = jnp.sum(gain_acc[g], axis=0, keepdims=True)
    total = SmallSum(me, small, small_got, ss_s, ss_r)
    for k in range(5):
        total.start(k)
        if settled[0] < len(scatter_units) + 3:
            next_settle()
        total.finish(k)
    settle_to(len(scatter_units) + 3)
    small[5:6, :] = jnp.broadcast_to(root_mean, (1, width))
    small_out[...] = small[...]

    for u in range(len(gather.units)):
        gather.sent(u)
    for u in range(len(scatter_units) - PARTIALS, len(scatter_units)):
        scatter.sent(u)
    swap(0, g_out, g_out_in).wait_send()
    across(0, g_out.at[mine], g_out.at[theirs]).wait_send()
    for c in packed_swaps:
        c.wait_send()
    swap(7, g_branch, g_branch_in).wait_send()
    for c in given:
        c.wait_send()
    grad_copy.wait()
    pix_copies[1].wait()
    out_copy.wait()
    across(3, tmp, outer).wait_send()


def mega(latents, pixels, counts, cotangent, gain_block, shards):
    rows, slots, width = latents.shape[1], pixels.shape[1], latents.shape[2]
    hidden = shards[6].shape[1]
    vm = pltpu.VMEM
    xt = lambda k: vm((2, 2, 4, UNIT_ROWS, k), BF16)
    wide = lambda n: vm((rows, n), BF16)
    scratch = [
        vm((2, 2, 2, 4, 2, UNIT_ROWS, UNIT_COLS), BF16),
        vm((2, 4, 2, 128, UNIT_COLS), BF16),
        vm((PARTIALS, 2, 2, 4, UNIT_ROWS, UNIT_COLS), BF16),
        vm((PARTIALS, 2, 4, UNIT_ROWS, UNIT_COLS), BF16),
        vm((RING + 2, 4, UNIT_ROWS, UNIT_COLS), BF16),
        vm((RING, 4, 2, UNIT_ROWS, UNIT_COLS), BF16),
        xt(2 * rows), xt(2 * slots), xt(2 * rows), xt(2 * rows), xt(2 * rows), xt(4 * rows),
        vm((2, 4, 128, 4 * rows), BF16),
        vm((2, 4, 2, 128, rows), BF16),
        vm((2, 2, 2, 4, 2, UNIT_ROWS, 256), BF16),
        vm((2 * rows, width), BF16), vm((2 * rows, width), BF16), vm((2 * rows, hidden // 2), BF16), vm((2 * rows, hidden // 2), BF16),
        wide(width), wide(width), vm((2 * rows, hidden // 2), BF16), vm((3, rows, width), BF16),
        wide(width), wide(width), vm((slots, width), BF16), vm((slots, width), BF16), vm((slots, width), BF16), vm((slots, width), BF16),
        wide(width), vm((slots, width), BF16), vm((slots, width), BF16), wide(3 * width),
        vm((rows, width), F32), vm((rows, width), F32), vm((rows, width), F32), vm((slots, width), BF16), wide(width), vm((2, rows, width), F32),
        vm((2, 2, 4, 2, 8, 128), F32), vm((8, width), F32), vm((4, 8, width), F32), vm((8, width), F32), vm((5, 8, width), F32),
    ]
    sems = Gather.sems(12) + Scatter.sems(12)
    sems += [DMA((2,)), DMA((2,)), DMA((4,)), DMA((4,)), DMA((7,)), DMA((7,)), DMA((5,)), DMA((5,))]
    sems += [DMA((12,))] * 3 + [DMA((11,))] * 2 + [DMA((4,))] * 2
    outs = [
        jax.ShapeDtypeStruct(latents.shape, F32),
        jax.ShapeDtypeStruct(latents.shape, F32),
        jax.ShapeDtypeStruct(pixels.shape, F32),
        jax.ShapeDtypeStruct((8, width), F32),
    ]
    outs += [jax.ShapeDtypeStruct(s.shape, F32) for s in shards]
    outs += [jax.ShapeDtypeStruct((2, 2, 4, 2) + s.shape, s.dtype) for s in shards[:6]]
    outs.append(jax.ShapeDtypeStruct((2, 2, 4, 2, shards[6].shape[0], hidden // 2), BF16))
    outs.append(jax.ShapeDtypeStruct((2, 4, 2) + shards[7].shape, BF16))
    hbm, vmem = pl.BlockSpec(memory_space=pl.ANY), pl.BlockSpec(memory_space=pltpu.VMEM)
    smem = pl.BlockSpec(memory_space=pltpu.SMEM)
    results = pl.pallas_call(
        mega_kernel,
        out_shape=outs,
        in_specs=[hbm, hbm, smem, hbm, hbm] + [vmem] * 8,
        out_specs=[hbm] * 3 + [vmem] + [vmem] * 8 + [hbm] * 8,
        scratch_shapes=scratch + sems,
        compiler_params=pltpu.CompilerParams(collective_id=0, has_side_effects=True, vmem_limit_bytes=63 * 2**20),
    )(latents, pixels, counts, cotangent, gain_block, *shards)
    return results[:4], results[4:12]


def layer_norm(inputs, gain):
    center = inputs - jnp.mean(inputs, axis=-1, keepdims=True)
    spread = jnp.mean(center * center, axis=-1, keepdims=True)
    return center * lax.rsqrt(spread + EPS) * gain


def project(inputs, matrix):
    return jnp.einsum("gld,de->gle", inputs, matrix, preferred_element_type=jnp.float32)


def project_back(grad_rows, matrix):
    return jnp.einsum("gle,de->gld", grad_rows, matrix, preferred_element_type=jnp.float32)


def weight_grad(inputs, grad_rows):
    return jnp.einsum("gld,gle->de", inputs, grad_rows, preferred_element_type=jnp.float32)


def split_heads(tensor):
    return tensor.reshape(tensor.shape[0], tensor.shape[1], HEADS, -1)


def merge_heads(tensor):
    return tensor.reshape(tensor.shape[0], tensor.shape[1], -1)


def scores_of(queries, key_rows, visible):
    scores = jnp.einsum("glhd,gshd->ghls", queries, key_rows, preferred_element_type=jnp.float32)
    scores = scores * queries.shape[-1] ** (-0.5)
    if visible is not None:
        scores = jnp.where(visible[:, None, None, :], scores, -1e30)
    return scores


def attend_forward(queries, key_rows, value_rows, visible):
    scores = scores_of(queries, key_rows, visible)
    largest = jnp.max(scores, axis=-1, keepdims=True)
    exp_scores = jnp.exp(scores - largest)
    totals = jnp.sum(exp_scores, axis=-1, keepdims=True)
    attn_probs = exp_scores / totals
    log_total = largest + jnp.log(totals)
    mixed = jnp.einsum(
        "ghls,gshd->glhd",
        attn_probs.astype(jnp.bfloat16),
        value_rows,
        preferred_element_type=jnp.float32,
    ).astype(jnp.bfloat16)
    return (mixed, log_total)


def attend_backward(queries, key_rows, value_rows, visible, log_total, mixed_grad):
    scale = queries.shape[-1] ** (-0.5)
    attn_probs = jnp.exp(scores_of(queries, key_rows, visible) - log_total)
    probs_grad = jnp.einsum(
        "glhd,gshd->ghls", mixed_grad, value_rows, preferred_element_type=jnp.float32
    )
    value_grad = jnp.einsum(
        "ghls,glhd->gshd",
        attn_probs.astype(jnp.bfloat16),
        mixed_grad,
        preferred_element_type=jnp.float32,
    ).astype(jnp.bfloat16)
    score_grad = attn_probs * (
        probs_grad - jnp.sum(probs_grad * attn_probs, axis=-1, keepdims=True)
    )
    score_grad = score_grad.astype(jnp.bfloat16)
    query_grad = (
        jnp.einsum("ghls,gshd->glhd", score_grad, key_rows, preferred_element_type=jnp.float32)
        * scale
    ).astype(jnp.bfloat16)
    key_grad = (
        jnp.einsum("ghls,glhd->gshd", score_grad, queries, preferred_element_type=jnp.float32)
        * scale
    ).astype(jnp.bfloat16)
    return (query_grad, key_grad, value_grad)


def local_plain(
    latents,
    pixels,
    slot_index,
    counts,
    cotangent,
    gain_q,
    gain_kv,
    w_query,
    w_key,
    w_value,
    w_out,
    gain_self,
    w_qkv,
    w_self_out,
    gain_mlp,
    w_up,
    w_down,
):
    groups = latents.shape[0]
    slots = pixels.shape[1]
    width = latents.shape[2]
    local_slot = slot_index % groups
    chosen = jnp.take(pixels, local_slot, axis=0).astype(jnp.float32)
    visible_count = jnp.take(counts, local_slot, axis=0)
    visible = lax.broadcasted_iota(jnp.int32, (groups, slots), 1) < visible_count[:, None]
    cross_all = (
        lax.all_gather(gain_q, ("dp", "fsdp"), axis=0, tiled=True),
        lax.all_gather(gain_kv, ("dp", "fsdp"), axis=0, tiled=True),
        lax.all_gather(w_query, ("dp", "fsdp"), axis=0, tiled=True),
        lax.all_gather(w_key, ("dp", "fsdp"), axis=0, tiled=True),
        lax.all_gather(w_value, ("dp", "fsdp"), axis=0, tiled=True),
        lax.all_gather(w_out, ("dp", "fsdp"), axis=0, tiled=True),
    )
    normed = layer_norm(latents, cross_all[0].astype(jnp.float32)).astype(jnp.bfloat16)
    pix_normed = layer_norm(chosen, cross_all[1].astype(jnp.float32)).astype(jnp.bfloat16)
    queries = split_heads(project(normed, cross_all[2]).astype(jnp.bfloat16))
    key_rows = split_heads(project(pix_normed, cross_all[3]).astype(jnp.bfloat16))
    value_rows = split_heads(project(pix_normed, cross_all[4]).astype(jnp.bfloat16))
    cross_mixed, cross_total = attend_forward(queries, key_rows, value_rows, visible)
    cross_flat = merge_heads(cross_mixed)
    after_cross = latents + project(cross_flat, cross_all[5])
    self_all = (
        lax.all_gather(gain_self, ("dp", "fsdp"), axis=0, tiled=True),
        lax.all_gather(w_qkv, ("dp", "fsdp"), axis=0, tiled=True),
        lax.all_gather(w_self_out, ("dp", "fsdp"), axis=0, tiled=True),
    )
    normed_self = layer_norm(after_cross, self_all[0].astype(jnp.float32)).astype(jnp.bfloat16)
    packed = project(normed_self, self_all[1]).astype(jnp.bfloat16)
    self_queries = split_heads(packed[..., :width])
    self_keys = split_heads(packed[..., width : 2 * width])
    self_values = split_heads(packed[..., 2 * width :])
    self_mixed, self_total = attend_forward(self_queries, self_keys, self_values, None)
    self_flat = merge_heads(self_mixed)
    after_self = after_cross + project(self_flat, self_all[2])
    mlp_all = (
        lax.all_gather(gain_mlp, ("dp", "fsdp"), axis=0, tiled=True),
        lax.all_gather(w_up, ("dp", "fsdp"), axis=0, tiled=True),
        lax.all_gather(w_down, ("dp", "fsdp"), axis=0, tiled=True),
    )
    normed_mlp = layer_norm(after_self, mlp_all[0].astype(jnp.float32)).astype(jnp.bfloat16)
    hidden = project(normed_mlp, mlp_all[1])
    activated = jax.nn.gelu(hidden).astype(jnp.bfloat16)
    latents_out = after_self + project(activated, mlp_all[2])
    root_mean = jnp.sqrt(jnp.mean(latents_out * latents_out, axis=(1, 2)))
    total_norm = lax.psum(jnp.sum(root_mean), ("dp", "fsdp"))
    norms = root_mean * (groups * lax.axis_size(("dp", "fsdp"))) / total_norm
    mlp_back = (
        lax.all_gather(gain_mlp, ("dp", "fsdp"), axis=0, tiled=True),
        lax.all_gather(w_up, ("dp", "fsdp"), axis=0, tiled=True),
        lax.all_gather(w_down, ("dp", "fsdp"), axis=0, tiled=True),
    )
    out_grad = cotangent.astype(jnp.bfloat16)
    down_grad = weight_grad(activated, out_grad)
    act_grad = project_back(out_grad, mlp_back[2])
    hidden_grad = jax.vjp(jax.nn.gelu, hidden)[1](act_grad)[0].astype(jnp.bfloat16)
    up_grad = weight_grad(normed_mlp, hidden_grad)
    mlp_in_grad = project_back(hidden_grad, mlp_back[1])
    after_self_ln, mlp_gain_grad = jax.vjp(layer_norm, after_self, mlp_back[0].astype(jnp.float32))[
        1
    ](mlp_in_grad)
    after_self_grad = cotangent + after_self_ln
    mlp_grads = (
        lax.psum_scatter(mlp_gain_grad, ("dp", "fsdp"), scatter_dimension=0, tiled=True),
        lax.psum_scatter(up_grad, ("dp", "fsdp"), scatter_dimension=0, tiled=True),
        lax.psum_scatter(down_grad, ("dp", "fsdp"), scatter_dimension=0, tiled=True),
    )
    self_back = (
        lax.all_gather(gain_self, ("dp", "fsdp"), axis=0, tiled=True),
        lax.all_gather(w_qkv, ("dp", "fsdp"), axis=0, tiled=True),
        lax.all_gather(w_self_out, ("dp", "fsdp"), axis=0, tiled=True),
    )
    self_branch = after_self_grad.astype(jnp.bfloat16)
    self_out_grad = weight_grad(self_flat, self_branch)
    self_mixed_grad = split_heads(project_back(self_branch, self_back[2]).astype(jnp.bfloat16))
    self_q_grad, self_k_grad, self_v_grad = attend_backward(
        self_queries, self_keys, self_values, None, self_total, self_mixed_grad
    )
    packed_grad = jnp.concatenate(
        [merge_heads(self_q_grad), merge_heads(self_k_grad), merge_heads(self_v_grad)], axis=-1
    )
    qkv_grad = weight_grad(normed_self, packed_grad)
    self_in_grad = project_back(packed_grad, self_back[1])
    after_cross_ln, self_gain_grad = jax.vjp(
        layer_norm, after_cross, self_back[0].astype(jnp.float32)
    )[1](self_in_grad)
    after_cross_grad = after_self_grad + after_cross_ln
    self_grads = (
        lax.psum_scatter(self_gain_grad, ("dp", "fsdp"), scatter_dimension=0, tiled=True),
        lax.psum_scatter(qkv_grad, ("dp", "fsdp"), scatter_dimension=0, tiled=True),
        lax.psum_scatter(self_out_grad, ("dp", "fsdp"), scatter_dimension=0, tiled=True),
    )
    cross_back = (
        lax.all_gather(gain_q, ("dp", "fsdp"), axis=0, tiled=True),
        lax.all_gather(gain_kv, ("dp", "fsdp"), axis=0, tiled=True),
        lax.all_gather(w_query, ("dp", "fsdp"), axis=0, tiled=True),
        lax.all_gather(w_key, ("dp", "fsdp"), axis=0, tiled=True),
        lax.all_gather(w_value, ("dp", "fsdp"), axis=0, tiled=True),
        lax.all_gather(w_out, ("dp", "fsdp"), axis=0, tiled=True),
    )
    cross_branch = after_cross_grad.astype(jnp.bfloat16)
    out_w_grad = weight_grad(cross_flat, cross_branch)
    cross_mixed_grad = split_heads(project_back(cross_branch, cross_back[5]).astype(jnp.bfloat16))
    query_grad, key_grad, value_grad = attend_backward(
        queries, key_rows, value_rows, visible, cross_total, cross_mixed_grad
    )
    query_flat = merge_heads(query_grad)
    key_flat = merge_heads(key_grad)
    value_flat = merge_heads(value_grad)
    query_w_grad = weight_grad(normed, query_flat)
    key_w_grad = weight_grad(pix_normed, key_flat)
    value_w_grad = weight_grad(pix_normed, value_flat)
    normed_grad = project_back(query_flat, cross_back[2])
    pix_normed_grad = project_back(key_flat, cross_back[3]) + project_back(
        value_flat, cross_back[4]
    )
    latents_ln, query_gain_grad = jax.vjp(layer_norm, latents, cross_back[0].astype(jnp.float32))[
        1
    ](normed_grad)
    latents_grad = after_cross_grad + latents_ln
    chosen_grad, pixel_gain_grad = jax.vjp(layer_norm, chosen, cross_back[1].astype(jnp.float32))[
        1
    ](pix_normed_grad)
    pixels_grad = jnp.zeros(pixels.shape, jnp.float32).at[local_slot].add(chosen_grad)
    cross_grads = (
        lax.psum_scatter(query_gain_grad, ("dp", "fsdp"), scatter_dimension=0, tiled=True),
        lax.psum_scatter(pixel_gain_grad, ("dp", "fsdp"), scatter_dimension=0, tiled=True),
        lax.psum_scatter(query_w_grad, ("dp", "fsdp"), scatter_dimension=0, tiled=True),
        lax.psum_scatter(key_w_grad, ("dp", "fsdp"), scatter_dimension=0, tiled=True),
        lax.psum_scatter(value_w_grad, ("dp", "fsdp"), scatter_dimension=0, tiled=True),
        lax.psum_scatter(out_w_grad, ("dp", "fsdp"), scatter_dimension=0, tiled=True),
    )
    return (
        latents_out,
        latents_grad,
        pixels_grad,
        cross_grads[0],
        cross_grads[1],
        cross_grads[2],
        cross_grads[3],
        cross_grads[4],
        cross_grads[5],
        self_grads[0],
        self_grads[1],
        self_grads[2],
        mlp_grads[0],
        mlp_grads[1],
        mlp_grads[2],
        norms,
    )


def local_fast(
    latents,
    pixels,
    slot_index,
    counts,
    cotangent,
    gain_q,
    gain_kv,
    w_query,
    w_key,
    w_value,
    w_out,
    gain_self,
    w_qkv,
    w_self_out,
    gain_mlp,
    w_up,
    w_down,
):
    gains = jnp.concatenate([gain_q, gain_kv, gain_self, gain_mlp]).astype(jnp.float32)
    gain_block = jnp.pad(gains[None, :], ((0, 7), (0, 0)))
    shards = (w_query, w_key, w_value, w_out, w_qkv, w_self_out, w_up, w_down)
    (latents_out, latents_grad, pixels_grad, small), grads = mega(latents, pixels, counts, cotangent, gain_block, shards)
    latents_out, latents_grad, pixels_grad, *grads = hand_out([latents_out, latents_grad, pixels_grad] + list(grads))
    rows = gain_q.shape[0]
    devices = lax.axis_size(("dp", "fsdp"))
    mine = lax.dynamic_slice(small[:4], (0, lax.axis_index(("dp", "fsdp")) * rows), (4, rows))
    norms = small[5, :1] * devices / small[4, :1]
    g_query, g_key, g_value, g_out, g_qkv, g_self_out, g_up, g_down = grads
    return (
        latents_out,
        latents_grad,
        pixels_grad,
        mine[0],
        mine[1],
        g_query,
        g_key,
        g_value,
        g_out,
        mine[2],
        g_qkv,
        g_self_out,
        mine[3],
        g_up,
        g_down,
        norms,
    )


def hand_out(arrays):
    n = len(arrays)

    def kernel(*refs):
        sems = refs[3 * n]
        fetch = [pltpu.make_async_copy(refs[k], refs[2 * n + k], sems.at[0, k]) for k in range(n)]
        put = [pltpu.make_async_copy(refs[2 * n + k], refs[n + k], sems.at[1, k]) for k in range(n)]
        for c in fetch:
            c.start()
        for k in range(n):
            fetch[k].wait()
            put[k].start()
        for c in put:
            c.wait()

    return pl.pallas_call(
        kernel,
        out_shape=[jax.ShapeDtypeStruct(a.shape, a.dtype) for a in arrays],
        in_specs=[pl.BlockSpec(memory_space=pl.ANY)] * n,
        out_specs=[pl.BlockSpec(memory_space=pl.ANY)] * n,
        scratch_shapes=[pltpu.VMEM(a.shape, a.dtype) for a in arrays] + [DMA((2, n))],
        compiler_params=pltpu.CompilerParams(vmem_limit_bytes=63 * 2**20),
    )(*arrays)


def fits(mesh):
    return mesh.shape["dp"] == 4 and mesh.shape["fsdp"] == 8


def solution(mesh):
    in_specs = (
        P(("dp", "fsdp"), None, None),
        P(("dp", "fsdp"), None, None),
        P(("dp", "fsdp")),
        P(("dp", "fsdp")),
        P(("dp", "fsdp"), None, None),
        P(("dp", "fsdp")),
        P(("dp", "fsdp")),
        P(("dp", "fsdp"), None),
        P(("dp", "fsdp"), None),
        P(("dp", "fsdp"), None),
        P(("dp", "fsdp"), None),
        P(("dp", "fsdp")),
        P(("dp", "fsdp"), None),
        P(("dp", "fsdp"), None),
        P(("dp", "fsdp")),
        P(("dp", "fsdp"), None),
        P(("dp", "fsdp"), None),
    )
    out_specs = (
        P(("dp", "fsdp"), None, None),
        P(("dp", "fsdp"), None, None),
        P(("dp", "fsdp"), None, None),
        P(("dp", "fsdp")),
        P(("dp", "fsdp")),
        P(("dp", "fsdp"), None),
        P(("dp", "fsdp"), None),
        P(("dp", "fsdp"), None),
        P(("dp", "fsdp"), None),
        P(("dp", "fsdp")),
        P(("dp", "fsdp"), None),
        P(("dp", "fsdp"), None),
        P(("dp", "fsdp")),
        P(("dp", "fsdp"), None),
        P(("dp", "fsdp"), None),
        P(("dp", "fsdp")),
    )
    return jax.shard_map(local_fast if fits(mesh) else local_plain, mesh=mesh, in_specs=in_specs, out_specs=out_specs, check_vma=False)
```

```python
import functools

import jax
import jax.numpy as jnp
from jax import lax
from jax.experimental import pallas as pl
from jax.experimental.pallas import tpu as pltpu
from jax.sharding import PartitionSpec as P

MESH = pl.DeviceIdType.MESH
DMA = pltpu.SemaphoreType.DMA
UNIT_COLS = 1024
UNIT_ROWS = 32
RING = 4
PARTIALS = 8
SCATTER_WIDTHS = ((256, 256, 256, 256),) * RING
GATHER_WIDTHS = ((256, 256, 256, 256),)
WHOLE = (0, 0, UNIT_COLS, 0)


class Place:
    def __init__(self):
        dp, f = lax.axis_index("dp"), lax.axis_index("fsdp")
        self.y, self.x, self.z, self.c = dp // 2, dp % 2, f // 2, f % 2
        step = jnp.where(self.z < 2, 1, -1)
        self.is_end = (self.z == 0) | (self.z == 3)
        self.z1 = jnp.where(self.is_end, self.z + step, self.z - step)
        self.z2 = jnp.where(self.is_end, self.z + 2 * step, self.z + step)
        self.z3 = jnp.where(self.is_end, self.z + 3 * step, self.z + 2 * step)

    def dev(self, y=None, x=None, z=None, c=None):
        y = self.y if y is None else y
        x = self.x if x is None else x
        z = self.z if z is None else z
        c = self.c if c is None else c
        return (y * 2 + x, z * 2 + c)

    def barrier(self):
        bar = pltpu.get_barrier_semaphore()
        peers = [
            self.dev(c=1 - self.c),
            self.dev(x=1 - self.x),
            self.dev(y=1 - self.y),
            self.dev(z=self.z1),
            self.dev(z=self.z2),
            self.dev(z=self.z3),
        ]
        for peer in peers:
            pl.semaphore_signal(bar, inc=1, device_id=peer, device_id_type=MESH)
        pl.semaphore_wait(bar, len(peers))


def remote(src, dst, send_sem, recv_sem, dev):
    return pltpu.make_async_remote_copy(
        src_ref=src, dst_ref=dst, send_sem=send_sem, recv_sem=recv_sem, device_id=dev, device_id_type=MESH
    )


def columns(widths, p, base):
    return pl.ds(base + sum(widths[:p]), widths[p])


class Unit:
    def __init__(self, kind, shard, full, row=0, col=0, rows=UNIT_ROWS):
        self.kind, self.shard, self.full, self.row, self.col, self.rows = kind, shard, full, row, col, rows


class Gather:
    STAGES = 7

    def __init__(self, me, units, sems):
        self.me, self.units = me, units
        self.loc, self.sib_s, self.sib_r, self.zs, self.zr, self.xs, self.xr, self.ys, self.yr = sems
        self.widths, plain = [], 0
        for unit in units:
            self.widths.append(GATHER_WIDTHS[plain % len(GATHER_WIDTHS)] if unit.kind == "all" else WHOLE)
            plain += unit.kind == "all"

    @staticmethod
    def sems(n):
        return [DMA((n,))] * 3 + [DMA((n, 4, 4))] * 2 + [DMA((n, 4))] * 4

    def at(self, u, y, x, z, c, p=None):
        unit = self.units[u]
        cols = pl.ds(unit.col, UNIT_COLS) if p is None else columns(self.widths[u], p, unit.col)
        rows = pl.ds(unit.row, unit.rows)
        if unit.kind == "down":
            return unit.full.at[y, z, c, rows, cols]
        return unit.full.at[y, x, z, c, rows, cols]

    def parts(self, u, *which):
        return [p for p in which if self.widths[u][p]]

    def half(self, u, x):
        unit = self.units[u]
        col = pl.multiple_of(2 * unit.col + x * UNIT_COLS, UNIT_COLS)
        return unit.shard.at[pl.ds(unit.row, unit.rows), pl.ds(col, UNIT_COLS)]

    def own(self, u):
        me, unit = self.me, self.units[u]
        if unit.kind == "up":
            src = self.half(u, me.x)
        else:
            src = unit.shard.at[pl.ds(unit.row, unit.rows), pl.ds(unit.col, UNIT_COLS)]
        return pltpu.make_async_copy(src, self.at(u, me.y, me.x, me.z, me.c), self.loc.at[u])

    def zblk(self, u, p, z):
        me, s = self.me, slice(None)
        return self.at(u, me.y if p != 3 else s, me.x if p != 2 else s, z, me.c, p)

    def zcopy(self, u, p, z_to, z_block=None):
        me = self.me
        if z_block is None:
            b = self.zblk(u, p, me.z)
            return remote(b, b, self.zs.at[u, p, z_to], self.zr.at[u, p, me.z], me.dev(z=z_to))
        b = self.zblk(u, p, z_block)
        return remote(b, b, self.zs.at[u, p, me.z], self.zr.at[u, p, z_block], me.dev(z=z_to))

    def zin(self, u, p, z_block):
        b = self.zblk(u, p, z_block)
        return remote(b, b, self.zs.at[u, p, z_block], self.zr.at[u, p, z_block], self.me.dev(z=z_block))

    def z_a(self, u, p):
        me = self.me
        self.zcopy(u, p, me.z1).start()
        self.zcopy(u, p, me.z2).start()

        @pl.when(~me.is_end)
        def _():
            self.zcopy(u, p, me.z3).start()

    def z_b(self, u, p):
        me = self.me

        @pl.when(~me.is_end)
        def _():
            self.zin(u, p, me.z3).wait_recv()
            self.zcopy(u, p, me.z1, me.z3).start()

    def z_wait(self, u, p):
        me = self.me
        self.zin(u, p, me.z1).wait_recv()
        self.zin(u, p, me.z2).wait_recv()

        @pl.when(me.is_end)
        def _():
            self.zin(u, p, me.z3).wait_recv()

    def z_sent(self, u, p):
        me = self.me
        self.zcopy(u, p, me.z1).wait_send()
        self.zcopy(u, p, me.z2).wait_send()

        @pl.when(~me.is_end)
        def _():
            self.zcopy(u, p, me.z3).wait_send()
            self.zcopy(u, p, me.z1, me.z3).wait_send()

    def xcopy(self, u, p, out=True):
        me, s = self.me, slice(None)
        b = self.at(u, me.y if p != 3 and p != 1 else s, me.x if out else 1 - me.x, me.z if p == 2 else s, me.c, p)
        if self.units[u].kind == "up" and out:
            return remote(self.half(u, 1 - me.x), b, self.xs.at[u, p], self.xr.at[u, p], me.dev(x=1 - me.x))
        return remote(b, b, self.xs.at[u, p], self.xr.at[u, p], me.dev(x=1 - me.x))

    def ycopy(self, u, p, out=True):
        me, s = self.me, slice(None)
        b = self.at(u, me.y if out else 1 - me.y, me.x if p != 2 and p != 0 else s, me.z if p == 3 else s, me.c, p)
        return remote(b, b, self.ys.at[u, p], self.yr.at[u, p], me.dev(y=1 - me.y))

    def final(self, u, out=True):
        me, s = self.me, slice(None)
        b = self.at(u, s, s, s, me.c if out else 1 - me.c)
        return remote(b, b, self.sib_s.at[u], self.sib_r.at[u], me.dev(c=1 - me.c))

    def stage(self, s, u):
        kind = self.units[u].kind
        if s == 1:
            for p in self.parts(u, 0, 1):
                self.z_a(u, p)
        elif s == 2:
            for p in self.parts(u, 0, 1):
                self.z_b(u, p)
            for p in self.parts(u, 2, 3):
                if kind != "down":
                    (self.xcopy if p == 2 else self.ycopy)(u, p, False).wait_recv()
                self.z_a(u, p)
        elif s == 3:
            for p in self.parts(u, 0, 1):
                self.z_wait(u, p)
                (self.xcopy if p == 0 else self.ycopy)(u, p).start()
            for p in self.parts(u, 2, 3):
                self.z_b(u, p)
        elif s == 4:
            for p in self.parts(u, 2, 3):
                self.z_wait(u, p)
                (self.ycopy if p == 2 else self.xcopy)(u, p).start()
            for p in self.parts(u, 0, 1):
                (self.xcopy if p == 0 else self.ycopy)(u, p, False).wait_recv()
                (self.ycopy if p == 0 else self.xcopy)(u, p).start()
        elif s == 5:
            for p in self.parts(u, 2, 3, 0, 1):
                (self.ycopy if p in (0, 2) else self.xcopy)(u, p, False).wait_recv()
            self.final(u).start()
        elif s == 6:
            self.final(u, False).wait_recv()

    def early(self, u):
        self.own(u).wait()
        for p in self.parts(u, 2, 3):
            if self.units[u].kind != "down":
                (self.xcopy if p == 2 else self.ycopy)(u, p).start()

    def sent(self, u):
        for p in self.parts(u, 0, 1, 2, 3):
            self.z_sent(u, p)
            if self.units[u].kind != "down":
                self.xcopy(u, p).wait_send()
            self.ycopy(u, p).wait_send()
        self.final(u).wait_send()

    def tick(self, t, wide):
        for u in range(len(self.units)):
            s = t - max(0, u - wide + 1)
            if 0 <= s < self.STAGES:
                self.stage(s, u)

    def ticks(self, wide):
        return self.STAGES + max(0, len(self.units) - wide)


class Scatter:
    STAGES = 5

    def __init__(self, me, units, refs, sems):
        self.me, self.units = me, units
        self.part, self.r1, self.r2, self.rz = refs
        self.s1, self.q1, self.s2, self.q2, self.zs, self.zr = sems

    @staticmethod
    def sems(n):
        return [DMA((n, 4))] * 4 + [DMA((n, 4, 4))] * 2

    def kind(self, u):
        return self.units[u][0]

    def widths(self, u):
        return SCATTER_WIDTHS[u % RING] if self.kind(u) == "all" else WHOLE

    def cols(self, u, p):
        return columns(self.widths(u), p, 0)

    def parts(self, u, *which):
        return [p for p in which if self.widths(u)[p]]

    def slot2(self, u):
        return u % RING if self.kind(u) == "all" else RING + u % 2

    def pt(self, u, p, y, x, z):
        return self.part.at[u % PARTIALS, y, x, z, :, self.cols(u, p)]

    def first(self, u, p):
        me, s = self.me, slice(None)
        dst = self.r1.at[u % PARTIALS, :, :, :, self.cols(u, p)]
        if p in (0, 2):
            return remote(self.pt(u, p, 1 - me.y, s, s), dst, self.s1.at[u, p], self.q1.at[u, p], me.dev(y=1 - me.y))
        return remote(self.pt(u, p, s, 1 - me.x, s), dst, self.s1.at[u, p], self.q1.at[u, p], me.dev(x=1 - me.x))

    def add(self, count, dst, srcs):
        def body(i, carry):
            total = dst(i)[...].astype(jnp.float32)
            for src in srcs:
                total = total + src(i)[...].astype(jnp.float32)
            dst(i)[...] = total.astype(jnp.bfloat16)
            return carry

        if count == 1:
            body(0, 0)
        else:
            lax.fori_loop(0, count, body, 0)

    def first_in(self, u, p):
        me = self.me
        self.first(u, p).wait_recv()
        if p in (0, 2):
            dst = lambda i: self.pt(u, p, me.y, i // 4, i % 4)
        else:
            dst = lambda i: self.pt(u, p, i // 4, me.x, i % 4)
        self.add(8, dst, [lambda i: self.r1.at[u % PARTIALS, i // 4, i % 4, :, self.cols(u, p)]])

    def second(self, u, p):
        me, s = self.me, slice(None)
        cols = self.cols(u, p)
        z = s if p < 2 else me.z
        dst = self.r2.at[self.slot2(u), :, :, cols] if p < 2 else self.r2.at[self.slot2(u), 0, :, cols]
        if p in (0, 2):
            return remote(self.pt(u, p, me.y, 1 - me.x, z), dst, self.s2.at[u, p], self.q2.at[u, p], me.dev(x=1 - me.x))
        return remote(self.pt(u, p, 1 - me.y, me.x, z), dst, self.s2.at[u, p], self.q2.at[u, p], me.dev(y=1 - me.y))

    def second_in(self, u, p):
        me = self.me
        self.second(u, p).wait_recv()
        self.add(
            4,
            lambda i: self.pt(u, p, me.y, me.x, i),
            [lambda i: self.r2.at[self.slot2(u), i, :, self.cols(u, p)]],
        )

    def zblk(self, u, p, z):
        me, s = self.me, slice(None)
        return self.pt(u, p, me.y if p != 3 else s, me.x if p != 2 else s, z)

    def zslot(self, u, p, slot):
        cols = self.cols(u, p)
        return self.rz.at[u % RING, slot, 0, :, cols] if p < 2 else self.rz.at[u % RING, slot, :, :, cols]

    def zcopy(self, u, p, which, block, slot, z_to):
        return remote(
            self.zblk(u, p, block), self.zslot(u, p, slot), self.zs.at[u, p, which], self.zr.at[u, p, slot], self.me.dev(z=z_to)
        )

    def z_ends(self, u, p):
        me = self.me
        return [
            self.zcopy(u, p, 2, me.z3, 3, me.z1),
            self.zcopy(u, p, 1, me.z2, 2, me.z2),
            self.zcopy(u, p, 0, me.z1, 0, me.z1),
        ]

    def z_mids(self, u, p):
        me = self.me
        return [self.zcopy(u, p, 0, me.z1, 0, me.z1), self.zcopy(u, p, 1, me.z2, 1, me.z2)]

    def z_gone(self, u, p):
        return self.zcopy(u, p, 2, self.me.z3, 1, self.me.z3)

    def z_a(self, u, p):
        me = self.me

        @pl.when(me.is_end)
        def _():
            for c in self.z_ends(u, p):
                c.start()

        @pl.when(~me.is_end)
        def _():
            for c in self.z_mids(u, p):
                c.start()

    def zget(self, u, p, slot):
        return self.zcopy(u, p, 0, self.me.z, slot, self.me.z1)

    def z_b(self, u, p):
        me = self.me

        @pl.when(~me.is_end)
        def _():
            self.zget(u, p, 3).wait_recv()
            self.z_add(u, p, me.z3, (3,))
            self.z_gone(u, p).start()

    def z_add(self, u, p, block, slots):
        cols = self.cols(u, p)
        me = self.me
        if p < 2:
            dst, count = (lambda i: self.pt(u, p, me.y, me.x, block)), 1
        elif p == 2:
            dst, count = (lambda i: self.pt(u, p, me.y, i, block)), 2
        else:
            dst, count = (lambda i: self.pt(u, p, i, me.x, block)), 2
        self.add(count, dst, [functools.partial(lambda slot, i: self.rz.at[u % RING, slot, i, :, cols], k) for k in slots])

    def z_in(self, u, p):
        me = self.me
        self.zget(u, p, 0).wait_recv()
        self.zget(u, p, 1).wait_recv()

        @pl.when(~me.is_end)
        def _():
            self.zget(u, p, 2).wait_recv()

    def out(self, u, p):
        _, out, row, col = self.units[u]
        return out.at[pl.ds(row, UNIT_ROWS), columns(self.widths(u), p, col)]

    def finish_z(self, u, p):
        me, cols = self.me, self.cols(u, p)
        self.z_in(u, p)
        f32 = lambda ref: ref[...].astype(jnp.float32)
        total = f32(self.pt(u, p, me.y, me.x, me.z)) + f32(self.rz.at[u % RING, 0, 0, :, cols]) + f32(self.rz.at[u % RING, 1, 0, :, cols])

        @pl.when(me.is_end)
        def _():
            self.out(u, p)[...] = total

        @pl.when(~me.is_end)
        def _():
            self.out(u, p)[...] = total + f32(self.rz.at[u % RING, 2, 0, :, cols])

    def finish_down(self, u):
        me = self.me
        _, out, row, col = self.units[u]
        self.z_in(u, 2)
        f32 = lambda ref: ref[...].astype(jnp.float32)
        for r in range(2):
            dst = out.at[pl.ds(row + r * UNIT_ROWS, UNIT_ROWS), pl.ds(col, UNIT_COLS)]
            dst[...] = f32(self.pt(u, 2, me.y, r, me.z)) + f32(self.rz.at[u % RING, 0, r]) + f32(self.rz.at[u % RING, 1, r])

            @pl.when(~me.is_end)
            def _():
                dst[...] = dst[...] + f32(self.rz.at[u % RING, 2, r])

    def finish_up(self, u):
        me = self.me
        _, out, row, col = self.units[u]
        self.second(u, 2).wait_recv()
        rows = pl.ds(row, UNIT_ROWS)
        for x, ref in ((me.x, self.pt(u, 2, me.y, me.x, me.z)), (1 - me.x, self.r2.at[self.slot2(u), 0])):
            cols = pl.ds(pl.multiple_of(2 * col + x * UNIT_COLS, UNIT_COLS), UNIT_COLS)
            out[rows, cols] = ref[...].astype(jnp.float32)

    def pass_z(self, u, p):
        me = self.me
        self.z_in(u, p)

        @pl.when(me.is_end)
        def _():
            self.z_add(u, p, me.z, (0, 1))

        @pl.when(~me.is_end)
        def _():
            self.z_add(u, p, me.z, (0, 1, 2))

        self.second(u, p).start()

    def finish_last(self, u, p):
        me, cols = self.me, self.cols(u, p)
        self.second(u, p).wait_recv()
        total = self.pt(u, p, me.y, me.x, me.z)[...].astype(jnp.float32) + self.r2.at[self.slot2(u), 0, :, cols][...].astype(jnp.float32)
        self.out(u, p)[...] = total

    def stage(self, s, u):
        kind = self.kind(u)
        if s == 0:
            for p in self.parts(u, 2, 3, 0, 1):
                self.first(u, p).start()
        elif s == 1:
            for p in self.parts(u, 2, 3):
                self.first_in(u, p)
                self.z_a(u, p)
            for p in self.parts(u, 0, 1):
                self.first_in(u, p)
                self.second(u, p).start()
        elif s == 2:
            for p in self.parts(u, 2, 3):
                self.z_b(u, p)
            for p in self.parts(u, 0, 1):
                self.second_in(u, p)
                self.z_a(u, p)
        elif s == 3:
            if kind == "down":
                self.finish_down(u)
            else:
                for p in self.parts(u, 2, 3):
                    self.pass_z(u, p)
            for p in self.parts(u, 0, 1):
                self.z_b(u, p)
        elif s == 4:
            if kind == "up":
                self.finish_up(u)
            elif kind == "all":
                for p in (0, 1):
                    self.finish_z(u, p)
                for p in (2, 3):
                    self.finish_last(u, p)

    def sent(self, u):
        me = self.me
        for p in self.parts(u, 0, 1, 2, 3):
            self.first(u, p).wait_send()
            if self.kind(u) != "down":
                self.second(u, p).wait_send()

            @pl.when(me.is_end)
            def _():
                for c in self.z_ends(u, p):
                    c.wait_send()

            @pl.when(~me.is_end)
            def _():
                for c in self.z_mids(u, p) + [self.z_gone(u, p)]:
                    c.wait_send()


EPS = 1e-05
HEADS = 8
GELU_A = 0.7978845608028654
GELU_B = 0.044715
NT = (((1,), (1,)), ((), ()))
F32, BF16 = jnp.float32, jnp.bfloat16


def matmul(a, b):
    return jnp.dot(a, b, preferred_element_type=F32)


def matmul_nt(a, b):
    return lax.dot_general(a, b, NT, preferred_element_type=F32)


def block(i, size):
    return pl.ds(pl.multiple_of(i * size, size), size)


def for_each(count, body):
    def step(i, carry):
        body(i)
        return carry

    lax.fori_loop(0, count, step, 0)


def normalise(v):
    center = v - jnp.mean(v, axis=-1, keepdims=True)
    inv = lax.rsqrt(jnp.mean(center * center, axis=-1, keepdims=True) + EPS)
    return center * inv, inv


def ln_forward(src, gain, dst):
    def body(i):
        rows = block(i, 32)
        n, _ = normalise(src[rows, :].astype(F32))
        dst[rows, :] = (n * gain[...]).astype(BF16)

    for_each(src.shape[0] // 32, body)


def ln_backward(src, row0, gain, incoming, base, gain_grad):
    def body(i):
        rows = block(i, 32)
        n, inv = normalise(src[pl.ds(pl.multiple_of(row0 + i * 32, 32), 32), :].astype(F32))
        g = incoming[rows, :]
        e = g * gain[...]
        grad = inv * (e - jnp.mean(e, axis=-1, keepdims=True) - n * jnp.mean(e * n, axis=-1, keepdims=True))
        prod = g * n
        gain_grad[...] += prod[0:8] + prod[8:16] + prod[16:24] + prod[24:32]
        if base is None:
            incoming[rows, :] = grad
        else:
            base[rows, :] = base[rows, :] + grad

    for_each(incoming.shape[0] // 32, body)


def attend_forward_heads(first, heads, q, q0, k, k0, v, v0, out, count):
    def body(i):
        h = first + i

        def head(ref, at):
            return ref[:, pl.ds(pl.multiple_of(at + h * 128, 128), 128)]

        s = matmul_nt(head(q, q0), head(k, k0)) * 128 ** (-0.5)
        if count is not None:
            s = jnp.where(lax.broadcasted_iota(jnp.int32, s.shape, 1) < count, s, -1e30)
        e = jnp.exp(s - jnp.max(s, axis=-1, keepdims=True))
        p = (e * (1.0 / jnp.sum(e, axis=-1, keepdims=True))).astype(BF16)
        out[:, block(h, 128)] = matmul(p, head(v, v0)).astype(BF16)

    for_each(heads, body)


def attend_backward_heads(first, heads, q, q0, k, k0, v, v0, mixed_grad, count, dq, dq0, dk, dk0, dv, dv0):
    scale = 128 ** (-0.5)

    def body(i):
        h = first + i

        def head(ref, at):
            return ref[:, pl.ds(pl.multiple_of(at + h * 128, 128), 128)]

        qh, kh, vh, gh = head(q, q0), head(k, k0), head(v, v0), head(mixed_grad, 0)
        s = matmul_nt(kh, qh) * scale
        if count is not None:
            s = jnp.where(lax.broadcasted_iota(jnp.int32, s.shape, 0) < count, s, -1e30)
        e = jnp.exp(s - jnp.max(s, axis=0, keepdims=True))
        p = e * (1.0 / jnp.sum(e, axis=0, keepdims=True))
        dv[:, pl.ds(pl.multiple_of(dv0 + h * 128, 128), 128)] = matmul(p.astype(BF16), gh).astype(BF16)
        dp = matmul_nt(vh, gh)
        ds = (p * (dp - jnp.sum(dp * p, axis=0, keepdims=True))).astype(BF16)
        dk[:, pl.ds(pl.multiple_of(dk0 + h * 128, 128), 128)] = (matmul(ds, qh) * scale).astype(BF16)
        dq[:, pl.ds(pl.multiple_of(dq0 + h * 128, 128), 128)] = (matmul(kh.T, ds).T * scale).astype(BF16)

    for_each(heads, body)


class SmallGather:
    def __init__(self, me, full, send, recv):
        self.me, self.full, self.send, self.recv = me, full, send, recv

    def copy(self, src, k, r, dev):
        return remote(src, src, self.send.at[k], self.recv.at[r], dev)

    def sib(self, out=True):
        me = self.me
        return self.copy(self.full.at[me.y, me.x, me.z, me.c if out else 1 - me.c], 0, 0, me.dev(c=1 - me.c))

    def zc(self, blk, k, r, to):
        me = self.me
        return self.copy(self.full.at[me.y, me.x, blk], k, r, me.dev(z=to))

    def xc(self, out=True):
        me = self.me
        return self.copy(self.full.at[me.y, me.x if out else 1 - me.x], 5, 5, me.dev(x=1 - me.x))

    def yc(self, out=True):
        me = self.me
        return self.copy(self.full.at[me.y if out else 1 - me.y], 6, 6, me.dev(y=1 - me.y))

    def run(self, s):
        me = self.me
        if s == 0:
            self.sib().start()
        elif s == 1:
            self.sib(False).wait_recv()
            self.zc(me.z, 1, 1 + me.z, me.z1).start()
            self.zc(me.z, 2, 1 + me.z, me.z2).start()

            @pl.when(~me.is_end)
            def _():
                self.zc(me.z, 3, 1 + me.z, me.z3).start()

        elif s == 2:

            @pl.when(~me.is_end)
            def _():
                self.zc(me.z3, 4, 1 + me.z3, me.z1).wait_recv()
                self.zc(me.z3, 4, 1 + me.z3, me.z1).start()

        elif s == 3:
            for z in (me.z1, me.z2):
                self.zc(z, 1, 1 + z, me.z1).wait_recv()

            @pl.when(me.is_end)
            def _():
                self.zc(me.z3, 1, 1 + me.z3, me.z1).wait_recv()

            self.xc().start()
        elif s == 4:
            self.xc(False).wait_recv()
            self.yc().start()
        elif s == 5:
            self.yc(False).wait_recv()
            self.sib().wait_send()
            self.zc(me.z, 1, 1 + me.z, me.z1).wait_send()
            self.zc(me.z, 2, 1 + me.z, me.z2).wait_send()

            @pl.when(~me.is_end)
            def _():
                self.zc(me.z, 3, 1 + me.z, me.z3).wait_send()
                self.zc(me.z3, 4, 1 + me.z3, me.z1).wait_send()

            self.xc().wait_send()
            self.yc().wait_send()


class SmallSum:
    def __init__(self, me, acc, got, send, recv):
        z_near = jnp.where(me.is_end, me.z1, me.z1)
        z_far = jnp.where(me.is_end, me.z2, me.z3)
        self.devs = [me.dev(c=1 - me.c), me.dev(x=1 - me.x), me.dev(y=1 - me.y), me.dev(z=z_near), me.dev(z=z_far)]
        self.acc, self.got, self.send, self.recv = acc, got, send, recv

    def copy(self, k):
        return remote(self.acc, self.got.at[k], self.send.at[k], self.recv.at[k], self.devs[k])

    def start(self, k):
        self.copy(k).start()

    def finish(self, k):
        c = self.copy(k)
        c.wait_send()
        c.wait_recv()
        self.acc[...] += self.got[k]


def mega_kernel(*refs):
    it = iter(refs)
    take = lambda n: [next(it) for _ in range(n)]
    latents, pixels, counts, cotangent, gain_block = take(5)
    shards = take(8)
    latents_out, latents_grad, pixels_grad, small_out = take(4)
    grads_out = take(8)
    fulls = take(8)
    (
        w_buf, wd_buf, part, r1, r2, rz,
        xt_normed, xt_pix, xt_mixed, xt_nself, xt_smixed, xt_nmlp, xt_act, st_a, st_b,
        g_out, g_out_in, hid, hid_in, g_branch, g_branch_in, act, packed_in,
        dq, dq_in, big, dk_in, dv, dv_in,
        queries, keys, values, packed, after_cross, after_self, resid, pix, tmp, acc,
        gain_full, gain_vec, gain_acc, small, small_got,
    ) = take(44)
    gather_sems, scatter_sems = take(9), take(6)
    w_sem, wd_sem, in_sem, out_sem, sg_s, sg_r, ss_s, ss_r, xl, xs, xr, gs, gr, across_s, across_r = take(15)
    me = Place()

    plain = lambda i, k: Unit("all", shards[i], fulls[i], 0, k * UNIT_COLS)
    up_unit = lambda k: Unit("up", shards[6], fulls[6], 0, k * UNIT_COLS)
    down_unit = lambda k: Unit("down", shards[7], fulls[7], 2 * k * UNIT_ROWS, 0, 2 * UNIT_ROWS)
    order = ["key", "value", "query", "out", "qkv0", "qkv1", "qkv2", "self", "up0", "up1", "down0", "down1"]
    made = {"query": plain(0, 0), "key": plain(1, 0), "value": plain(2, 0), "out": plain(3, 0), "self": plain(5, 0)}
    made.update({f"qkv{k}": plain(4, k) for k in range(3)})
    made.update({f"up{k}": up_unit(k) for k in range(2)})
    made.update({f"down{k}": down_unit(k) for k in range(2)})
    gather = Gather(me, [made[name] for name in order], gather_sems)
    scatter_units = [("down", grads_out[7], 2 * k * UNIT_ROWS, 0) for k in range(2)]
    scatter_units += [("up", grads_out[6], 0, k * UNIT_COLS) for k in range(2)]
    scatter_units += [("all", grads_out[5], 0, 0)] + [("all", grads_out[4], 0, k * UNIT_COLS) for k in range(3)]
    scatter_units += [("all", grads_out[i], 0, 0) for i in (3, 2, 1, 0)]
    scatter = Scatter(me, scatter_units, (part, r1, r2, rz), scatter_sems)
    pushed = [0]
    tick = [0]

    clock = [0.0]
    settled = [-1]
    ready = []

    def tick_ready(t):
        return 17 + 3.7 * min(t, 6) + 8.4 * min(max(0, t - 6), 8) + 11.5 * max(0, t - 14)

    def settle_ready(k):
        return ready[k] if k < len(ready) else ready[-1] + 4.0 * (k - len(ready) + 1)

    def next_tick():
        clock[0] = max(clock[0], tick_ready(tick[0])) + 0.5
        gather.tick(tick[0], 1)
        tick[0] += 1

    def next_settle():
        settled[0] += 1
        last = settled[0]
        clock[0] = max(clock[0], settle_ready(last)) + 1.0
        for s in range(Scatter.STAGES - 1, 0, -1):
            if 0 <= last - s < len(scatter_units):
                scatter.stage(s, last - s)

    def spend(us):
        clock[0] += us
        while True:
            k = settled[0] + 1
            if tick[0] < gather.ticks(1) and tick_ready(tick[0]) <= clock[0]:
                next_tick()
            elif pushed[0] and k <= pushed[0] and k < len(scatter_units) + 4 and settle_ready(k) <= clock[0]:
                next_settle()
            else:
                break

    def arrived(name):
        u = order.index(name)
        while tick[0] < gather.ticks(1) and tick[0] <= u + Gather.STAGES - 1:
            next_tick()

    def gather_to(t):
        while tick[0] <= t:
            next_tick()

    def settle_to(last):
        while settled[0] < last:
            next_settle()

    def load(k, src, dst):
        return pltpu.make_async_copy(src, dst, in_sem.at[k])

    def across(k, src, dst):
        return remote(src, dst, across_s.at[k], across_r.at[k], me.dev(x=1 - me.x))

    mine, theirs = pl.ds(0, 256), pl.ds(256, 256)
    loads = [load(0, latents.at[0], after_self), load(1, pixels.at[0], pix), load(2, cotangent.at[0], resid)]
    own_gain = load(3, gain_block, gain_full.at[me.y, me.x, me.z, me.c])
    own_gain.start()
    loads[2].start()
    for u in range(len(gather.units)):
        gather.own(u).start()
    loads[0].start()
    loads[1].start()
    loads[2].wait()
    for_each(8, lambda i: g_out.__setitem__((block(i, 32), slice(None)), resid[block(i, 32), :].astype(BF16)))
    own_gain.wait()
    gains = SmallGather(me, gain_full, sg_s, sg_r)
    me.barrier()
    gains.run(0)
    gather.early(0)
    gather_to(1)
    for u in range(1, len(gather.units)):
        gather.early(u)
    gains.run(1)
    for s in range(2, 6):
        gather_to(s)
        gains.run(s)
    table = jnp.sum(gain_full[...].reshape(32, 8, 128), axis=1).astype(BF16)
    width = latents.shape[2]
    lane = lax.broadcasted_iota(jnp.int32, (128, width), 1)
    place = lax.broadcasted_iota(jnp.int32, (128, width), 0)
    owner = lax.broadcasted_iota(jnp.int32, (32, width), 0) == (lax.broadcasted_iota(jnp.int32, (32, width), 1) >> 5)
    for g in range(4):
        pick = jnp.where(place == (lane & 31) + 32 * g, 1.0, 0.0).astype(BF16)
        spread = jnp.where(owner, matmul(table, pick), 0.0)
        gain_vec[g : g + 1, :] = jnp.sum(spread, axis=0, keepdims=True)
    gain = [gain_vec.at[g : g + 1, :] for g in range(4)]
    for g in range(4):
        gain_acc[g] = jnp.zeros_like(gain_acc[g])

    staged = [None, None]

    def hand_over(k, stage, mine, slot, own_dst, far_dst):
        a = pltpu.make_async_copy(mine, own_dst, xl.at[k])
        b = remote(stage, far_dst, xs.at[k], xr.at[k], me.dev(c=1 - me.c))
        a.start()
        b.start()
        staged[slot] = (a, b)

    def clear(slot):
        if staged[slot] is not None:
            a, b = staged[slot]
            a.wait()
            b.wait_send()
            staged[slot] = None

    turn = [0]

    def transpose_out(k, x, row0, xt, k_rows):
        slot = turn[0] % 2
        turn[0] += 1
        clear(slot)

        def body(j):
            piece = x[pl.ds(row0, 256), block(j, 256)].T
            st_b[slot, j // 2, j % 2] = piece.reshape(4, 2, 32, 256)

        for_each(4, body)
        hand_over(
            k,
            st_b.at[slot, :, :, :, 1 - me.c],
            st_b.at[slot, :, :, :, me.c],
            slot,
            xt.at[:, :, :, :, pl.ds(row0, 256)],
            xt.at[:, :, :, :, pl.ds(k_rows + row0, 256)],
        )

    def xt_wait(k, xt, row0, k_rows):
        remote(
            st_b.at[0, :, :, :, 0],
            xt.at[:, :, :, :, pl.ds(k_rows + row0, 256)],
            xs.at[k],
            xr.at[k],
            me.dev(c=1 - me.c),
        ).wait_recv()

    def swap(k, src, dst):
        return remote(src, dst, gs.at[k], gr.at[k], me.dev(c=1 - me.c))

    w_turn = [0]

    def w_start(full, col):
        slot = w_turn[0] % 2
        w_turn[0] += 1
        c = pltpu.make_async_copy(full.at[:, :, :, :, :, pl.ds(col, UNIT_COLS)], w_buf.at[slot], w_sem.at[slot])
        c.start()
        return slot, c

    def w_fetch(full, col):
        slot, c = w_start(full, col)
        c.wait()
        return slot

    def w_cols(slot, j):
        return w_buf[slot, :, :, :, :, :, block(j, 256)].reshape(width, 256)

    def w_rows(slot, j):
        return w_buf[slot, j // 2, j % 2].reshape(256, UNIT_COLS)

    def project(x, slot, out):
        for_each(4, lambda j: out(j, matmul(x[...], w_cols(slot, j))))

    def store(dst, col0=0):
        def put(j, tile):
            dst[:, pl.ds(pl.multiple_of(col0 + j * 256, 256), 256)] = tile.astype(dst.dtype)

        return put

    def back(g, col0, slot, dst, first):
        def body(j):
            tile = matmul_nt(g[:, pl.ds(col0, UNIT_COLS)], w_rows(slot, j))
            cols = block(j, 256)
            if first:
                dst[:, cols] = tile.astype(dst.dtype)
            else:
                dst[:, cols] = dst[:, cols] + tile

        for_each(4, body)

    def partial_sums(us, body):
        u = pushed[0]
        settle_to(u - 3)
        if u >= PARTIALS:
            scatter.sent(u - PARTIALS)
        body(u % PARTIALS)
        scatter.stage(0, u)
        pushed[0] += 1
        clock[0] += us
        lag, gap = (14, 9) if scatter.kind(u) == "all" else (20, 11.5)
        ready.append(max(clock[0] + lag, (ready[-1] if ready else 0) + gap))
        spend(0)

    def weight_grad(xt_at, rows, own, far, col0):
        def fill(slot):
            def body(j):
                cols = pl.ds(pl.multiple_of(col0 + j * 256, 256), 256)
                total = matmul(xt_at(0), own[:, cols]) + matmul(xt_at(rows), far[:, cols])
                part[slot, :, :, :, :, block(j, 256)] = total.astype(BF16).reshape(2, 2, 4, UNIT_ROWS, 256)

            for_each(4, body)

        partial_sums(1.7 if rows > 256 else 1.2, fill)

    def xt_of(xt, rows):
        return lambda at: xt[:, :, :, :, pl.ds(at, rows)].reshape(512, rows)

    loads[0].wait()
    loads[1].wait()
    ln_forward(after_self, gain[0], tmp)
    transpose_out(0, tmp, 0, xt_normed, 256)
    spend(2)
    ln_forward(pix, gain[1], big)
    transpose_out(1, big, 0, xt_pix, 512)
    spend(3.3)
    transpose_out(2, big, 256, xt_pix, 512)
    count = counts[0]
    arrived("key")
    project(big, w_fetch(fulls[1], 0), store(keys))
    spend(3.3)
    arrived("value")
    project(big, w_fetch(fulls[2], 0), store(values))
    spend(3.3)
    arrived("query")
    project(tmp, w_fetch(fulls[0], 0), store(queries))
    spend(2.7)
    for half in range(2):
        attend_forward_heads(4 * half, 4, queries, 0, keys, 0, values, 0, tmp, count)
        spend(2.3)
    arrived("out")
    transpose_out(3, tmp, 0, xt_mixed, 256)

    def add_to(dst, src):
        def put(j, tile):
            dst[:, block(j, 256)] = src[:, block(j, 256)] + tile

        return put

    project(tmp, w_fetch(fulls[3], 0), add_to(after_cross, after_self))
    spend(3)

    ln_forward(after_cross, gain[2], tmp)
    transpose_out(4, tmp, 0, xt_nself, 256)
    spend(1.8)
    for k in range(3):
        arrived(f"qkv{k}")
        project(tmp, w_fetch(fulls[4], k * UNIT_COLS), store(packed, k * UNIT_COLS))
        spend(2.7)
    for half in range(2):
        attend_forward_heads(4 * half, 4, packed, 0, packed, UNIT_COLS, packed, 2 * UNIT_COLS, tmp, None)
        spend(2.2)
    arrived("self")
    transpose_out(5, tmp, 0, xt_smixed, 256)
    project(tmp, w_fetch(fulls[5], 0), add_to(after_self, after_cross))
    spend(3)

    ln_forward(after_self, gain[3], big.at[mine])
    across(1, big.at[mine], big.at[theirs]).start()
    across(0, g_out.at[mine], g_out.at[theirs]).start()
    transpose_out(6, big, 0, xt_nmlp, 512)
    spend(1.8)

    def up_rows(slot, k, rows):
        def up(j):
            x = matmul(big[rows, :], w_cols(slot, j))
            t = jnp.tanh(GELU_A * (x + GELU_B * (x * x * x)))
            half = 0.5 * (1.0 + t)
            cols = pl.ds(pl.multiple_of(k * UNIT_COLS + j * 256, 256), 256)
            act[rows, cols] = (x * half).astype(BF16)
            slope = half + (0.5 * GELU_A) * x * (1.0 - t * t) * (1.0 + (3 * GELU_B) * (x * x))
            hid[rows, cols] = slope.astype(BF16)

        for_each(4, up)

    a_staged = [None, None]
    act_copies = []

    def act_out(k, row0):
        n = len(act_copies)
        slot = n % 2
        if n >= 2:
            act_copies[n - 2][0].wait()
            act_copies[n - 2][1].wait_send()

        def body(m):
            st_a[slot, m // 2, m % 2] = act[pl.ds(row0, 256), pl.ds(pl.multiple_of(k * UNIT_COLS + m * 128, 128), 128)].T

        for_each(8, body)
        a = pltpu.make_async_copy(st_a.at[slot, :, me.c], xt_act.at[k, :, :, pl.ds(row0, 256)], xl.at[8 + n])
        b = remote(
            st_a.at[slot, :, 1 - me.c],
            xt_act.at[k, :, :, pl.ds(512 + row0, 256)],
            xs.at[8 + n],
            xr.at[8 + n],
            me.dev(c=1 - me.c),
        )
        a.start()
        b.start()
        act_copies.append((a, b))

    up_slots = []
    for k in range(2):
        arrived(f"up{k}")
        up_slots.append(w_fetch(fulls[6], k * UNIT_COLS))
        up_rows(up_slots[k], k, mine)
        spend(2.8)
        act_out(k, 0)
        spend(0.5)
    across(1, big.at[mine], big.at[theirs]).wait_recv()
    for k in range(2):
        up_rows(up_slots[k], k, theirs)
        spend(1.3)
        act_out(k, 256)
        spend(0.5)
    across(0, g_out.at[mine], g_out.at[theirs]).wait_recv()
    swap(0, g_out, g_out_in).start()
    transpose_out(7, big, 256, xt_nmlp, 512)
    for a, b in act_copies[2:]:
        a.wait()
        b.wait_send()
    for _, b in act_copies:
        b.wait_recv()
    for slot in range(2):
        clear(slot)
    spend(2)

    swap(0, g_out, g_out_in).wait_recv()

    def down_grad(k):
        def fill(slot):
            def body(i):
                r, cols = i // 4, block(i % 4, 256)
                rows = pl.ds(pl.multiple_of((2 * k + r) * UNIT_ROWS, UNIT_ROWS), UNIT_ROWS)
                near = xt_act[:, :, rows, pl.ds(0, 512)].reshape(256, 512)
                far = xt_act[:, :, rows, pl.ds(512, 512)].reshape(256, 512)
                total = matmul(near, g_out[:, cols]) + matmul(far, g_out_in[:, cols])
                part[slot, :, r, :, :, cols] = total.astype(BF16).reshape(2, 4, UNIT_ROWS, 256)

            for_each(8, body)

        partial_sums(2, fill)

    down_grad(0)
    arrived("down1")

    wd_turn = [0]

    def wd_start(q):
        slot = wd_turn[0] % 2
        wd_turn[0] += 1
        c = pltpu.make_async_copy(fulls[7].at[q], wd_buf.at[slot], wd_sem.at[slot])
        c.start()
        return slot, c

    wd = [wd_start(0), wd_start(1)]
    for q in range(2):
        slot, c = wd[q]
        c.wait()

        def hidden_back(j):
            w = wd_buf[slot, j].reshape(256, width)
            tile = matmul_nt(g_out[...], w)
            cols = pl.ds(pl.multiple_of(q * UNIT_COLS + j * 256, 256), 256)
            hid[:, cols] = (hid[:, cols].astype(F32) * tile).astype(BF16)

        for_each(4, hidden_back)
        cols = pl.ds(q * UNIT_COLS, UNIT_COLS)
        swap(1 + q, hid.at[:, cols], hid_in.at[:, cols]).start()
        spend(2)
    for k in range(2):
        back(hid.at[theirs], k * UNIT_COLS, up_slots[k], acc.at[0], k == 0)
        spend(1.3)
    across(1, big.at[mine], big.at[theirs]).wait_send()
    for_each(8, lambda i: big.__setitem__((block(i, 32), slice(None)), acc[0, block(i, 32), :].astype(BF16)))
    across(2, big.at[mine], tmp).start()
    down_grad(1)
    for k in range(2):
        back(hid.at[mine], k * UNIT_COLS, up_slots[k], acc.at[1], k == 0)
        spend(1.3)
    xt_wait(6, xt_nmlp, 0, 512)
    xt_wait(7, xt_nmlp, 256, 512)
    for k in range(2):
        cols = pl.ds(k * UNIT_COLS, UNIT_COLS)
        swap(1 + k, hid.at[:, cols], hid_in.at[:, cols]).wait_recv()
        weight_grad(xt_of(xt_nmlp, 512), 512, hid, hid_in, k * UNIT_COLS)
    across(2, big.at[mine], tmp).wait_recv()

    def add_theirs(i):
        rows = block(i, 32)
        acc[1, rows, :] = acc[1, rows, :] + tmp[rows, :].astype(F32)

    for_each(8, add_theirs)
    so_slot, c_so = w_start(fulls[5], 0)
    ln_backward(after_self, 0, gain[3], acc.at[1], resid, gain_acc.at[3])
    spend(2.3)

    def round_rows(dst):
        for_each(8, lambda i: dst.__setitem__((block(i, 32), slice(None)), resid[block(i, 32), :].astype(BF16)))

    round_rows(g_branch)
    swap(3, g_branch, g_branch_in).start()
    c_so.wait()
    qkv_w = w_start(fulls[4], 0)
    back(g_branch, 0, so_slot, tmp, True)
    spend(1.8)
    swap(3, g_branch, g_branch_in).wait_recv()
    xt_wait(5, xt_smixed, 0, 256)
    weight_grad(xt_of(xt_smixed, 256), 256, g_branch, g_branch_in, 0)
    for q in range(2):
        cols = pl.ds(q * UNIT_COLS, UNIT_COLS)
        swap(1 + q, hid.at[:, cols], hid_in.at[:, cols]).wait_send()
    corner = [hid.at[mine, pl.ds(0, UNIT_COLS)], hid.at[mine, pl.ds(UNIT_COLS, UNIT_COLS)], hid.at[theirs, pl.ds(0, UNIT_COLS)]]
    for half in range(2):
        attend_backward_heads(
            4 * half, 4, packed, 0, packed, UNIT_COLS, packed, 2 * UNIT_COLS, tmp, None,
            corner[0], 0, corner[1], 0, corner[2], 0,
        )
        spend(3.4)
    packed_swaps = [swap(4 + k, corner[k], packed_in.at[k]) for k in range(3)]
    for c in packed_swaps:
        c.start()
    for k in range(3):
        slot, c = qkv_w
        c.wait()
        if k < 2:
            qkv_w = w_start(fulls[4], (k + 1) * UNIT_COLS)
        back(corner[k], 0, slot, acc.at[0], k == 0)
        spend(1.3)
        packed_swaps[k].wait_recv()
        if k == 0:
            xt_wait(4, xt_nself, 0, 256)
        weight_grad(xt_of(xt_nself, 256), 256, corner[k], packed_in.at[k], 0)
    wo_slot, c_wo = w_start(fulls[3], 0)
    ln_backward(after_cross, 0, gain[2], acc.at[0], resid, gain_acc.at[2])
    spend(2.3)

    swap(3, g_branch, g_branch_in).wait_send()
    round_rows(g_branch)
    swap(7, g_branch, g_branch_in).start()
    c_wo.wait()
    back(g_branch, 0, wo_slot, tmp, True)
    spend(1.8)
    swap(7, g_branch, g_branch_in).wait_recv()
    xt_wait(3, xt_mixed, 0, 256)
    weight_grad(xt_of(xt_mixed, 256), 256, g_branch, g_branch_in, 0)

    across(2, big.at[mine], tmp).wait_send()
    for half in range(2):
        attend_backward_heads(4 * half, 4, queries, 0, keys, 0, values, 0, tmp, count, dq, 0, big, 0, dv, 0)
        spend(3.2)
    given = [swap(8, dv, dv_in), swap(9, big, dk_in), swap(10, dq, dq_in)]
    for c in given:
        c.start()
    w_v = w_start(fulls[2], 0)
    w_k = w_start(fulls[1], 0)
    xt_wait(1, xt_pix, 0, 512)
    xt_wait(2, xt_pix, 256, 512)
    given[0].wait_recv()
    weight_grad(xt_of(xt_pix, 512), 512, dv, dv_in, 0)
    given[1].wait_recv()
    weight_grad(xt_of(xt_pix, 512), 512, big, dk_in, 0)
    xt_wait(0, xt_normed, 0, 256)
    given[2].wait_recv()
    weight_grad(xt_of(xt_normed, 256), 256, dq, dq_in, 0)
    def down(rows, slot, q, dst, base):
        def body(j):
            w = wd_buf[slot, :, :, :, block(j, 256)].reshape(UNIT_COLS, 256)
            tile = matmul(act[rows, pl.ds(q * UNIT_COLS, UNIT_COLS)], w)
            cols = block(j, 256)
            if base is None:
                dst[:, cols] = tile
            else:
                dst[:, cols] = base[:, cols] + tile

        for_each(4, body)
        spend(1.3)

    outer = hid.at[theirs, pl.ds(UNIT_COLS, UNIT_COLS)]
    down(theirs, wd[0][0], 0, after_cross, None)
    down(theirs, wd[1][0], 1, after_cross, after_cross)
    for_each(8, lambda i: tmp.__setitem__((block(i, 32), slice(None)), after_cross[block(i, 32), :].astype(BF16)))
    across(3, tmp, outer).start()
    w_v[1].wait()
    for r in range(2):
        back(dv.at[pl.ds(256 * r, 256)], 0, w_v[0], acc.at[r], True)
        spend(1.3)
    w_q = w_start(fulls[0], 0)
    w_k[1].wait()
    pix_copies = []
    for r in range(2):
        back(big.at[pl.ds(256 * r, 256)], 0, w_k[0], acc.at[r], False)
        spend(1.3)
        ln_backward(pix, 256 * r, gain[1], acc.at[r], None, gain_acc.at[1])
        c = pltpu.make_async_copy(acc.at[r], pixels_grad.at[0, pl.ds(256 * r, 256)], out_sem.at[2 + r])
        c.start()
        pix_copies.append(c)
        spend(2.3)
    down(mine, wd[0][0], 0, after_cross, after_self)
    down(mine, wd[1][0], 1, after_cross, after_cross)
    again = load(0, latents.at[0], after_self)
    again.start()
    across(3, tmp, outer).wait_recv()
    small[...] = jnp.zeros_like(small)

    def add_output(i, total):
        rows = block(i, 32)
        v = after_cross[rows, :] + outer[rows, :].astype(F32)
        after_cross[rows, :] = v
        v = v * v
        return total + v[0:8] + v[8:16] + v[16:24] + v[24:32]

    squares = lax.fori_loop(0, 8, add_output, jnp.zeros((8, width), F32))
    out_copy = pltpu.make_async_copy(after_cross, latents_out.at[0], out_sem.at[0])
    out_copy.start()
    mean_square = jnp.sum(jnp.sum(squares, axis=1, keepdims=True), axis=0, keepdims=True) / (latents.shape[1] * width)
    root_mean = jnp.sqrt(mean_square)
    small[4:5, :] = jnp.broadcast_to(root_mean, (1, width))
    spend(1)
    pix_copies[0].wait()
    w_q[1].wait()
    back(dq, 0, w_q[0], acc.at[0], True)
    spend(1.3)
    again.wait()
    ln_backward(after_self, 0, gain[0], acc.at[0], resid, gain_acc.at[0])
    grad_copy = pltpu.make_async_copy(resid, latents_grad.at[0], out_sem.at[1])
    grad_copy.start()
    spend(2.3)
    for g in range(4):
        small[g : g + 1, :] = jnp.sum(gain_acc[g], axis=0, keepdims=True)
    total = SmallSum(me, small, small_got, ss_s, ss_r)
    for k in range(5):
        total.start(k)
        if settled[0] < len(scatter_units) + 3:
            next_settle()
        total.finish(k)
    settle_to(len(scatter_units) + 3)
    small[5:6, :] = jnp.broadcast_to(root_mean, (1, width))
    small_out[...] = small[...]

    for u in range(len(gather.units)):
        gather.sent(u)
    for u in range(len(scatter_units) - PARTIALS, len(scatter_units)):
        scatter.sent(u)
    swap(0, g_out, g_out_in).wait_send()
    across(0, g_out.at[mine], g_out.at[theirs]).wait_send()
    for c in packed_swaps:
        c.wait_send()
    swap(7, g_branch, g_branch_in).wait_send()
    for c in given:
        c.wait_send()
    grad_copy.wait()
    pix_copies[1].wait()
    out_copy.wait()
    across(3, tmp, outer).wait_send()


def mega(latents, pixels, counts, cotangent, gain_block, shards):
    rows, slots, width = latents.shape[1], pixels.shape[1], latents.shape[2]
    hidden = shards[6].shape[1]
    vm = pltpu.VMEM
    xt = lambda k: vm((2, 2, 4, UNIT_ROWS, k), BF16)
    wide = lambda n: vm((rows, n), BF16)
    scratch = [
        vm((2, 2, 2, 4, 2, UNIT_ROWS, UNIT_COLS), BF16),
        vm((2, 4, 2, 128, UNIT_COLS), BF16),
        vm((PARTIALS, 2, 2, 4, UNIT_ROWS, UNIT_COLS), BF16),
        vm((PARTIALS, 2, 4, UNIT_ROWS, UNIT_COLS), BF16),
        vm((RING + 2, 4, UNIT_ROWS, UNIT_COLS), BF16),
        vm((RING, 4, 2, UNIT_ROWS, UNIT_COLS), BF16),
        xt(2 * rows), xt(2 * slots), xt(2 * rows), xt(2 * rows), xt(2 * rows), xt(4 * rows),
        vm((2, 4, 128, 4 * rows), BF16),
        vm((2, 4, 2, 128, rows), BF16),
        vm((2, 2, 2, 4, 2, UNIT_ROWS, 256), BF16),
        vm((2 * rows, width), BF16), vm((2 * rows, width), BF16), vm((2 * rows, hidden // 2), BF16), vm((2 * rows, hidden // 2), BF16),
        wide(width), wide(width), vm((2 * rows, hidden // 2), BF16), vm((3, rows, width), BF16),
        wide(width), wide(width), vm((slots, width), BF16), vm((slots, width), BF16), vm((slots, width), BF16), vm((slots, width), BF16),
        wide(width), vm((slots, width), BF16), vm((slots, width), BF16), wide(3 * width),
        vm((rows, width), F32), vm((rows, width), F32), vm((rows, width), F32), vm((slots, width), BF16), wide(width), vm((2, rows, width), F32),
        vm((2, 2, 4, 2, 8, 128), F32), vm((8, width), F32), vm((4, 8, width), F32), vm((8, width), F32), vm((5, 8, width), F32),
    ]
    sems = Gather.sems(12) + Scatter.sems(12)
    sems += [DMA((2,)), DMA((2,)), DMA((4,)), DMA((4,)), DMA((7,)), DMA((7,)), DMA((5,)), DMA((5,))]
    sems += [DMA((12,))] * 3 + [DMA((11,))] * 2 + [DMA((4,))] * 2
    outs = [
        jax.ShapeDtypeStruct(latents.shape, F32),
        jax.ShapeDtypeStruct(latents.shape, F32),
        jax.ShapeDtypeStruct(pixels.shape, F32),
        jax.ShapeDtypeStruct((8, width), F32),
    ]
    outs += [jax.ShapeDtypeStruct(s.shape, F32) for s in shards]
    outs += [jax.ShapeDtypeStruct((2, 2, 4, 2) + s.shape, s.dtype) for s in shards[:6]]
    outs.append(jax.ShapeDtypeStruct((2, 2, 4, 2, shards[6].shape[0], hidden // 2), BF16))
    outs.append(jax.ShapeDtypeStruct((2, 4, 2) + shards[7].shape, BF16))
    hbm, vmem = pl.BlockSpec(memory_space=pl.ANY), pl.BlockSpec(memory_space=pltpu.VMEM)
    smem = pl.BlockSpec(memory_space=pltpu.SMEM)
    results = pl.pallas_call(
        mega_kernel,
        out_shape=outs,
        in_specs=[hbm, hbm, smem, hbm, hbm] + [vmem] * 8,
        out_specs=[hbm] * 3 + [vmem] + [vmem] * 8 + [hbm] * 8,
        scratch_shapes=scratch + sems,
        compiler_params=pltpu.CompilerParams(collective_id=0, has_side_effects=True, vmem_limit_bytes=63 * 2**20),
    )(latents, pixels, counts, cotangent, gain_block, *shards)
    return results[:4], results[4:12]


def layer_norm(inputs, gain):
    center = inputs - jnp.mean(inputs, axis=-1, keepdims=True)
    spread = jnp.mean(center * center, axis=-1, keepdims=True)
    return center * lax.rsqrt(spread + EPS) * gain


def project(inputs, matrix):
    return jnp.einsum("gld,de->gle", inputs, matrix, preferred_element_type=jnp.float32)


def project_back(grad_rows, matrix):
    return jnp.einsum("gle,de->gld", grad_rows, matrix, preferred_element_type=jnp.float32)


def weight_grad(inputs, grad_rows):
    return jnp.einsum("gld,gle->de", inputs, grad_rows, preferred_element_type=jnp.float32)


def split_heads(tensor):
    return tensor.reshape(tensor.shape[0], tensor.shape[1], HEADS, -1)


def merge_heads(tensor):
    return tensor.reshape(tensor.shape[0], tensor.shape[1], -1)


def scores_of(queries, key_rows, visible):
    scores = jnp.einsum("glhd,gshd->ghls", queries, key_rows, preferred_element_type=jnp.float32)
    scores = scores * queries.shape[-1] ** (-0.5)
    if visible is not None:
        scores = jnp.where(visible[:, None, None, :], scores, -1e30)
    return scores


def attend_forward(queries, key_rows, value_rows, visible):
    scores = scores_of(queries, key_rows, visible)
    largest = jnp.max(scores, axis=-1, keepdims=True)
    exp_scores = jnp.exp(scores - largest)
    totals = jnp.sum(exp_scores, axis=-1, keepdims=True)
    attn_probs = exp_scores / totals
    log_total = largest + jnp.log(totals)
    mixed = jnp.einsum(
        "ghls,gshd->glhd",
        attn_probs.astype(jnp.bfloat16),
        value_rows,
        preferred_element_type=jnp.float32,
    ).astype(jnp.bfloat16)
    return (mixed, log_total)


def attend_backward(queries, key_rows, value_rows, visible, log_total, mixed_grad):
    scale = queries.shape[-1] ** (-0.5)
    attn_probs = jnp.exp(scores_of(queries, key_rows, visible) - log_total)
    probs_grad = jnp.einsum(
        "glhd,gshd->ghls", mixed_grad, value_rows, preferred_element_type=jnp.float32
    )
    value_grad = jnp.einsum(
        "ghls,glhd->gshd",
        attn_probs.astype(jnp.bfloat16),
        mixed_grad,
        preferred_element_type=jnp.float32,
    ).astype(jnp.bfloat16)
    score_grad = attn_probs * (
        probs_grad - jnp.sum(probs_grad * attn_probs, axis=-1, keepdims=True)
    )
    score_grad = score_grad.astype(jnp.bfloat16)
    query_grad = (
        jnp.einsum("ghls,gshd->glhd", score_grad, key_rows, preferred_element_type=jnp.float32)
        * scale
    ).astype(jnp.bfloat16)
    key_grad = (
        jnp.einsum("ghls,glhd->gshd", score_grad, queries, preferred_element_type=jnp.float32)
        * scale
    ).astype(jnp.bfloat16)
    return (query_grad, key_grad, value_grad)


def local_plain(
    latents,
    pixels,
    slot_index,
    counts,
    cotangent,
    gain_q,
    gain_kv,
    w_query,
    w_key,
    w_value,
    w_out,
    gain_self,
    w_qkv,
    w_self_out,
    gain_mlp,
    w_up,
    w_down,
):
    groups = latents.shape[0]
    slots = pixels.shape[1]
    width = latents.shape[2]
    local_slot = slot_index % groups
    chosen = jnp.take(pixels, local_slot, axis=0).astype(jnp.float32)
    visible_count = jnp.take(counts, local_slot, axis=0)
    visible = lax.broadcasted_iota(jnp.int32, (groups, slots), 1) < visible_count[:, None]
    cross_all = (
        lax.all_gather(gain_q, ("dp", "fsdp"), axis=0, tiled=True),
        lax.all_gather(gain_kv, ("dp", "fsdp"), axis=0, tiled=True),
        lax.all_gather(w_query, ("dp", "fsdp"), axis=0, tiled=True),
        lax.all_gather(w_key, ("dp", "fsdp"), axis=0, tiled=True),
        lax.all_gather(w_value, ("dp", "fsdp"), axis=0, tiled=True),
        lax.all_gather(w_out, ("dp", "fsdp"), axis=0, tiled=True),
    )
    normed = layer_norm(latents, cross_all[0].astype(jnp.float32)).astype(jnp.bfloat16)
    pix_normed = layer_norm(chosen, cross_all[1].astype(jnp.float32)).astype(jnp.bfloat16)
    queries = split_heads(project(normed, cross_all[2]).astype(jnp.bfloat16))
    key_rows = split_heads(project(pix_normed, cross_all[3]).astype(jnp.bfloat16))
    value_rows = split_heads(project(pix_normed, cross_all[4]).astype(jnp.bfloat16))
    cross_mixed, cross_total = attend_forward(queries, key_rows, value_rows, visible)
    cross_flat = merge_heads(cross_mixed)
    after_cross = latents + project(cross_flat, cross_all[5])
    self_all = (
        lax.all_gather(gain_self, ("dp", "fsdp"), axis=0, tiled=True),
        lax.all_gather(w_qkv, ("dp", "fsdp"), axis=0, tiled=True),
        lax.all_gather(w_self_out, ("dp", "fsdp"), axis=0, tiled=True),
    )
    normed_self = layer_norm(after_cross, self_all[0].astype(jnp.float32)).astype(jnp.bfloat16)
    packed = project(normed_self, self_all[1]).astype(jnp.bfloat16)
    self_queries = split_heads(packed[..., :width])
    self_keys = split_heads(packed[..., width : 2 * width])
    self_values = split_heads(packed[..., 2 * width :])
    self_mixed, self_total = attend_forward(self_queries, self_keys, self_values, None)
    self_flat = merge_heads(self_mixed)
    after_self = after_cross + project(self_flat, self_all[2])
    mlp_all = (
        lax.all_gather(gain_mlp, ("dp", "fsdp"), axis=0, tiled=True),
        lax.all_gather(w_up, ("dp", "fsdp"), axis=0, tiled=True),
        lax.all_gather(w_down, ("dp", "fsdp"), axis=0, tiled=True),
    )
    normed_mlp = layer_norm(after_self, mlp_all[0].astype(jnp.float32)).astype(jnp.bfloat16)
    hidden = project(normed_mlp, mlp_all[1])
    activated = jax.nn.gelu(hidden).astype(jnp.bfloat16)
    latents_out = after_self + project(activated, mlp_all[2])
    root_mean = jnp.sqrt(jnp.mean(latents_out * latents_out, axis=(1, 2)))
    total_norm = lax.psum(jnp.sum(root_mean), ("dp", "fsdp"))
    norms = root_mean * (groups * lax.axis_size(("dp", "fsdp"))) / total_norm
    mlp_back = (
        lax.all_gather(gain_mlp, ("dp", "fsdp"), axis=0, tiled=True),
        lax.all_gather(w_up, ("dp", "fsdp"), axis=0, tiled=True),
        lax.all_gather(w_down, ("dp", "fsdp"), axis=0, tiled=True),
    )
    out_grad = cotangent.astype(jnp.bfloat16)
    down_grad = weight_grad(activated, out_grad)
    act_grad = project_back(out_grad, mlp_back[2])
    hidden_grad = jax.vjp(jax.nn.gelu, hidden)[1](act_grad)[0].astype(jnp.bfloat16)
    up_grad = weight_grad(normed_mlp, hidden_grad)
    mlp_in_grad = project_back(hidden_grad, mlp_back[1])
    after_self_ln, mlp_gain_grad = jax.vjp(layer_norm, after_self, mlp_back[0].astype(jnp.float32))[
        1
    ](mlp_in_grad)
    after_self_grad = cotangent + after_self_ln
    mlp_grads = (
        lax.psum_scatter(mlp_gain_grad, ("dp", "fsdp"), scatter_dimension=0, tiled=True),
        lax.psum_scatter(up_grad, ("dp", "fsdp"), scatter_dimension=0, tiled=True),
        lax.psum_scatter(down_grad, ("dp", "fsdp"), scatter_dimension=0, tiled=True),
    )
    self_back = (
        lax.all_gather(gain_self, ("dp", "fsdp"), axis=0, tiled=True),
        lax.all_gather(w_qkv, ("dp", "fsdp"), axis=0, tiled=True),
        lax.all_gather(w_self_out, ("dp", "fsdp"), axis=0, tiled=True),
    )
    self_branch = after_self_grad.astype(jnp.bfloat16)
    self_out_grad = weight_grad(self_flat, self_branch)
    self_mixed_grad = split_heads(project_back(self_branch, self_back[2]).astype(jnp.bfloat16))
    self_q_grad, self_k_grad, self_v_grad = attend_backward(
        self_queries, self_keys, self_values, None, self_total, self_mixed_grad
    )
    packed_grad = jnp.concatenate(
        [merge_heads(self_q_grad), merge_heads(self_k_grad), merge_heads(self_v_grad)], axis=-1
    )
    qkv_grad = weight_grad(normed_self, packed_grad)
    self_in_grad = project_back(packed_grad, self_back[1])
    after_cross_ln, self_gain_grad = jax.vjp(
        layer_norm, after_cross, self_back[0].astype(jnp.float32)
    )[1](self_in_grad)
    after_cross_grad = after_self_grad + after_cross_ln
    self_grads = (
        lax.psum_scatter(self_gain_grad, ("dp", "fsdp"), scatter_dimension=0, tiled=True),
        lax.psum_scatter(qkv_grad, ("dp", "fsdp"), scatter_dimension=0, tiled=True),
        lax.psum_scatter(self_out_grad, ("dp", "fsdp"), scatter_dimension=0, tiled=True),
    )
    cross_back = (
        lax.all_gather(gain_q, ("dp", "fsdp"), axis=0, tiled=True),
        lax.all_gather(gain_kv, ("dp", "fsdp"), axis=0, tiled=True),
        lax.all_gather(w_query, ("dp", "fsdp"), axis=0, tiled=True),
        lax.all_gather(w_key, ("dp", "fsdp"), axis=0, tiled=True),
        lax.all_gather(w_value, ("dp", "fsdp"), axis=0, tiled=True),
        lax.all_gather(w_out, ("dp", "fsdp"), axis=0, tiled=True),
    )
    cross_branch = after_cross_grad.astype(jnp.bfloat16)
    out_w_grad = weight_grad(cross_flat, cross_branch)
    cross_mixed_grad = split_heads(project_back(cross_branch, cross_back[5]).astype(jnp.bfloat16))
    query_grad, key_grad, value_grad = attend_backward(
        queries, key_rows, value_rows, visible, cross_total, cross_mixed_grad
    )
    query_flat = merge_heads(query_grad)
    key_flat = merge_heads(key_grad)
    value_flat = merge_heads(value_grad)
    query_w_grad = weight_grad(normed, query_flat)
    key_w_grad = weight_grad(pix_normed, key_flat)
    value_w_grad = weight_grad(pix_normed, value_flat)
    normed_grad = project_back(query_flat, cross_back[2])
    pix_normed_grad = project_back(key_flat, cross_back[3]) + project_back(
        value_flat, cross_back[4]
    )
    latents_ln, query_gain_grad = jax.vjp(layer_norm, latents, cross_back[0].astype(jnp.float32))[
        1
    ](normed_grad)
    latents_grad = after_cross_grad + latents_ln
    chosen_grad, pixel_gain_grad = jax.vjp(layer_norm, chosen, cross_back[1].astype(jnp.float32))[
        1
    ](pix_normed_grad)
    pixels_grad = jnp.zeros(pixels.shape, jnp.float32).at[local_slot].add(chosen_grad)
    cross_grads = (
        lax.psum_scatter(query_gain_grad, ("dp", "fsdp"), scatter_dimension=0, tiled=True),
        lax.psum_scatter(pixel_gain_grad, ("dp", "fsdp"), scatter_dimension=0, tiled=True),
        lax.psum_scatter(query_w_grad, ("dp", "fsdp"), scatter_dimension=0, tiled=True),
        lax.psum_scatter(key_w_grad, ("dp", "fsdp"), scatter_dimension=0, tiled=True),
        lax.psum_scatter(value_w_grad, ("dp", "fsdp"), scatter_dimension=0, tiled=True),
        lax.psum_scatter(out_w_grad, ("dp", "fsdp"), scatter_dimension=0, tiled=True),
    )
    return (
        latents_out,
        latents_grad,
        pixels_grad,
        cross_grads[0],
        cross_grads[1],
        cross_grads[2],
        cross_grads[3],
        cross_grads[4],
        cross_grads[5],
        self_grads[0],
        self_grads[1],
        self_grads[2],
        mlp_grads[0],
        mlp_grads[1],
        mlp_grads[2],
        norms,
    )


def local_fast(
    latents,
    pixels,
    slot_index,
    counts,
    cotangent,
    gain_q,
    gain_kv,
    w_query,
    w_key,
    w_value,
    w_out,
    gain_self,
    w_qkv,
    w_self_out,
    gain_mlp,
    w_up,
    w_down,
):
    gains = jnp.concatenate([gain_q, gain_kv, gain_self, gain_mlp]).astype(jnp.float32)
    gain_block = jnp.pad(gains[None, :], ((0, 7), (0, 0)))
    shards = (w_query, w_key, w_value, w_out, w_qkv, w_self_out, w_up, w_down)
    (latents_out, latents_grad, pixels_grad, small), grads = mega(latents, pixels, counts, cotangent, gain_block, shards)
    latents_out, latents_grad, pixels_grad, *grads = hand_out([latents_out, latents_grad, pixels_grad] + list(grads))
    rows = gain_q.shape[0]
    devices = lax.axis_size(("dp", "fsdp"))
    mine = lax.dynamic_slice(small[:4], (0, lax.axis_index(("dp", "fsdp")) * rows), (4, rows))
    norms = small[5, :1] * devices / small[4, :1]
    g_query, g_key, g_value, g_out, g_qkv, g_self_out, g_up, g_down = grads
    return (
        latents_out,
        latents_grad,
        pixels_grad,
        mine[0],
        mine[1],
        g_query,
        g_key,
        g_value,
        g_out,
        mine[2],
        g_qkv,
        g_self_out,
        mine[3],
        g_up,
        g_down,
        norms,
    )


def hand_out(arrays):
    n = len(arrays)

    def kernel(*refs):
        sems = refs[3 * n]
        fetch = [pltpu.make_async_copy(refs[k], refs[2 * n + k], sems.at[0, k]) for k in range(n)]
        put = [pltpu.make_async_copy(refs[2 * n + k], refs[n + k], sems.at[1, k]) for k in range(n)]
        for c in fetch:
            c.start()
        for k in range(n):
            fetch[k].wait()
            put[k].start()
        for c in put:
            c.wait()

    return pl.pallas_call(
        kernel,
        out_shape=[jax.ShapeDtypeStruct(a.shape, a.dtype) for a in arrays],
        in_specs=[pl.BlockSpec(memory_space=pl.ANY)] * n,
        out_specs=[pl.BlockSpec(memory_space=pl.ANY)] * n,
        scratch_shapes=[pltpu.VMEM(a.shape, a.dtype) for a in arrays] + [DMA((2, n))],
        compiler_params=pltpu.CompilerParams(vmem_limit_bytes=63 * 2**20),
    )(*arrays)


def fits(mesh):
    return mesh.shape["dp"] == 4 and mesh.shape["fsdp"] == 8


def solution(mesh):
    in_specs = (
        P(("dp", "fsdp"), None, None),
        P(("dp", "fsdp"), None, None),
        P(("dp", "fsdp")),
        P(("dp", "fsdp")),
        P(("dp", "fsdp"), None, None),
        P(("dp", "fsdp")),
        P(("dp", "fsdp")),
        P(("dp", "fsdp"), None),
        P(("dp", "fsdp"), None),
        P(("dp", "fsdp"), None),
        P(("dp", "fsdp"), None),
        P(("dp", "fsdp")),
        P(("dp", "fsdp"), None),
        P(("dp", "fsdp"), None),
        P(("dp", "fsdp")),
        P(("dp", "fsdp"), None),
        P(("dp", "fsdp"), None),
    )
    out_specs = (
        P(("dp", "fsdp"), None, None),
        P(("dp", "fsdp"), None, None),
        P(("dp", "fsdp"), None, None),
        P(("dp", "fsdp")),
        P(("dp", "fsdp")),
        P(("dp", "fsdp"), None),
        P(("dp", "fsdp"), None),
        P(("dp", "fsdp"), None),
        P(("dp", "fsdp"), None),
        P(("dp", "fsdp")),
        P(("dp", "fsdp"), None),
        P(("dp", "fsdp"), None),
        P(("dp", "fsdp")),
        P(("dp", "fsdp"), None),
        P(("dp", "fsdp"), None),
        P(("dp", "fsdp")),
    )
    return jax.shard_map(local_fast if fits(mesh) else local_plain, mesh=mesh, in_specs=in_specs, out_specs=out_specs, check_vma=False)
```

```python
import functools

import jax
import jax.numpy as jnp
from jax import lax
from jax.experimental import pallas as pl
from jax.experimental.pallas import tpu as pltpu
from jax.sharding import PartitionSpec as P

MESH = pl.DeviceIdType.MESH
DMA = pltpu.SemaphoreType.DMA
UNIT_COLS = 1024
UNIT_ROWS = 32
RING = 4
PARTIALS = 8
SCATTER_WIDTHS = ((256, 256, 256, 256),) * RING
GATHER_WIDTHS = ((256, 256, 256, 256),)
WHOLE = (0, 0, UNIT_COLS, 0)


class Place:
    def __init__(self):
        dp, f = lax.axis_index("dp"), lax.axis_index("fsdp")
        self.y, self.x, self.z, self.c = dp // 2, dp % 2, f // 2, f % 2
        step = jnp.where(self.z < 2, 1, -1)
        self.is_end = (self.z == 0) | (self.z == 3)
        self.z1 = jnp.where(self.is_end, self.z + step, self.z - step)
        self.z2 = jnp.where(self.is_end, self.z + 2 * step, self.z + step)
        self.z3 = jnp.where(self.is_end, self.z + 3 * step, self.z + 2 * step)

    def dev(self, y=None, x=None, z=None, c=None):
        y = self.y if y is None else y
        x = self.x if x is None else x
        z = self.z if z is None else z
        c = self.c if c is None else c
        return (y * 2 + x, z * 2 + c)

    def barrier(self):
        bar = pltpu.get_barrier_semaphore()
        peers = [
            self.dev(c=1 - self.c),
            self.dev(x=1 - self.x),
            self.dev(y=1 - self.y),
            self.dev(z=self.z1),
            self.dev(z=self.z2),
            self.dev(z=self.z3),
        ]
        for peer in peers:
            pl.semaphore_signal(bar, inc=1, device_id=peer, device_id_type=MESH)
        pl.semaphore_wait(bar, len(peers))


def remote(src, dst, send_sem, recv_sem, dev):
    return pltpu.make_async_remote_copy(
        src_ref=src, dst_ref=dst, send_sem=send_sem, recv_sem=recv_sem, device_id=dev, device_id_type=MESH
    )


def columns(widths, p, base):
    return pl.ds(base + sum(widths[:p]), widths[p])


class Unit:
    def __init__(self, kind, shard, full, row=0, col=0, rows=UNIT_ROWS):
        self.kind, self.shard, self.full, self.row, self.col, self.rows = kind, shard, full, row, col, rows


class Gather:
    STAGES = 7

    def __init__(self, me, units, sems):
        self.me, self.units = me, units
        self.loc, self.sib_s, self.sib_r, self.zs, self.zr, self.xs, self.xr, self.ys, self.yr = sems
        self.widths, plain = [], 0
        for unit in units:
            self.widths.append(GATHER_WIDTHS[plain % len(GATHER_WIDTHS)] if unit.kind == "all" else WHOLE)
            plain += unit.kind == "all"

    @staticmethod
    def sems(n):
        return [DMA((n,))] * 3 + [DMA((n, 4, 4))] * 2 + [DMA((n, 4))] * 4

    def at(self, u, y, x, z, c, p=None):
        unit = self.units[u]
        cols = pl.ds(unit.col, UNIT_COLS) if p is None else columns(self.widths[u], p, unit.col)
        rows = pl.ds(unit.row, unit.rows)
        if unit.kind == "down":
            return unit.full.at[y, z, c, rows, cols]
        return unit.full.at[y, x, z, c, rows, cols]

    def parts(self, u, *which):
        return [p for p in which if self.widths[u][p]]

    def half(self, u, x):
        unit = self.units[u]
        col = pl.multiple_of(2 * unit.col + x * UNIT_COLS, UNIT_COLS)
        return unit.shard.at[pl.ds(unit.row, unit.rows), pl.ds(col, UNIT_COLS)]

    def own(self, u):
        me, unit = self.me, self.units[u]
        if unit.kind == "up":
            src = self.half(u, me.x)
        else:
            src = unit.shard.at[pl.ds(unit.row, unit.rows), pl.ds(unit.col, UNIT_COLS)]
        return pltpu.make_async_copy(src, self.at(u, me.y, me.x, me.z, me.c), self.loc.at[u])

    def zblk(self, u, p, z):
        me, s = self.me, slice(None)
        return self.at(u, me.y if p != 3 else s, me.x if p != 2 else s, z, me.c, p)

    def zcopy(self, u, p, z_to, z_block=None):
        me = self.me
        if z_block is None:
            b = self.zblk(u, p, me.z)
            return remote(b, b, self.zs.at[u, p, z_to], self.zr.at[u, p, me.z], me.dev(z=z_to))
        b = self.zblk(u, p, z_block)
        return remote(b, b, self.zs.at[u, p, me.z], self.zr.at[u, p, z_block], me.dev(z=z_to))

    def zin(self, u, p, z_block):
        b = self.zblk(u, p, z_block)
        return remote(b, b, self.zs.at[u, p, z_block], self.zr.at[u, p, z_block], self.me.dev(z=z_block))

    def z_a(self, u, p):
        me = self.me
        self.zcopy(u, p, me.z1).start()
        self.zcopy(u, p, me.z2).start()

        @pl.when(~me.is_end)
        def _():
            self.zcopy(u, p, me.z3).start()

    def z_b(self, u, p):
        me = self.me

        @pl.when(~me.is_end)
        def _():
            self.zin(u, p, me.z3).wait_recv()
            self.zcopy(u, p, me.z1, me.z3).start()

    def z_wait(self, u, p):
        me = self.me
        self.zin(u, p, me.z1).wait_recv()
        self.zin(u, p, me.z2).wait_recv()

        @pl.when(me.is_end)
        def _():
            self.zin(u, p, me.z3).wait_recv()

    def z_sent(self, u, p):
        me = self.me
        self.zcopy(u, p, me.z1).wait_send()
        self.zcopy(u, p, me.z2).wait_send()

        @pl.when(~me.is_end)
        def _():
            self.zcopy(u, p, me.z3).wait_send()
            self.zcopy(u, p, me.z1, me.z3).wait_send()

    def xcopy(self, u, p, out=True):
        me, s = self.me, slice(None)
        b = self.at(u, me.y if p != 3 and p != 1 else s, me.x if out else 1 - me.x, me.z if p == 2 else s, me.c, p)
        if self.units[u].kind == "up" and out:
            return remote(self.half(u, 1 - me.x), b, self.xs.at[u, p], self.xr.at[u, p], me.dev(x=1 - me.x))
        return remote(b, b, self.xs.at[u, p], self.xr.at[u, p], me.dev(x=1 - me.x))

    def ycopy(self, u, p, out=True):
        me, s = self.me, slice(None)
        b = self.at(u, me.y if out else 1 - me.y, me.x if p != 2 and p != 0 else s, me.z if p == 3 else s, me.c, p)
        return remote(b, b, self.ys.at[u, p], self.yr.at[u, p], me.dev(y=1 - me.y))

    def final(self, u, out=True):
        me, s = self.me, slice(None)
        b = self.at(u, s, s, s, me.c if out else 1 - me.c)
        return remote(b, b, self.sib_s.at[u], self.sib_r.at[u], me.dev(c=1 - me.c))

    def stage(self, s, u):
        kind = self.units[u].kind
        if s == 1:
            for p in self.parts(u, 0, 1):
                self.z_a(u, p)
        elif s == 2:
            for p in self.parts(u, 0, 1):
                self.z_b(u, p)
            for p in self.parts(u, 2, 3):
                if kind != "down":
                    (self.xcopy if p == 2 else self.ycopy)(u, p, False).wait_recv()
                self.z_a(u, p)
        elif s == 3:
            for p in self.parts(u, 0, 1):
                self.z_wait(u, p)
                (self.xcopy if p == 0 else self.ycopy)(u, p).start()
            for p in self.parts(u, 2, 3):
                self.z_b(u, p)
        elif s == 4:
            for p in self.parts(u, 2, 3):
                self.z_wait(u, p)
                (self.ycopy if p == 2 else self.xcopy)(u, p).start()
            for p in self.parts(u, 0, 1):
                (self.xcopy if p == 0 else self.ycopy)(u, p, False).wait_recv()
                (self.ycopy if p == 0 else self.xcopy)(u, p).start()
        elif s == 5:
            for p in self.parts(u, 2, 3, 0, 1):
                (self.ycopy if p in (0, 2) else self.xcopy)(u, p, False).wait_recv()
            self.final(u).start()
        elif s == 6:
            self.final(u, False).wait_recv()

    def early(self, u):
        self.own(u).wait()
        for p in self.parts(u, 2, 3):
            if self.units[u].kind != "down":
                (self.xcopy if p == 2 else self.ycopy)(u, p).start()

    def sent(self, u):
        for p in self.parts(u, 0, 1, 2, 3):
            self.z_sent(u, p)
            if self.units[u].kind != "down":
                self.xcopy(u, p).wait_send()
            self.ycopy(u, p).wait_send()
        self.final(u).wait_send()

    def tick(self, t, wide):
        for u in range(len(self.units)):
            s = t - max(0, u - wide + 1)
            if 0 <= s < self.STAGES:
                self.stage(s, u)

    def ticks(self, wide):
        return self.STAGES + max(0, len(self.units) - wide)


class Scatter:
    STAGES = 5

    def __init__(self, me, units, refs, sems):
        self.me, self.units = me, units
        self.part, self.r1, self.r2, self.rz = refs
        self.s1, self.q1, self.s2, self.q2, self.zs, self.zr = sems

    @staticmethod
    def sems(n):
        return [DMA((n, 4))] * 4 + [DMA((n, 4, 4))] * 2

    def kind(self, u):
        return self.units[u][0]

    def widths(self, u):
        return SCATTER_WIDTHS[u % RING] if self.kind(u) == "all" else WHOLE

    def cols(self, u, p):
        return columns(self.widths(u), p, 0)

    def parts(self, u, *which):
        return [p for p in which if self.widths(u)[p]]

    def slot2(self, u):
        return u % RING if self.kind(u) == "all" else RING + u % 2

    def pt(self, u, p, y, x, z):
        return self.part.at[u % PARTIALS, y, x, z, :, self.cols(u, p)]

    def first(self, u, p):
        me, s = self.me, slice(None)
        dst = self.r1.at[u % PARTIALS, :, :, :, self.cols(u, p)]
        if p in (0, 2):
            return remote(self.pt(u, p, 1 - me.y, s, s), dst, self.s1.at[u, p], self.q1.at[u, p], me.dev(y=1 - me.y))
        return remote(self.pt(u, p, s, 1 - me.x, s), dst, self.s1.at[u, p], self.q1.at[u, p], me.dev(x=1 - me.x))

    def add(self, count, dst, srcs):
        def body(i, carry):
            total = dst(i)[...].astype(jnp.float32)
            for src in srcs:
                total = total + src(i)[...].astype(jnp.float32)
            dst(i)[...] = total.astype(jnp.bfloat16)
            return carry

        if count == 1:
            body(0, 0)
        else:
            lax.fori_loop(0, count, body, 0)

    def first_in(self, u, p):
        me = self.me
        self.first(u, p).wait_recv()
        if p in (0, 2):
            dst = lambda i: self.pt(u, p, me.y, i // 4, i % 4)
        else:
            dst = lambda i: self.pt(u, p, i // 4, me.x, i % 4)
        self.add(8, dst, [lambda i: self.r1.at[u % PARTIALS, i // 4, i % 4, :, self.cols(u, p)]])

    def second(self, u, p):
        me, s = self.me, slice(None)
        cols = self.cols(u, p)
        z = s if p < 2 else me.z
        dst = self.r2.at[self.slot2(u), :, :, cols] if p < 2 else self.r2.at[self.slot2(u), 0, :, cols]
        if p in (0, 2):
            return remote(self.pt(u, p, me.y, 1 - me.x, z), dst, self.s2.at[u, p], self.q2.at[u, p], me.dev(x=1 - me.x))
        return remote(self.pt(u, p, 1 - me.y, me.x, z), dst, self.s2.at[u, p], self.q2.at[u, p], me.dev(y=1 - me.y))

    def second_in(self, u, p):
        me = self.me
        self.second(u, p).wait_recv()
        self.add(
            4,
            lambda i: self.pt(u, p, me.y, me.x, i),
            [lambda i: self.r2.at[self.slot2(u), i, :, self.cols(u, p)]],
        )

    def zblk(self, u, p, z):
        me, s = self.me, slice(None)
        return self.pt(u, p, me.y if p != 3 else s, me.x if p != 2 else s, z)

    def zslot(self, u, p, slot):
        cols = self.cols(u, p)
        return self.rz.at[u % RING, slot, 0, :, cols] if p < 2 else self.rz.at[u % RING, slot, :, :, cols]

    def zcopy(self, u, p, which, block, slot, z_to):
        return remote(
            self.zblk(u, p, block), self.zslot(u, p, slot), self.zs.at[u, p, which], self.zr.at[u, p, slot], self.me.dev(z=z_to)
        )

    def z_ends(self, u, p):
        me = self.me
        return [
            self.zcopy(u, p, 2, me.z3, 3, me.z1),
            self.zcopy(u, p, 1, me.z2, 2, me.z2),
            self.zcopy(u, p, 0, me.z1, 0, me.z1),
        ]

    def z_mids(self, u, p):
        me = self.me
        return [self.zcopy(u, p, 0, me.z1, 0, me.z1), self.zcopy(u, p, 1, me.z2, 1, me.z2)]

    def z_gone(self, u, p):
        return self.zcopy(u, p, 2, self.me.z3, 1, self.me.z3)

    def z_a(self, u, p):
        me = self.me

        @pl.when(me.is_end)
        def _():
            for c in self.z_ends(u, p):
                c.start()

        @pl.when(~me.is_end)
        def _():
            for c in self.z_mids(u, p):
                c.start()

    def zget(self, u, p, slot):
        return self.zcopy(u, p, 0, self.me.z, slot, self.me.z1)

    def z_b(self, u, p):
        me = self.me

        @pl.when(~me.is_end)
        def _():
            self.zget(u, p, 3).wait_recv()
            self.z_add(u, p, me.z3, (3,))
            self.z_gone(u, p).start()

    def z_add(self, u, p, block, slots):
        cols = self.cols(u, p)
        me = self.me
        if p < 2:
            dst, count = (lambda i: self.pt(u, p, me.y, me.x, block)), 1
        elif p == 2:
            dst, count = (lambda i: self.pt(u, p, me.y, i, block)), 2
        else:
            dst, count = (lambda i: self.pt(u, p, i, me.x, block)), 2
        self.add(count, dst, [functools.partial(lambda slot, i: self.rz.at[u % RING, slot, i, :, cols], k) for k in slots])

    def z_in(self, u, p):
        me = self.me
        self.zget(u, p, 0).wait_recv()
        self.zget(u, p, 1).wait_recv()

        @pl.when(~me.is_end)
        def _():
            self.zget(u, p, 2).wait_recv()

    def out(self, u, p):
        _, out, row, col = self.units[u]
        return out.at[pl.ds(row, UNIT_ROWS), columns(self.widths(u), p, col)]

    def finish_z(self, u, p):
        me, cols = self.me, self.cols(u, p)
        self.z_in(u, p)
        f32 = lambda ref: ref[...].astype(jnp.float32)
        total = f32(self.pt(u, p, me.y, me.x, me.z)) + f32(self.rz.at[u % RING, 0, 0, :, cols]) + f32(self.rz.at[u % RING, 1, 0, :, cols])

        @pl.when(me.is_end)
        def _():
            self.out(u, p)[...] = total

        @pl.when(~me.is_end)
        def _():
            self.out(u, p)[...] = total + f32(self.rz.at[u % RING, 2, 0, :, cols])

    def finish_down(self, u):
        me = self.me
        _, out, row, col = self.units[u]
        self.z_in(u, 2)
        f32 = lambda ref: ref[...].astype(jnp.float32)
        for r in range(2):
            dst = out.at[pl.ds(row + r * UNIT_ROWS, UNIT_ROWS), pl.ds(col, UNIT_COLS)]
            dst[...] = f32(self.pt(u, 2, me.y, r, me.z)) + f32(self.rz.at[u % RING, 0, r]) + f32(self.rz.at[u % RING, 1, r])

            @pl.when(~me.is_end)
            def _():
                dst[...] = dst[...] + f32(self.rz.at[u % RING, 2, r])

    def finish_up(self, u):
        me = self.me
        _, out, row, col = self.units[u]
        self.second(u, 2).wait_recv()
        rows = pl.ds(row, UNIT_ROWS)
        for x, ref in ((me.x, self.pt(u, 2, me.y, me.x, me.z)), (1 - me.x, self.r2.at[self.slot2(u), 0])):
            cols = pl.ds(pl.multiple_of(2 * col + x * UNIT_COLS, UNIT_COLS), UNIT_COLS)
            out[rows, cols] = ref[...].astype(jnp.float32)

    def pass_z(self, u, p):
        me = self.me
        self.z_in(u, p)

        @pl.when(me.is_end)
        def _():
            self.z_add(u, p, me.z, (0, 1))

        @pl.when(~me.is_end)
        def _():
            self.z_add(u, p, me.z, (0, 1, 2))

        self.second(u, p).start()

    def finish_last(self, u, p):
        me, cols = self.me, self.cols(u, p)
        self.second(u, p).wait_recv()
        total = self.pt(u, p, me.y, me.x, me.z)[...].astype(jnp.float32) + self.r2.at[self.slot2(u), 0, :, cols][...].astype(jnp.float32)
        self.out(u, p)[...] = total

    def stage(self, s, u):
        kind = self.kind(u)
        if s == 0:
            for p in self.parts(u, 2, 3, 0, 1):
                self.first(u, p).start()
        elif s == 1:
            for p in self.parts(u, 2, 3):
                self.first_in(u, p)
                self.z_a(u, p)
            for p in self.parts(u, 0, 1):
                self.first_in(u, p)
                self.second(u, p).start()
        elif s == 2:
            for p in self.parts(u, 2, 3):
                self.z_b(u, p)
            for p in self.parts(u, 0, 1):
                self.second_in(u, p)
                self.z_a(u, p)
        elif s == 3:
            if kind == "down":
                self.finish_down(u)
            else:
                for p in self.parts(u, 2, 3):
                    self.pass_z(u, p)
            for p in self.parts(u, 0, 1):
                self.z_b(u, p)
        elif s == 4:
            if kind == "up":
                self.finish_up(u)
            elif kind == "all":
                for p in (0, 1):
                    self.finish_z(u, p)
                for p in (2, 3):
                    self.finish_last(u, p)

    def sent(self, u):
        me = self.me
        for p in self.parts(u, 0, 1, 2, 3):
            self.first(u, p).wait_send()
            if self.kind(u) != "down":
                self.second(u, p).wait_send()

            @pl.when(me.is_end)
            def _():
                for c in self.z_ends(u, p):
                    c.wait_send()

            @pl.when(~me.is_end)
            def _():
                for c in self.z_mids(u, p) + [self.z_gone(u, p)]:
                    c.wait_send()


EPS = 1e-05
HEADS = 8
GELU_A = 0.7978845608028654
GELU_B = 0.044715
NT = (((1,), (1,)), ((), ()))
F32, BF16 = jnp.float32, jnp.bfloat16


def matmul(a, b):
    return jnp.dot(a, b, preferred_element_type=F32)


def matmul_nt(a, b):
    return lax.dot_general(a, b, NT, preferred_element_type=F32)


def block(i, size):
    return pl.ds(pl.multiple_of(i * size, size), size)


def for_each(count, body):
    def step(i, carry):
        body(i)
        return carry

    lax.fori_loop(0, count, step, 0)


def normalise(v):
    center = v - jnp.mean(v, axis=-1, keepdims=True)
    inv = lax.rsqrt(jnp.mean(center * center, axis=-1, keepdims=True) + EPS)
    return center * inv, inv


def ln_forward(src, gain, dst):
    def body(i):
        rows = block(i, 32)
        n, _ = normalise(src[rows, :].astype(F32))
        dst[rows, :] = (n * gain[...]).astype(BF16)

    for_each(src.shape[0] // 32, body)


def ln_backward(src, row0, gain, incoming, base, gain_grad):
    def body(i):
        rows = block(i, 32)
        n, inv = normalise(src[pl.ds(pl.multiple_of(row0 + i * 32, 32), 32), :].astype(F32))
        g = incoming[rows, :]
        e = g * gain[...]
        grad = inv * (e - jnp.mean(e, axis=-1, keepdims=True) - n * jnp.mean(e * n, axis=-1, keepdims=True))
        prod = g * n
        gain_grad[...] += prod[0:8] + prod[8:16] + prod[16:24] + prod[24:32]
        if base is None:
            incoming[rows, :] = grad
        else:
            base[rows, :] = base[rows, :] + grad

    for_each(incoming.shape[0] // 32, body)


def attend_forward_heads(first, heads, q, q0, k, k0, v, v0, out, count):
    def body(i):
        h = first + i

        def head(ref, at):
            return ref[:, pl.ds(pl.multiple_of(at + h * 128, 128), 128)]

        s = matmul_nt(head(q, q0), head(k, k0)) * 128 ** (-0.5)
        if count is not None:
            s = jnp.where(lax.broadcasted_iota(jnp.int32, s.shape, 1) < count, s, -1e30)
        e = jnp.exp(s - jnp.max(s, axis=-1, keepdims=True))
        p = (e * (1.0 / jnp.sum(e, axis=-1, keepdims=True))).astype(BF16)
        out[:, block(h, 128)] = matmul(p, head(v, v0)).astype(BF16)

    for_each(heads, body)


def attend_backward_heads(first, heads, q, q0, k, k0, v, v0, mixed_grad, count, dq, dq0, dk, dk0, dv, dv0):
    scale = 128 ** (-0.5)

    def body(i):
        h = first + i

        def head(ref, at):
            return ref[:, pl.ds(pl.multiple_of(at + h * 128, 128), 128)]

        qh, kh, vh, gh = head(q, q0), head(k, k0), head(v, v0), head(mixed_grad, 0)
        s = matmul_nt(kh, qh) * scale
        if count is not None:
            s = jnp.where(lax.broadcasted_iota(jnp.int32, s.shape, 0) < count, s, -1e30)
        e = jnp.exp(s - jnp.max(s, axis=0, keepdims=True))
        p = e * (1.0 / jnp.sum(e, axis=0, keepdims=True))
        dv[:, pl.ds(pl.multiple_of(dv0 + h * 128, 128), 128)] = matmul(p.astype(BF16), gh).astype(BF16)
        dp = matmul_nt(vh, gh)
        ds = (p * (dp - jnp.sum(dp * p, axis=0, keepdims=True))).astype(BF16)
        dk[:, pl.ds(pl.multiple_of(dk0 + h * 128, 128), 128)] = (matmul(ds, qh) * scale).astype(BF16)
        dq[:, pl.ds(pl.multiple_of(dq0 + h * 128, 128), 128)] = (matmul(kh.T, ds).T * scale).astype(BF16)

    for_each(heads, body)


class SmallGather:
    def __init__(self, me, full, send, recv):
        self.me, self.full, self.send, self.recv = me, full, send, recv

    def copy(self, src, k, r, dev):
        return remote(src, src, self.send.at[k], self.recv.at[r], dev)

    def sib(self, out=True):
        me = self.me
        return self.copy(self.full.at[me.y, me.x, me.z, me.c if out else 1 - me.c], 0, 0, me.dev(c=1 - me.c))

    def zc(self, blk, k, r, to):
        me = self.me
        return self.copy(self.full.at[me.y, me.x, blk], k, r, me.dev(z=to))

    def xc(self, out=True):
        me = self.me
        return self.copy(self.full.at[me.y, me.x if out else 1 - me.x], 5, 5, me.dev(x=1 - me.x))

    def yc(self, out=True):
        me = self.me
        return self.copy(self.full.at[me.y if out else 1 - me.y], 6, 6, me.dev(y=1 - me.y))

    def run(self, s):
        me = self.me
        if s == 0:
            self.sib().start()
        elif s == 1:
            self.sib(False).wait_recv()
            self.zc(me.z, 1, 1 + me.z, me.z1).start()
            self.zc(me.z, 2, 1 + me.z, me.z2).start()

            @pl.when(~me.is_end)
            def _():
                self.zc(me.z, 3, 1 + me.z, me.z3).start()

        elif s == 2:

            @pl.when(~me.is_end)
            def _():
                self.zc(me.z3, 4, 1 + me.z3, me.z1).wait_recv()
                self.zc(me.z3, 4, 1 + me.z3, me.z1).start()

        elif s == 3:
            for z in (me.z1, me.z2):
                self.zc(z, 1, 1 + z, me.z1).wait_recv()

            @pl.when(me.is_end)
            def _():
                self.zc(me.z3, 1, 1 + me.z3, me.z1).wait_recv()

            self.xc().start()
        elif s == 4:
            self.xc(False).wait_recv()
            self.yc().start()
        elif s == 5:
            self.yc(False).wait_recv()
            self.sib().wait_send()
            self.zc(me.z, 1, 1 + me.z, me.z1).wait_send()
            self.zc(me.z, 2, 1 + me.z, me.z2).wait_send()

            @pl.when(~me.is_end)
            def _():
                self.zc(me.z, 3, 1 + me.z, me.z3).wait_send()
                self.zc(me.z3, 4, 1 + me.z3, me.z1).wait_send()

            self.xc().wait_send()
            self.yc().wait_send()


class SmallSum:
    def __init__(self, me, acc, got, send, recv):
        z_near = jnp.where(me.is_end, me.z1, me.z1)
        z_far = jnp.where(me.is_end, me.z2, me.z3)
        self.devs = [me.dev(c=1 - me.c), me.dev(x=1 - me.x), me.dev(y=1 - me.y), me.dev(z=z_near), me.dev(z=z_far)]
        self.acc, self.got, self.send, self.recv = acc, got, send, recv

    def copy(self, k):
        return remote(self.acc, self.got.at[k], self.send.at[k], self.recv.at[k], self.devs[k])

    def start(self, k):
        self.copy(k).start()

    def finish(self, k):
        c = self.copy(k)
        c.wait_send()
        c.wait_recv()
        self.acc[...] += self.got[k]


def mega_kernel(*refs):
    it = iter(refs)
    take = lambda n: [next(it) for _ in range(n)]
    latents, pixels, counts, cotangent, gain_block = take(5)
    shards = take(8)
    latents_out, latents_grad, pixels_grad, small_out = take(4)
    grads_out = take(8)
    fulls = take(8)
    (
        w_buf, wd_buf, part, r1, r2, rz,
        xt_normed, xt_pix, xt_mixed, xt_nself, xt_smixed, xt_nmlp, xt_act, st_a, st_b,
        g_out, g_out_in, hid, hid_in, g_branch, g_branch_in, act, packed_in,
        dq, dq_in, big, dk_in, dv, dv_in,
        queries, keys, values, packed, after_cross, after_self, resid, pix, tmp, acc,
        gain_full, gain_vec, gain_acc, small, small_got,
    ) = take(44)
    gather_sems, scatter_sems = take(9), take(6)
    w_sem, wd_sem, in_sem, out_sem, sg_s, sg_r, ss_s, ss_r, xl, xs, xr, gs, gr, across_s, across_r = take(15)
    me = Place()

    plain = lambda i, k: Unit("all", shards[i], fulls[i], 0, k * UNIT_COLS)
    up_unit = lambda k: Unit("up", shards[6], fulls[6], 0, k * UNIT_COLS)
    down_unit = lambda k: Unit("down", shards[7], fulls[7], 2 * k * UNIT_ROWS, 0, 2 * UNIT_ROWS)
    order = ["key", "value", "query", "out", "qkv0", "qkv1", "qkv2", "self", "up0", "up1", "down0", "down1"]
    made = {"query": plain(0, 0), "key": plain(1, 0), "value": plain(2, 0), "out": plain(3, 0), "self": plain(5, 0)}
    made.update({f"qkv{k}": plain(4, k) for k in range(3)})
    made.update({f"up{k}": up_unit(k) for k in range(2)})
    made.update({f"down{k}": down_unit(k) for k in range(2)})
    gather = Gather(me, [made[name] for name in order], gather_sems)
    scatter_units = [("down", grads_out[7], 2 * k * UNIT_ROWS, 0) for k in range(2)]
    scatter_units += [("up", grads_out[6], 0, k * UNIT_COLS) for k in range(2)]
    scatter_units += [("all", grads_out[5], 0, 0)] + [("all", grads_out[4], 0, k * UNIT_COLS) for k in range(3)]
    scatter_units += [("all", grads_out[i], 0, 0) for i in (3, 2, 1, 0)]
    scatter = Scatter(me, scatter_units, (part, r1, r2, rz), scatter_sems)
    pushed = [0]
    tick = [0]

    clock = [0.0]
    settled = [-1]
    ready = []

    def tick_ready(t):
        return 17 + 3.7 * min(t, 6) + 8.4 * min(max(0, t - 6), 8) + 11.5 * max(0, t - 14)

    def settle_ready(k):
        return ready[k] if k < len(ready) else ready[-1] + 4.0 * (k - len(ready) + 1)

    def next_tick():
        clock[0] = max(clock[0], tick_ready(tick[0])) + 0.5
        gather.tick(tick[0], 1)
        tick[0] += 1

    def next_settle():
        settled[0] += 1
        last = settled[0]
        clock[0] = max(clock[0], settle_ready(last)) + 1.0
        for s in range(Scatter.STAGES - 1, 0, -1):
            if 0 <= last - s < len(scatter_units):
                scatter.stage(s, last - s)

    def spend(us):
        clock[0] += us
        while True:
            k = settled[0] + 1
            if tick[0] < gather.ticks(1) and tick_ready(tick[0]) <= clock[0]:
                next_tick()
            elif pushed[0] and k <= pushed[0] and k < len(scatter_units) + 4 and settle_ready(k) <= clock[0]:
                next_settle()
            else:
                break

    def arrived(name):
        u = order.index(name)
        while tick[0] < gather.ticks(1) and tick[0] <= u + Gather.STAGES - 1:
            next_tick()

    def gather_to(t):
        while tick[0] <= t:
            next_tick()

    def settle_to(last):
        while settled[0] < last:
            next_settle()

    def load(k, src, dst):
        return pltpu.make_async_copy(src, dst, in_sem.at[k])

    def across(k, src, dst):
        return remote(src, dst, across_s.at[k], across_r.at[k], me.dev(x=1 - me.x))

    mine, theirs = pl.ds(0, 256), pl.ds(256, 256)
    loads = [load(0, latents.at[0], after_self), load(1, pixels.at[0], pix), load(2, cotangent.at[0], resid)]
    own_gain = load(3, gain_block, gain_full.at[me.y, me.x, me.z, me.c])
    own_gain.start()
    loads[2].start()
    for u in range(len(gather.units)):
        gather.own(u).start()
    loads[0].start()
    loads[1].start()
    loads[2].wait()
    for_each(8, lambda i: g_out.__setitem__((block(i, 32), slice(None)), resid[block(i, 32), :].astype(BF16)))
    own_gain.wait()
    gains = SmallGather(me, gain_full, sg_s, sg_r)
    me.barrier()
    gains.run(0)
    gather.early(0)
    gather_to(1)
    for u in range(1, len(gather.units)):
        gather.early(u)
    gains.run(1)
    for s in range(2, 6):
        gather_to(s)
        gains.run(s)
    table = jnp.sum(gain_full[...].reshape(32, 8, 128), axis=1).astype(BF16)
    width = latents.shape[2]
    lane = lax.broadcasted_iota(jnp.int32, (128, width), 1)
    place = lax.broadcasted_iota(jnp.int32, (128, width), 0)
    owner = lax.broadcasted_iota(jnp.int32, (32, width), 0) == (lax.broadcasted_iota(jnp.int32, (32, width), 1) >> 5)
    for g in range(4):
        pick = jnp.where(place == (lane & 31) + 32 * g, 1.0, 0.0).astype(BF16)
        spread = jnp.where(owner, matmul(table, pick), 0.0)
        gain_vec[g : g + 1, :] = jnp.sum(spread, axis=0, keepdims=True)
    gain = [gain_vec.at[g : g + 1, :] for g in range(4)]
    for g in range(4):
        gain_acc[g] = jnp.zeros_like(gain_acc[g])

    staged = [None, None]

    def hand_over(k, stage, mine, slot, own_dst, far_dst):
        a = pltpu.make_async_copy(mine, own_dst, xl.at[k])
        b = remote(stage, far_dst, xs.at[k], xr.at[k], me.dev(c=1 - me.c))
        a.start()
        b.start()
        staged[slot] = (a, b)

    def clear(slot):
        if staged[slot] is not None:
            a, b = staged[slot]
            a.wait()
            b.wait_send()
            staged[slot] = None

    turn = [0]

    def transpose_out(k, x, row0, xt, k_rows):
        slot = turn[0] % 2
        turn[0] += 1
        clear(slot)

        def body(j):
            piece = x[pl.ds(row0, 256), block(j, 256)].T
            st_b[slot, j // 2, j % 2] = piece.reshape(4, 2, 32, 256)

        for_each(4, body)
        hand_over(
            k,
            st_b.at[slot, :, :, :, 1 - me.c],
            st_b.at[slot, :, :, :, me.c],
            slot,
            xt.at[:, :, :, :, pl.ds(row0, 256)],
            xt.at[:, :, :, :, pl.ds(k_rows + row0, 256)],
        )

    def xt_wait(k, xt, row0, k_rows):
        remote(
            st_b.at[0, :, :, :, 0],
            xt.at[:, :, :, :, pl.ds(k_rows + row0, 256)],
            xs.at[k],
            xr.at[k],
            me.dev(c=1 - me.c),
        ).wait_recv()

    def swap(k, src, dst):
        return remote(src, dst, gs.at[k], gr.at[k], me.dev(c=1 - me.c))

    w_turn = [0]

    def w_start(full, col):
        slot = w_turn[0] % 2
        w_turn[0] += 1
        c = pltpu.make_async_copy(full.at[:, :, :, :, :, pl.ds(col, UNIT_COLS)], w_buf.at[slot], w_sem.at[slot])
        c.start()
        return slot, c

    def w_fetch(full, col):
        slot, c = w_start(full, col)
        c.wait()
        return slot

    def w_cols(slot, j):
        return w_buf[slot, :, :, :, :, :, block(j, 256)].reshape(width, 256)

    def w_rows(slot, j):
        return w_buf[slot, j // 2, j % 2].reshape(256, UNIT_COLS)

    def project(x, slot, out):
        for_each(4, lambda j: out(j, matmul(x[...], w_cols(slot, j))))

    def store(dst, col0=0):
        def put(j, tile):
            dst[:, pl.ds(pl.multiple_of(col0 + j * 256, 256), 256)] = tile.astype(dst.dtype)

        return put

    def back(g, col0, slot, dst, first):
        def body(j):
            tile = matmul_nt(g[:, pl.ds(col0, UNIT_COLS)], w_rows(slot, j))
            cols = block(j, 256)
            if first:
                dst[:, cols] = tile.astype(dst.dtype)
            else:
                dst[:, cols] = dst[:, cols] + tile

        for_each(4, body)

    def partial_sums(us, body):
        u = pushed[0]
        settle_to(u - 3)
        if u >= PARTIALS:
            scatter.sent(u - PARTIALS)
        body(u % PARTIALS)
        scatter.stage(0, u)
        pushed[0] += 1
        clock[0] += us
        lag, gap = (14, 9) if scatter.kind(u) == "all" else (20, 11.5)
        ready.append(max(clock[0] + lag, (ready[-1] if ready else 0) + gap))
        spend(0)

    def weight_grad(xt_at, rows, own, far, col0):
        def fill(slot):
            def body(j):
                cols = pl.ds(pl.multiple_of(col0 + j * 256, 256), 256)
                total = matmul(xt_at(0), own[:, cols]) + matmul(xt_at(rows), far[:, cols])
                part[slot, :, :, :, :, block(j, 256)] = total.astype(BF16).reshape(2, 2, 4, UNIT_ROWS, 256)

            for_each(4, body)

        partial_sums(1.7 if rows > 256 else 1.2, fill)

    def xt_of(xt, rows):
        return lambda at: xt[:, :, :, :, pl.ds(at, rows)].reshape(512, rows)

    loads[0].wait()
    loads[1].wait()
    ln_forward(after_self, gain[0], tmp)
    transpose_out(0, tmp, 0, xt_normed, 256)
    spend(2)
    ln_forward(pix, gain[1], big)
    transpose_out(1, big, 0, xt_pix, 512)
    spend(3.3)
    transpose_out(2, big, 256, xt_pix, 512)
    count = counts[0]
    arrived("key")
    project(big, w_fetch(fulls[1], 0), store(keys))
    spend(3.3)
    arrived("value")
    project(big, w_fetch(fulls[2], 0), store(values))
    spend(3.3)
    arrived("query")
    project(tmp, w_fetch(fulls[0], 0), store(queries))
    spend(2.7)
    for half in range(2):
        attend_forward_heads(4 * half, 4, queries, 0, keys, 0, values, 0, tmp, count)
        spend(2.3)
    arrived("out")
    transpose_out(3, tmp, 0, xt_mixed, 256)

    def add_to(dst, src):
        def put(j, tile):
            dst[:, block(j, 256)] = src[:, block(j, 256)] + tile

        return put

    project(tmp, w_fetch(fulls[3], 0), add_to(after_cross, after_self))
    spend(3)

    ln_forward(after_cross, gain[2], tmp)
    transpose_out(4, tmp, 0, xt_nself, 256)
    spend(1.8)
    for k in range(3):
        arrived(f"qkv{k}")
        project(tmp, w_fetch(fulls[4], k * UNIT_COLS), store(packed, k * UNIT_COLS))
        spend(2.7)
    for half in range(2):
        attend_forward_heads(4 * half, 4, packed, 0, packed, UNIT_COLS, packed, 2 * UNIT_COLS, tmp, None)
        spend(2.2)
    arrived("self")
    transpose_out(5, tmp, 0, xt_smixed, 256)
    project(tmp, w_fetch(fulls[5], 0), add_to(after_self, after_cross))
    spend(3)

    ln_forward(after_self, gain[3], big.at[mine])
    across(1, big.at[mine], big.at[theirs]).start()
    across(0, g_out.at[mine], g_out.at[theirs]).start()
    transpose_out(6, big, 0, xt_nmlp, 512)
    spend(1.8)

    def up_rows(slot, k, rows):
        def up(j):
            x = matmul(big[rows, :], w_cols(slot, j))
            t = jnp.tanh(GELU_A * (x + GELU_B * (x * x * x)))
            half = 0.5 * (1.0 + t)
            cols = pl.ds(pl.multiple_of(k * UNIT_COLS + j * 256, 256), 256)
            act[rows, cols] = (x * half).astype(BF16)
            slope = half + (0.5 * GELU_A) * x * (1.0 - t * t) * (1.0 + (3 * GELU_B) * (x * x))
            hid[rows, cols] = slope.astype(BF16)

        for_each(4, up)

    a_staged = [None, None]
    act_copies = []

    def act_out(k, row0):
        n = len(act_copies)
        slot = n % 2
        if n >= 2:
            act_copies[n - 2][0].wait()
            act_copies[n - 2][1].wait_send()

        def body(m):
            st_a[slot, m // 2, m % 2] = act[pl.ds(row0, 256), pl.ds(pl.multiple_of(k * UNIT_COLS + m * 128, 128), 128)].T

        for_each(8, body)
        a = pltpu.make_async_copy(st_a.at[slot, :, me.c], xt_act.at[k, :, :, pl.ds(row0, 256)], xl.at[8 + n])
        b = remote(
            st_a.at[slot, :, 1 - me.c],
            xt_act.at[k, :, :, pl.ds(512 + row0, 256)],
            xs.at[8 + n],
            xr.at[8 + n],
            me.dev(c=1 - me.c),
        )
        a.start()
        b.start()
        act_copies.append((a, b))

    up_slots = []
    for k in range(2):
        arrived(f"up{k}")
        up_slots.append(w_fetch(fulls[6], k * UNIT_COLS))
        up_rows(up_slots[k], k, mine)
        spend(2.8)
        act_out(k, 0)
        spend(0.5)
    across(1, big.at[mine], big.at[theirs]).wait_recv()
    for k in range(2):
        up_rows(up_slots[k], k, theirs)
        spend(1.3)
        act_out(k, 256)
        spend(0.5)
    across(0, g_out.at[mine], g_out.at[theirs]).wait_recv()
    swap(0, g_out, g_out_in).start()
    transpose_out(7, big, 256, xt_nmlp, 512)
    for a, b in act_copies[2:]:
        a.wait()
        b.wait_send()
    for _, b in act_copies:
        b.wait_recv()
    for slot in range(2):
        clear(slot)
    spend(2)

    swap(0, g_out, g_out_in).wait_recv()

    def down_grad(k):
        def fill(slot):
            def body(i):
                r, cols = i // 4, block(i % 4, 256)
                rows = pl.ds(pl.multiple_of((2 * k + r) * UNIT_ROWS, UNIT_ROWS), UNIT_ROWS)
                near = xt_act[:, :, rows, pl.ds(0, 512)].reshape(256, 512)
                far = xt_act[:, :, rows, pl.ds(512, 512)].reshape(256, 512)
                total = matmul(near, g_out[:, cols]) + matmul(far, g_out_in[:, cols])
                part[slot, :, r, :, :, cols] = total.astype(BF16).reshape(2, 4, UNIT_ROWS, 256)

            for_each(8, body)

        partial_sums(2, fill)

    down_grad(0)
    arrived("down1")

    wd_turn = [0]

    def wd_start(q):
        slot = wd_turn[0] % 2
        wd_turn[0] += 1
        c = pltpu.make_async_copy(fulls[7].at[q], wd_buf.at[slot], wd_sem.at[slot])
        c.start()
        return slot, c

    wd = [wd_start(0), wd_start(1)]
    for q in range(2):
        slot, c = wd[q]
        c.wait()

        def hidden_back(j):
            w = wd_buf[slot, j].reshape(256, width)
            tile = matmul_nt(g_out[...], w)
            cols = pl.ds(pl.multiple_of(q * UNIT_COLS + j * 256, 256), 256)
            hid[:, cols] = (hid[:, cols].astype(F32) * tile).astype(BF16)

        for_each(4, hidden_back)
        cols = pl.ds(q * UNIT_COLS, UNIT_COLS)
        swap(1 + q, hid.at[:, cols], hid_in.at[:, cols]).start()
        spend(2)
    across(1, big.at[mine], big.at[theirs]).wait_send()
    sides = [pl.ds(0, UNIT_COLS // 2), pl.ds(UNIT_COLS // 2, UNIT_COLS // 2)]
    sums = [across(k, big.at[mine, cols], tmp.at[:, cols]) for k, cols in zip((2, 4), sides)]

    def sums_for(side):
        def body(i):
            j = 2 * side + i
            tile = matmul_nt(hid[theirs, pl.ds(0, UNIT_COLS)], w_rows(up_slots[0], j))
            tile = tile + matmul_nt(hid[theirs, pl.ds(UNIT_COLS, UNIT_COLS)], w_rows(up_slots[1], j))
            big[mine, block(j, 256)] = tile.astype(BF16)

        for_each(2, body)
        sums[side].start()
        spend(1.3)

    sums_for(0)
    sums_for(1)
    down_grad(1)
    for k in range(2):
        back(hid.at[mine], k * UNIT_COLS, up_slots[k], acc.at[1], k == 0)
        spend(1.3)
    xt_wait(6, xt_nmlp, 0, 512)
    xt_wait(7, xt_nmlp, 256, 512)
    for k in range(2):
        cols = pl.ds(k * UNIT_COLS, UNIT_COLS)
        swap(1 + k, hid.at[:, cols], hid_in.at[:, cols]).wait_recv()
        weight_grad(xt_of(xt_nmlp, 512), 512, hid, hid_in, k * UNIT_COLS)
    for c in sums:
        c.wait_recv()

    def add_theirs(i):
        rows = block(i, 32)
        acc[1, rows, :] = acc[1, rows, :] + tmp[rows, :].astype(F32)

    for_each(8, add_theirs)
    so_slot, c_so = w_start(fulls[5], 0)
    ln_backward(after_self, 0, gain[3], acc.at[1], resid, gain_acc.at[3])
    spend(2.3)

    def round_rows(dst):
        for_each(8, lambda i: dst.__setitem__((block(i, 32), slice(None)), resid[block(i, 32), :].astype(BF16)))

    round_rows(g_branch)
    swap(3, g_branch, g_branch_in).start()
    c_so.wait()
    qkv_w = w_start(fulls[4], 0)
    back(g_branch, 0, so_slot, tmp, True)
    spend(1.8)
    swap(3, g_branch, g_branch_in).wait_recv()
    xt_wait(5, xt_smixed, 0, 256)
    weight_grad(xt_of(xt_smixed, 256), 256, g_branch, g_branch_in, 0)
    for q in range(2):
        cols = pl.ds(q * UNIT_COLS, UNIT_COLS)
        swap(1 + q, hid.at[:, cols], hid_in.at[:, cols]).wait_send()
    corner = [hid.at[mine, pl.ds(0, UNIT_COLS)], hid.at[mine, pl.ds(UNIT_COLS, UNIT_COLS)], hid.at[theirs, pl.ds(0, UNIT_COLS)]]
    for half in range(2):
        attend_backward_heads(
            4 * half, 4, packed, 0, packed, UNIT_COLS, packed, 2 * UNIT_COLS, tmp, None,
            corner[0], 0, corner[1], 0, corner[2], 0,
        )
        spend(3.4)
    packed_swaps = [swap(4 + k, corner[k], packed_in.at[k]) for k in range(3)]
    for c in packed_swaps:
        c.start()
    for k in range(3):
        slot, c = qkv_w
        c.wait()
        if k < 2:
            qkv_w = w_start(fulls[4], (k + 1) * UNIT_COLS)
        back(corner[k], 0, slot, acc.at[0], k == 0)
        spend(1.3)
        packed_swaps[k].wait_recv()
        if k == 0:
            xt_wait(4, xt_nself, 0, 256)
        weight_grad(xt_of(xt_nself, 256), 256, corner[k], packed_in.at[k], 0)
    wo_slot, c_wo = w_start(fulls[3], 0)
    ln_backward(after_cross, 0, gain[2], acc.at[0], resid, gain_acc.at[2])
    spend(2.3)

    swap(3, g_branch, g_branch_in).wait_send()
    round_rows(g_branch)
    swap(7, g_branch, g_branch_in).start()
    c_wo.wait()
    back(g_branch, 0, wo_slot, tmp, True)
    spend(1.8)
    swap(7, g_branch, g_branch_in).wait_recv()
    xt_wait(3, xt_mixed, 0, 256)
    weight_grad(xt_of(xt_mixed, 256), 256, g_branch, g_branch_in, 0)

    for c in sums:
        c.wait_send()
    for half in range(2):
        attend_backward_heads(4 * half, 4, queries, 0, keys, 0, values, 0, tmp, count, dq, 0, big, 0, dv, 0)
        spend(3.2)
    given = [swap(8, dv, dv_in), swap(9, big, dk_in), swap(10, dq, dq_in)]
    for c in given:
        c.start()
    w_v = w_start(fulls[2], 0)
    w_k = w_start(fulls[1], 0)
    xt_wait(1, xt_pix, 0, 512)
    xt_wait(2, xt_pix, 256, 512)
    given[0].wait_recv()
    weight_grad(xt_of(xt_pix, 512), 512, dv, dv_in, 0)
    given[1].wait_recv()
    weight_grad(xt_of(xt_pix, 512), 512, big, dk_in, 0)
    xt_wait(0, xt_normed, 0, 256)
    given[2].wait_recv()
    weight_grad(xt_of(xt_normed, 256), 256, dq, dq_in, 0)
    def down(rows, slot, q, dst, base):
        def body(j):
            w = wd_buf[slot, :, :, :, block(j, 256)].reshape(UNIT_COLS, 256)
            tile = matmul(act[rows, pl.ds(q * UNIT_COLS, UNIT_COLS)], w)
            cols = block(j, 256)
            if base is None:
                dst[:, cols] = tile
            else:
                dst[:, cols] = base[:, cols] + tile

        for_each(4, body)
        spend(1.3)

    outer = hid.at[theirs, pl.ds(UNIT_COLS, UNIT_COLS)]
    down(theirs, wd[0][0], 0, after_cross, None)
    down(theirs, wd[1][0], 1, after_cross, after_cross)
    for_each(8, lambda i: tmp.__setitem__((block(i, 32), slice(None)), after_cross[block(i, 32), :].astype(BF16)))
    across(3, tmp, outer).start()
    w_v[1].wait()
    for r in range(2):
        back(dv.at[pl.ds(256 * r, 256)], 0, w_v[0], acc.at[r], True)
        spend(1.3)
    w_q = w_start(fulls[0], 0)
    w_k[1].wait()
    pix_copies = []
    for r in range(2):
        back(big.at[pl.ds(256 * r, 256)], 0, w_k[0], acc.at[r], False)
        spend(1.3)
        ln_backward(pix, 256 * r, gain[1], acc.at[r], None, gain_acc.at[1])
        c = pltpu.make_async_copy(acc.at[r], pixels_grad.at[0, pl.ds(256 * r, 256)], out_sem.at[2 + r])
        c.start()
        pix_copies.append(c)
        spend(2.3)
    down(mine, wd[0][0], 0, after_cross, after_self)
    down(mine, wd[1][0], 1, after_cross, after_cross)
    again = load(0, latents.at[0], after_self)
    again.start()
    across(3, tmp, outer).wait_recv()
    small[...] = jnp.zeros_like(small)

    def add_output(i, total):
        rows = block(i, 32)
        v = after_cross[rows, :] + outer[rows, :].astype(F32)
        after_cross[rows, :] = v
        v = v * v
        return total + v[0:8] + v[8:16] + v[16:24] + v[24:32]

    squares = lax.fori_loop(0, 8, add_output, jnp.zeros((8, width), F32))
    out_copy = pltpu.make_async_copy(after_cross, latents_out.at[0], out_sem.at[0])
    out_copy.start()
    mean_square = jnp.sum(jnp.sum(squares, axis=1, keepdims=True), axis=0, keepdims=True) / (latents.shape[1] * width)
    root_mean = jnp.sqrt(mean_square)
    small[4:5, :] = jnp.broadcast_to(root_mean, (1, width))
    spend(1)
    pix_copies[0].wait()
    w_q[1].wait()
    back(dq, 0, w_q[0], acc.at[0], True)
    spend(1.3)
    again.wait()
    ln_backward(after_self, 0, gain[0], acc.at[0], resid, gain_acc.at[0])
    grad_copy = pltpu.make_async_copy(resid, latents_grad.at[0], out_sem.at[1])
    grad_copy.start()
    spend(2.3)
    for g in range(4):
        small[g : g + 1, :] = jnp.sum(gain_acc[g], axis=0, keepdims=True)
    total = SmallSum(me, small, small_got, ss_s, ss_r)
    for k in range(5):
        total.start(k)
        if settled[0] < len(scatter_units) + 3:
            next_settle()
        total.finish(k)
    settle_to(len(scatter_units) + 3)
    small[5:6, :] = jnp.broadcast_to(root_mean, (1, width))
    small_out[...] = small[...]

    for u in range(len(gather.units)):
        gather.sent(u)
    for u in range(len(scatter_units) - PARTIALS, len(scatter_units)):
        scatter.sent(u)
    swap(0, g_out, g_out_in).wait_send()
    across(0, g_out.at[mine], g_out.at[theirs]).wait_send()
    for c in packed_swaps:
        c.wait_send()
    swap(7, g_branch, g_branch_in).wait_send()
    for c in given:
        c.wait_send()
    grad_copy.wait()
    pix_copies[1].wait()
    out_copy.wait()
    across(3, tmp, outer).wait_send()


def mega(latents, pixels, counts, cotangent, gain_block, shards):
    rows, slots, width = latents.shape[1], pixels.shape[1], latents.shape[2]
    hidden = shards[6].shape[1]
    vm = pltpu.VMEM
    xt = lambda k: vm((2, 2, 4, UNIT_ROWS, k), BF16)
    wide = lambda n: vm((rows, n), BF16)
    scratch = [
        vm((2, 2, 2, 4, 2, UNIT_ROWS, UNIT_COLS), BF16),
        vm((2, 4, 2, 128, UNIT_COLS), BF16),
        vm((PARTIALS, 2, 2, 4, UNIT_ROWS, UNIT_COLS), BF16),
        vm((PARTIALS, 2, 4, UNIT_ROWS, UNIT_COLS), BF16),
        vm((RING + 2, 4, UNIT_ROWS, UNIT_COLS), BF16),
        vm((RING, 4, 2, UNIT_ROWS, UNIT_COLS), BF16),
        xt(2 * rows), xt(2 * slots), xt(2 * rows), xt(2 * rows), xt(2 * rows), xt(4 * rows),
        vm((2, 4, 128, 4 * rows), BF16),
        vm((2, 4, 2, 128, rows), BF16),
        vm((2, 2, 2, 4, 2, UNIT_ROWS, 256), BF16),
        vm((2 * rows, width), BF16), vm((2 * rows, width), BF16), vm((2 * rows, hidden // 2), BF16), vm((2 * rows, hidden // 2), BF16),
        wide(width), wide(width), vm((2 * rows, hidden // 2), BF16), vm((3, rows, width), BF16),
        wide(width), wide(width), vm((slots, width), BF16), vm((slots, width), BF16), vm((slots, width), BF16), vm((slots, width), BF16),
        wide(width), vm((slots, width), BF16), vm((slots, width), BF16), wide(3 * width),
        vm((rows, width), F32), vm((rows, width), F32), vm((rows, width), F32), vm((slots, width), BF16), wide(width), vm((2, rows, width), F32),
        vm((2, 2, 4, 2, 8, 128), F32), vm((8, width), F32), vm((4, 8, width), F32), vm((8, width), F32), vm((5, 8, width), F32),
    ]
    sems = Gather.sems(12) + Scatter.sems(12)
    sems += [DMA((2,)), DMA((2,)), DMA((4,)), DMA((4,)), DMA((7,)), DMA((7,)), DMA((5,)), DMA((5,))]
    sems += [DMA((12,))] * 3 + [DMA((11,))] * 2 + [DMA((5,))] * 2
    outs = [
        jax.ShapeDtypeStruct(latents.shape, F32),
        jax.ShapeDtypeStruct(latents.shape, F32),
        jax.ShapeDtypeStruct(pixels.shape, F32),
        jax.ShapeDtypeStruct((8, width), F32),
    ]
    outs += [jax.ShapeDtypeStruct(s.shape, F32) for s in shards]
    outs += [jax.ShapeDtypeStruct((2, 2, 4, 2) + s.shape, s.dtype) for s in shards[:6]]
    outs.append(jax.ShapeDtypeStruct((2, 2, 4, 2, shards[6].shape[0], hidden // 2), BF16))
    outs.append(jax.ShapeDtypeStruct((2, 4, 2) + shards[7].shape, BF16))
    hbm, vmem = pl.BlockSpec(memory_space=pl.ANY), pl.BlockSpec(memory_space=pltpu.VMEM)
    smem = pl.BlockSpec(memory_space=pltpu.SMEM)
    results = pl.pallas_call(
        mega_kernel,
        out_shape=outs,
        in_specs=[hbm, hbm, smem, hbm, hbm] + [vmem] * 8,
        out_specs=[hbm] * 3 + [vmem] + [vmem] * 8 + [hbm] * 8,
        scratch_shapes=scratch + sems,
        compiler_params=pltpu.CompilerParams(collective_id=0, has_side_effects=True, vmem_limit_bytes=63 * 2**20),
    )(latents, pixels, counts, cotangent, gain_block, *shards)
    return results[:4], results[4:12]


def layer_norm(inputs, gain):
    center = inputs - jnp.mean(inputs, axis=-1, keepdims=True)
    spread = jnp.mean(center * center, axis=-1, keepdims=True)
    return center * lax.rsqrt(spread + EPS) * gain


def project(inputs, matrix):
    return jnp.einsum("gld,de->gle", inputs, matrix, preferred_element_type=jnp.float32)


def project_back(grad_rows, matrix):
    return jnp.einsum("gle,de->gld", grad_rows, matrix, preferred_element_type=jnp.float32)


def weight_grad(inputs, grad_rows):
    return jnp.einsum("gld,gle->de", inputs, grad_rows, preferred_element_type=jnp.float32)


def split_heads(tensor):
    return tensor.reshape(tensor.shape[0], tensor.shape[1], HEADS, -1)


def merge_heads(tensor):
    return tensor.reshape(tensor.shape[0], tensor.shape[1], -1)


def scores_of(queries, key_rows, visible):
    scores = jnp.einsum("glhd,gshd->ghls", queries, key_rows, preferred_element_type=jnp.float32)
    scores = scores * queries.shape[-1] ** (-0.5)
    if visible is not None:
        scores = jnp.where(visible[:, None, None, :], scores, -1e30)
    return scores


def attend_forward(queries, key_rows, value_rows, visible):
    scores = scores_of(queries, key_rows, visible)
    largest = jnp.max(scores, axis=-1, keepdims=True)
    exp_scores = jnp.exp(scores - largest)
    totals = jnp.sum(exp_scores, axis=-1, keepdims=True)
    attn_probs = exp_scores / totals
    log_total = largest + jnp.log(totals)
    mixed = jnp.einsum(
        "ghls,gshd->glhd",
        attn_probs.astype(jnp.bfloat16),
        value_rows,
        preferred_element_type=jnp.float32,
    ).astype(jnp.bfloat16)
    return (mixed, log_total)


def attend_backward(queries, key_rows, value_rows, visible, log_total, mixed_grad):
    scale = queries.shape[-1] ** (-0.5)
    attn_probs = jnp.exp(scores_of(queries, key_rows, visible) - log_total)
    probs_grad = jnp.einsum(
        "glhd,gshd->ghls", mixed_grad, value_rows, preferred_element_type=jnp.float32
    )
    value_grad = jnp.einsum(
        "ghls,glhd->gshd",
        attn_probs.astype(jnp.bfloat16),
        mixed_grad,
        preferred_element_type=jnp.float32,
    ).astype(jnp.bfloat16)
    score_grad = attn_probs * (
        probs_grad - jnp.sum(probs_grad * attn_probs, axis=-1, keepdims=True)
    )
    score_grad = score_grad.astype(jnp.bfloat16)
    query_grad = (
        jnp.einsum("ghls,gshd->glhd", score_grad, key_rows, preferred_element_type=jnp.float32)
        * scale
    ).astype(jnp.bfloat16)
    key_grad = (
        jnp.einsum("ghls,glhd->gshd", score_grad, queries, preferred_element_type=jnp.float32)
        * scale
    ).astype(jnp.bfloat16)
    return (query_grad, key_grad, value_grad)


def local_plain(
    latents,
    pixels,
    slot_index,
    counts,
    cotangent,
    gain_q,
    gain_kv,
    w_query,
    w_key,
    w_value,
    w_out,
    gain_self,
    w_qkv,
    w_self_out,
    gain_mlp,
    w_up,
    w_down,
):
    groups = latents.shape[0]
    slots = pixels.shape[1]
    width = latents.shape[2]
    local_slot = slot_index % groups
    chosen = jnp.take(pixels, local_slot, axis=0).astype(jnp.float32)
    visible_count = jnp.take(counts, local_slot, axis=0)
    visible = lax.broadcasted_iota(jnp.int32, (groups, slots), 1) < visible_count[:, None]
    cross_all = (
        lax.all_gather(gain_q, ("dp", "fsdp"), axis=0, tiled=True),
        lax.all_gather(gain_kv, ("dp", "fsdp"), axis=0, tiled=True),
        lax.all_gather(w_query, ("dp", "fsdp"), axis=0, tiled=True),
        lax.all_gather(w_key, ("dp", "fsdp"), axis=0, tiled=True),
        lax.all_gather(w_value, ("dp", "fsdp"), axis=0, tiled=True),
        lax.all_gather(w_out, ("dp", "fsdp"), axis=0, tiled=True),
    )
    normed = layer_norm(latents, cross_all[0].astype(jnp.float32)).astype(jnp.bfloat16)
    pix_normed = layer_norm(chosen, cross_all[1].astype(jnp.float32)).astype(jnp.bfloat16)
    queries = split_heads(project(normed, cross_all[2]).astype(jnp.bfloat16))
    key_rows = split_heads(project(pix_normed, cross_all[3]).astype(jnp.bfloat16))
    value_rows = split_heads(project(pix_normed, cross_all[4]).astype(jnp.bfloat16))
    cross_mixed, cross_total = attend_forward(queries, key_rows, value_rows, visible)
    cross_flat = merge_heads(cross_mixed)
    after_cross = latents + project(cross_flat, cross_all[5])
    self_all = (
        lax.all_gather(gain_self, ("dp", "fsdp"), axis=0, tiled=True),
        lax.all_gather(w_qkv, ("dp", "fsdp"), axis=0, tiled=True),
        lax.all_gather(w_self_out, ("dp", "fsdp"), axis=0, tiled=True),
    )
    normed_self = layer_norm(after_cross, self_all[0].astype(jnp.float32)).astype(jnp.bfloat16)
    packed = project(normed_self, self_all[1]).astype(jnp.bfloat16)
    self_queries = split_heads(packed[..., :width])
    self_keys = split_heads(packed[..., width : 2 * width])
    self_values = split_heads(packed[..., 2 * width :])
    self_mixed, self_total = attend_forward(self_queries, self_keys, self_values, None)
    self_flat = merge_heads(self_mixed)
    after_self = after_cross + project(self_flat, self_all[2])
    mlp_all = (
        lax.all_gather(gain_mlp, ("dp", "fsdp"), axis=0, tiled=True),
        lax.all_gather(w_up, ("dp", "fsdp"), axis=0, tiled=True),
        lax.all_gather(w_down, ("dp", "fsdp"), axis=0, tiled=True),
    )
    normed_mlp = layer_norm(after_self, mlp_all[0].astype(jnp.float32)).astype(jnp.bfloat16)
    hidden = project(normed_mlp, mlp_all[1])
    activated = jax.nn.gelu(hidden).astype(jnp.bfloat16)
    latents_out = after_self + project(activated, mlp_all[2])
    root_mean = jnp.sqrt(jnp.mean(latents_out * latents_out, axis=(1, 2)))
    total_norm = lax.psum(jnp.sum(root_mean), ("dp", "fsdp"))
    norms = root_mean * (groups * lax.axis_size(("dp", "fsdp"))) / total_norm
    mlp_back = (
        lax.all_gather(gain_mlp, ("dp", "fsdp"), axis=0, tiled=True),
        lax.all_gather(w_up, ("dp", "fsdp"), axis=0, tiled=True),
        lax.all_gather(w_down, ("dp", "fsdp"), axis=0, tiled=True),
    )
    out_grad = cotangent.astype(jnp.bfloat16)
    down_grad = weight_grad(activated, out_grad)
    act_grad = project_back(out_grad, mlp_back[2])
    hidden_grad = jax.vjp(jax.nn.gelu, hidden)[1](act_grad)[0].astype(jnp.bfloat16)
    up_grad = weight_grad(normed_mlp, hidden_grad)
    mlp_in_grad = project_back(hidden_grad, mlp_back[1])
    after_self_ln, mlp_gain_grad = jax.vjp(layer_norm, after_self, mlp_back[0].astype(jnp.float32))[
        1
    ](mlp_in_grad)
    after_self_grad = cotangent + after_self_ln
    mlp_grads = (
        lax.psum_scatter(mlp_gain_grad, ("dp", "fsdp"), scatter_dimension=0, tiled=True),
        lax.psum_scatter(up_grad, ("dp", "fsdp"), scatter_dimension=0, tiled=True),
        lax.psum_scatter(down_grad, ("dp", "fsdp"), scatter_dimension=0, tiled=True),
    )
    self_back = (
        lax.all_gather(gain_self, ("dp", "fsdp"), axis=0, tiled=True),
        lax.all_gather(w_qkv, ("dp", "fsdp"), axis=0, tiled=True),
        lax.all_gather(w_self_out, ("dp", "fsdp"), axis=0, tiled=True),
    )
    self_branch = after_self_grad.astype(jnp.bfloat16)
    self_out_grad = weight_grad(self_flat, self_branch)
    self_mixed_grad = split_heads(project_back(self_branch, self_back[2]).astype(jnp.bfloat16))
    self_q_grad, self_k_grad, self_v_grad = attend_backward(
        self_queries, self_keys, self_values, None, self_total, self_mixed_grad
    )
    packed_grad = jnp.concatenate(
        [merge_heads(self_q_grad), merge_heads(self_k_grad), merge_heads(self_v_grad)], axis=-1
    )
    qkv_grad = weight_grad(normed_self, packed_grad)
    self_in_grad = project_back(packed_grad, self_back[1])
    after_cross_ln, self_gain_grad = jax.vjp(
        layer_norm, after_cross, self_back[0].astype(jnp.float32)
    )[1](self_in_grad)
    after_cross_grad = after_self_grad + after_cross_ln
    self_grads = (
        lax.psum_scatter(self_gain_grad, ("dp", "fsdp"), scatter_dimension=0, tiled=True),
        lax.psum_scatter(qkv_grad, ("dp", "fsdp"), scatter_dimension=0, tiled=True),
        lax.psum_scatter(self_out_grad, ("dp", "fsdp"), scatter_dimension=0, tiled=True),
    )
    cross_back = (
        lax.all_gather(gain_q, ("dp", "fsdp"), axis=0, tiled=True),
        lax.all_gather(gain_kv, ("dp", "fsdp"), axis=0, tiled=True),
        lax.all_gather(w_query, ("dp", "fsdp"), axis=0, tiled=True),
        lax.all_gather(w_key, ("dp", "fsdp"), axis=0, tiled=True),
        lax.all_gather(w_value, ("dp", "fsdp"), axis=0, tiled=True),
        lax.all_gather(w_out, ("dp", "fsdp"), axis=0, tiled=True),
    )
    cross_branch = after_cross_grad.astype(jnp.bfloat16)
    out_w_grad = weight_grad(cross_flat, cross_branch)
    cross_mixed_grad = split_heads(project_back(cross_branch, cross_back[5]).astype(jnp.bfloat16))
    query_grad, key_grad, value_grad = attend_backward(
        queries, key_rows, value_rows, visible, cross_total, cross_mixed_grad
    )
    query_flat = merge_heads(query_grad)
    key_flat = merge_heads(key_grad)
    value_flat = merge_heads(value_grad)
    query_w_grad = weight_grad(normed, query_flat)
    key_w_grad = weight_grad(pix_normed, key_flat)
    value_w_grad = weight_grad(pix_normed, value_flat)
    normed_grad = project_back(query_flat, cross_back[2])
    pix_normed_grad = project_back(key_flat, cross_back[3]) + project_back(
        value_flat, cross_back[4]
    )
    latents_ln, query_gain_grad = jax.vjp(layer_norm, latents, cross_back[0].astype(jnp.float32))[
        1
    ](normed_grad)
    latents_grad = after_cross_grad + latents_ln
    chosen_grad, pixel_gain_grad = jax.vjp(layer_norm, chosen, cross_back[1].astype(jnp.float32))[
        1
    ](pix_normed_grad)
    pixels_grad = jnp.zeros(pixels.shape, jnp.float32).at[local_slot].add(chosen_grad)
    cross_grads = (
        lax.psum_scatter(query_gain_grad, ("dp", "fsdp"), scatter_dimension=0, tiled=True),
        lax.psum_scatter(pixel_gain_grad, ("dp", "fsdp"), scatter_dimension=0, tiled=True),
        lax.psum_scatter(query_w_grad, ("dp", "fsdp"), scatter_dimension=0, tiled=True),
        lax.psum_scatter(key_w_grad, ("dp", "fsdp"), scatter_dimension=0, tiled=True),
        lax.psum_scatter(value_w_grad, ("dp", "fsdp"), scatter_dimension=0, tiled=True),
        lax.psum_scatter(out_w_grad, ("dp", "fsdp"), scatter_dimension=0, tiled=True),
    )
    return (
        latents_out,
        latents_grad,
        pixels_grad,
        cross_grads[0],
        cross_grads[1],
        cross_grads[2],
        cross_grads[3],
        cross_grads[4],
        cross_grads[5],
        self_grads[0],
        self_grads[1],
        self_grads[2],
        mlp_grads[0],
        mlp_grads[1],
        mlp_grads[2],
        norms,
    )


def local_fast(
    latents,
    pixels,
    slot_index,
    counts,
    cotangent,
    gain_q,
    gain_kv,
    w_query,
    w_key,
    w_value,
    w_out,
    gain_self,
    w_qkv,
    w_self_out,
    gain_mlp,
    w_up,
    w_down,
):
    gains = jnp.concatenate([gain_q, gain_kv, gain_self, gain_mlp]).astype(jnp.float32)
    gain_block = jnp.pad(gains[None, :], ((0, 7), (0, 0)))
    shards = (w_query, w_key, w_value, w_out, w_qkv, w_self_out, w_up, w_down)
    (latents_out, latents_grad, pixels_grad, small), grads = mega(latents, pixels, counts, cotangent, gain_block, shards)
    latents_out, latents_grad, pixels_grad, *grads = hand_out([latents_out, latents_grad, pixels_grad] + list(grads))
    rows = gain_q.shape[0]
    devices = lax.axis_size(("dp", "fsdp"))
    mine = lax.dynamic_slice(small[:4], (0, lax.axis_index(("dp", "fsdp")) * rows), (4, rows))
    norms = small[5, :1] * devices / small[4, :1]
    g_query, g_key, g_value, g_out, g_qkv, g_self_out, g_up, g_down = grads
    return (
        latents_out,
        latents_grad,
        pixels_grad,
        mine[0],
        mine[1],
        g_query,
        g_key,
        g_value,
        g_out,
        mine[2],
        g_qkv,
        g_self_out,
        mine[3],
        g_up,
        g_down,
        norms,
    )


def hand_out(arrays):
    n = len(arrays)

    def kernel(*refs):
        sems = refs[3 * n]
        fetch = [pltpu.make_async_copy(refs[k], refs[2 * n + k], sems.at[0, k]) for k in range(n)]
        put = [pltpu.make_async_copy(refs[2 * n + k], refs[n + k], sems.at[1, k]) for k in range(n)]
        for c in fetch:
            c.start()
        for k in range(n):
            fetch[k].wait()
            put[k].start()
        for c in put:
            c.wait()

    return pl.pallas_call(
        kernel,
        out_shape=[jax.ShapeDtypeStruct(a.shape, a.dtype) for a in arrays],
        in_specs=[pl.BlockSpec(memory_space=pl.ANY)] * n,
        out_specs=[pl.BlockSpec(memory_space=pl.ANY)] * n,
        scratch_shapes=[pltpu.VMEM(a.shape, a.dtype) for a in arrays] + [DMA((2, n))],
        compiler_params=pltpu.CompilerParams(vmem_limit_bytes=63 * 2**20),
    )(*arrays)


def fits(mesh):
    return mesh.shape["dp"] == 4 and mesh.shape["fsdp"] == 8


def solution(mesh):
    in_specs = (
        P(("dp", "fsdp"), None, None),
        P(("dp", "fsdp"), None, None),
        P(("dp", "fsdp")),
        P(("dp", "fsdp")),
        P(("dp", "fsdp"), None, None),
        P(("dp", "fsdp")),
        P(("dp", "fsdp")),
        P(("dp", "fsdp"), None),
        P(("dp", "fsdp"), None),
        P(("dp", "fsdp"), None),
        P(("dp", "fsdp"), None),
        P(("dp", "fsdp")),
        P(("dp", "fsdp"), None),
        P(("dp", "fsdp"), None),
        P(("dp", "fsdp")),
        P(("dp", "fsdp"), None),
        P(("dp", "fsdp"), None),
    )
    out_specs = (
        P(("dp", "fsdp"), None, None),
        P(("dp", "fsdp"), None, None),
        P(("dp", "fsdp"), None, None),
        P(("dp", "fsdp")),
        P(("dp", "fsdp")),
        P(("dp", "fsdp"), None),
        P(("dp", "fsdp"), None),
        P(("dp", "fsdp"), None),
        P(("dp", "fsdp"), None),
        P(("dp", "fsdp")),
        P(("dp", "fsdp"), None),
        P(("dp", "fsdp"), None),
        P(("dp", "fsdp")),
        P(("dp", "fsdp"), None),
        P(("dp", "fsdp"), None),
        P(("dp", "fsdp")),
    )
    return jax.shard_map(local_fast if fits(mesh) else local_plain, mesh=mesh, in_specs=in_specs, out_specs=out_specs, check_vma=False)
```
